128 devices in a mesh: dp: 4 (over y_hi, core), frames: 32 (over z, y_lo, x).
Axes of the slice: x: 4, y: 4 (y_hi: 2, y_lo: 2; y = y_hi * 2 + y_lo), z: 4, core: 2. Of those that a mesh axis runs over, the one named last changes fastest.
Arguments:
- clean_input: bfloat16 [4, 4096, 1024], P('dp', 'frames'), may hold values from -6 to 6
- corrupt_input: bfloat16 [4, 4096, 1024], P('dp', 'frames'), may hold values from -6 to 6
- patch_mask: int32 [4, 4096], P('dp', 'frames'), may hold values 0 or 1
- lengths: int32 [4], P('dp'), may hold values from 2049 to 4096, as said below
- site_ids: int32 [8], replicated, may hold values from 0 to 3
- w_query: bfloat16 [1024, 512], replicated
- w_key: bfloat16 [1024, 512], replicated
- w_value: bfloat16 [1024, 512], replicated, may hold values from -0.1875 to 0.1875
- w_attn_out: bfloat16 [512, 1024], replicated, may hold values from -0.25 to 0.25
- w_pointwise_in: bfloat16 [1024, 2048], replicated, may hold values from -0.1875 to 0.1875
- depth_kernel: bfloat16 [31, 1024], replicated, may hold values from -1 to 1
- w_pointwise_out: bfloat16 [1024, 1024], replicated, may hold values from -0.1875 to 0.1875
- cotangent: bfloat16 [4, 4096, 1024], P('dp', 'frames'), may hold values from -0.25 to 0.25
Outputs:
- attribution: float32 [4, 8, 4096], P('dp', None, 'frames')
- grad_pointwise_in: float32 [1024, 2048], P(('dp', 'frames'))
- grad_pointwise_out: float32 [1024, 1024], P(('dp', 'frames'))
The draws below stay inside these ranges and needn't reach their ends.
Inputs may be any that keep to these rules, and one draw needn't show every extreme that they name: `lengths`: in every draw one recording has 4096 frames.
All inputs are finite; a program needn't handle non-finite values. No bound on the sum of `patch_mask` on one device may be relied on, other than what follows from the above.
Results may differ from the reference program's by a relative error of at most 0.025.
Values may be sent and summed in bfloat16 or wider, within the bound.
No kernel may reach another device: no remote copies, remote signals or barrier semaphores. Data moves between devices by JAX's collectives and lax.ppermute only.
A program may use at most 128 MiB of HBM per device.

```python
import math
import jax
import jax.numpy as jnp
from jax import lax

D = 1024
HEADS = 8
DH = 64
KERNEL = 31
NSEL = 8
RECS = 4
LENGTH = 4096


def key_columns(key):
    return jax.random.normal(key, (D, HEADS * DH), jnp.float32) * D ** (-0.5)


def draw_w_key(key, part):
    shared = key_columns(key)
    key = jax.random.fold_in(key, 3)
    noise = jax.random.normal(key, (D, HEADS * DH), jnp.float32) * 0.1 * D ** (-0.5)
    return (shared + noise).astype(jnp.bfloat16)


def draw_w_query(key, part):
    key = jax.random.fold_in(key, 5)
    first_key = jax.random.fold_in(key, 0)
    own = jax.random.normal(first_key, (D, HEADS * DH), jnp.float32) * 2.5 * D ** (-0.5)
    return own.astype(jnp.bfloat16)


def draw_lengths(key, part):
    key = jax.random.fold_in(key, 7)
    first_key, second_key = jax.random.split(key)
    shorter = LENGTH - jax.random.randint(first_key, (RECS,), 0, LENGTH // 2)
    chosen = jax.random.randint(second_key, (), 0, RECS)
    return jnp.where(jnp.arange(RECS) == chosen, LENGTH, shorter).astype(jnp.int32)


def set_ends(drawn, stream_key, smallest, largest):
    index_at = [jax.random.randint(jax.random.fold_in(stream_key, axis), (), 0, length) for axis, length in enumerate(drawn.shape)]
    longest = drawn.shape.index(max(drawn.shape))
    beside = index_at[:longest] + [(index_at[longest] + 1) % drawn.shape[longest]] + index_at[longest + 1:]
    return drawn.at[tuple(index_at)].set(smallest).at[tuple(beside)].set(largest)


def block_levels(rng, dims, cuts, smallest, largest):
    factor_of = 1.0
    for dim, blocks in cuts:
        steps = jax.random.uniform(jax.random.fold_in(jax.random.fold_in(rng, 6), dim), (blocks,), jnp.float32, smallest / len(cuts), largest / len(cuts))
        factor_of = factor_of * jnp.repeat(jnp.exp(steps), dims[dim] // blocks).reshape((-1,) + (1,) * (len(dims) - 1 - dim))
    return factor_of


def gaussian(key, dims, scale, most, pieces=(), dtype=jnp.bfloat16):
    entries = jax.random.normal(key, dims, jnp.float32) * scale
    if len(pieces) > 0:
        entries = block_levels(key, dims, pieces, -0.22, 0.18) * entries
    return jnp.clip(entries, min=-most, max=most).astype(dtype)


def setup_inputs(seed: int = 0) -> dict:
    seeds = jax.random.split(jax.random.key(seed), 14)
    clean_input = gaussian(seeds[0], (RECS, LENGTH, D), 1.0, 6.0, ((0, 4), (1, 32)))
    corrupt_input = gaussian(seeds[1], (RECS, LENGTH, D), 1.0, 6.0, ((0, 4), (1, 32)))
    patch_mask = set_ends((jax.random.randint(seeds[2], (RECS, LENGTH), 0, 4) < 1).astype(jnp.int32), jax.random.fold_in(seeds[2], 1), 0, 1)
    lengths = draw_lengths(jax.random.fold_in(seeds[13], 71), 0)
    site_ids = set_ends(jax.random.randint(seeds[4], (NSEL,), 0, 4), jax.random.fold_in(seeds[4], 1), 0, 3).astype(jnp.int32)
    w_query = draw_w_query(jax.random.fold_in(seeds[13], 71), 0)
    w_key = draw_w_key(jax.random.fold_in(seeds[13], 71), 0)
    w_value = gaussian(seeds[7], (D, HEADS * DH), D ** -0.5, 0.1875)
    w_attn_out = gaussian(seeds[8], (HEADS * DH, D), (HEADS * DH) ** -0.5, 0.25)
    w_pointwise_in = gaussian(seeds[9], (D, 2 * D), D ** -0.5, 0.1875)
    depth_kernel = gaussian(seeds[10], (KERNEL, D), KERNEL ** -0.5, 1.0)
    w_pointwise_out = gaussian(seeds[11], (D, D), D ** -0.5, 0.1875)
    cotangent = gaussian(seeds[12], (RECS, LENGTH, D), 0.03125, 0.25, ((0, 4), (1, 32)))
    return {"clean_input": clean_input, "corrupt_input": corrupt_input, "patch_mask": patch_mask, "lengths": lengths, "site_ids": site_ids, "w_query": w_query, "w_key": w_key, "w_value": w_value, "w_attn_out": w_attn_out, "w_pointwise_in": w_pointwise_in, "depth_kernel": depth_kernel, "w_pointwise_out": w_pointwise_out, "cotangent": cotangent}


EPSILON = 1e-05
FLOOR = -1e+30

def normalize(values):
    mean = lax.optimization_barrier(jnp.mean(values, axis=-1, keepdims=True))
    centred = values - mean
    variance = lax.optimization_barrier(jnp.mean(centred * centred, axis=-1, keepdims=True))
    inverse = lax.rsqrt(variance + EPSILON)
    return (centred * inverse, inverse)

def norm_back(grad, normed, inverse):
    return (grad - lax.optimization_barrier(jnp.mean(grad, axis=-1, keepdims=True)) - normed * lax.optimization_barrier(jnp.mean(grad * normed, axis=-1, keepdims=True))) * inverse

def depthwise(padded, kernel, count):
    result = jnp.zeros((count, padded.shape[1]), jnp.float32)
    for tap_index in range(kernel.shape[0]):
        result = result + kernel[tap_index].astype(jnp.float32) * padded[tap_index:tap_index + count].astype(jnp.float32)
    return result

def attend_init(count):
    return (jnp.full((HEADS, count), FLOOR, jnp.float32), jnp.zeros((HEADS, count), jnp.float32), jnp.zeros((count, HEADS, DH), jnp.float32))

def attend_step(state, query, keys, values, start, length):
    best, total, accum = state
    count = keys.shape[0]
    query_heads = query.reshape(query.shape[0], HEADS, DH)
    key_heads = keys.reshape(count, HEADS, DH)
    value_heads = values.reshape(count, HEADS, DH)
    scores = jnp.einsum('qhd,khd->hqk', query_heads, key_heads, preferred_element_type=jnp.float32) * DH ** (-0.5)
    live = start + jnp.arange(count) < length
    scores = jnp.where(live[None, None, :], scores, FLOOR)
    newbest = jnp.maximum(best, lax.optimization_barrier(jnp.max(scores, axis=-1)))
    weights = jnp.exp(scores - newbest[:, :, None]) * live[None, None, :].astype(jnp.float32)
    rescale = jnp.exp(best - newbest)
    total = total * rescale + lax.optimization_barrier(jnp.sum(weights, axis=-1))
    addend = jnp.einsum('hqk,khd->qhd', weights.astype(jnp.bfloat16), value_heads, preferred_element_type=jnp.float32)
    accum = accum * jnp.transpose(rescale)[:, :, None] + addend
    return (newbest, total, accum)

def attend_finish(state):
    best, total, accum = state
    return (accum / jnp.transpose(total)[:, :, None]).reshape(accum.shape[0], HEADS * DH).astype(jnp.bfloat16)

def contract_rows(left, right):
    return lax.dot_general(left, right, (((0,), (0,)), ((), ())), preferred_element_type=jnp.float32)

def attention(query, keys, values, length):
    block = math.gcd(LENGTH, 512)
    blocks = query.reshape(LENGTH // block, block, HEADS * DH)

    def one_block(piece):
        return attend_finish(attend_step(attend_init(block), piece, keys, values, 0, length))
    return lax.map(one_block, blocks).reshape(LENGTH, HEADS * DH)

def reference(clean_input, corrupt_input, patch_mask, lengths, site_ids, w_query, w_key, w_value, w_attn_out, w_pointwise_in, depth_kernel, w_pointwise_out, cotangent):
    half = KERNEL // 2
    width = D
    tables = []
    lowered_all = []
    grad_mixed_all = []
    swished_all = []
    grad_output_all = []
    for record in range(RECS):
        length = lengths[record]
        valid = (jnp.arange(LENGTH) < length).astype(jnp.float32)[:, None]
        clean = clean_input[record]
        patched = jnp.where(patch_mask[record][:, None] == 1, corrupt_input[record], clean)
        runs = []
        for source in (clean, patched):
            normed, inverse = normalize(source.astype(jnp.float32))
            hidden = normed.astype(jnp.bfloat16)
            query = jnp.dot(hidden, w_query, preferred_element_type=jnp.float32).astype(jnp.bfloat16)
            keys = jnp.dot(hidden, w_key, preferred_element_type=jnp.float32).astype(jnp.bfloat16)
            values = jnp.dot(hidden, w_value, preferred_element_type=jnp.float32).astype(jnp.bfloat16)
            context = attention(query, keys, values, length)
            joined = source.astype(jnp.float32) + jnp.dot(context, w_attn_out, preferred_element_type=jnp.float32)
            resid = joined.astype(jnp.bfloat16)
            resid_normed, resid_inverse = normalize(resid.astype(jnp.float32))
            lowered = resid_normed.astype(jnp.bfloat16)
            mixed = jnp.dot(lowered, w_pointwise_in, preferred_element_type=jnp.float32)
            sigmoid_gate = jax.nn.sigmoid(mixed[:, width:])
            gated = (mixed[:, :width] * sigmoid_gate * valid).astype(jnp.bfloat16)
            padded = jnp.pad(gated, ((half, half), (0, 0)))
            spread = depthwise(padded, depth_kernel, LENGTH)
            zed, zed_inverse = normalize(spread)
            swished = (zed * jax.nn.sigmoid(zed)).astype(jnp.bfloat16)
            output = (resid.astype(jnp.float32) + jnp.dot(swished, w_pointwise_out, preferred_element_type=jnp.float32)).astype(jnp.bfloat16)
            runs.append((resid, resid_normed, resid_inverse, lowered, mixed, sigmoid_gate, gated, zed, zed_inverse, swished, output))
        resid, resid_normed, resid_inverse, lowered, mixed, sigmoid_gate, gated, zed, zed_inverse, swished, output = runs[0]
        patch_run = runs[1]
        grad_output = (cotangent[record].astype(jnp.float32) * valid).astype(jnp.bfloat16)
        grad_swished = lax.dot_general(grad_output, w_pointwise_out, (((1,), (1,)), ((), ())), preferred_element_type=jnp.float32)
        zed_sigmoid = jax.nn.sigmoid(zed)
        grad_zed = grad_swished * (zed_sigmoid * (1.0 + zed * (1.0 - zed_sigmoid)))
        grad_spread = norm_back(grad_zed, zed, zed_inverse)
        padded_grad = jnp.pad(grad_spread, ((half, half), (0, 0)))
        grad_gated = depthwise(padded_grad, depth_kernel[::-1], LENGTH) * valid
        grad_mixed = jnp.concatenate((grad_gated * sigmoid_gate, grad_gated * mixed[:, :width] * sigmoid_gate * (1.0 - sigmoid_gate)), axis=1).astype(jnp.bfloat16)
        grad_lowered = lax.dot_general(grad_mixed, w_pointwise_in, (((1,), (1,)), ((), ())), preferred_element_type=jnp.float32)
        grad_resid = grad_output.astype(jnp.float32) + norm_back(grad_lowered, resid_normed, resid_inverse)

        def score(patch_value, clean_value, grad):
            return lax.optimization_barrier(jnp.sum((patch_value.astype(jnp.float32) - clean_value.astype(jnp.float32)) * grad, axis=1))
        table = jnp.stack((score(patch_run[0], resid, grad_resid), score(patch_run[6], gated, grad_gated), score(patch_run[9], swished, grad_swished), score(patch_run[10], output, grad_output.astype(jnp.float32))), axis=0)
        chosen = (site_ids[:, None] == jnp.arange(4)[None, :]).astype(jnp.float32)
        tables.append(lax.optimization_barrier(jnp.sum(chosen[:, :, None] * table[None, :, :], axis=1)))
        lowered_all.append(lowered)
        grad_mixed_all.append(grad_mixed)
        swished_all.append(swished)
        grad_output_all.append(grad_output)
    attribution = jnp.stack(tables, axis=0)
    grad_pointwise_in = contract_rows(jnp.concatenate(lowered_all, axis=0), jnp.concatenate(grad_mixed_all, axis=0))
    grad_pointwise_out = contract_rows(jnp.concatenate(swished_all, axis=0), jnp.concatenate(grad_output_all, axis=0))
    return (attribution, grad_pointwise_in, grad_pointwise_out)
```

```python
import jax
import jax.numpy as jnp
from jax import lax
from jax.experimental import pallas as pl
from jax.experimental.pallas import tpu as pltpu
from jax.sharding import PartitionSpec as P

HEADS = 8
DH = 64
KERNEL = 31
RIM = 32
EPSILON = 1e-05
FLOOR = -1e30
LOG2E = 1.4426950408889634
F32 = jnp.float32
BF16 = jnp.bfloat16
ROWS = 128
WIDTH = 1024
CLEAN = ROWS + 2 * RIM
PATCH = ROWS + RIM
BOTH = CLEAN + PATCH
INNER = ROWS + RIM


def lane_of(rows):
    return lax.broadcasted_iota(jnp.int32, (rows, 128), 1)


def swap(tile):
    return pltpu.roll(tile, 64, 1)


def moments(values):
    mean = jnp.mean(values, axis=-1, keepdims=True)
    centred = values - mean
    variance = jnp.mean(centred * centred, axis=-1, keepdims=True)
    return centred, lax.rsqrt(variance + EPSILON)


def dot(left, right):
    return jnp.dot(left, right, preferred_element_type=F32)


def dot_nt(left, right):
    return lax.dot_general(left, right, (((1,), (1,)), ((), ())), preferred_element_type=F32)


def dot_tn(left, right):
    return lax.dot_general(left, right, (((0,), (0,)), ((), ())), preferred_element_type=F32)


def sigmoid(values):
    return 1.0 / (1.0 + jnp.exp(-values))


def lane_sum(values):
    total = values[:, :128]
    for start in range(128, values.shape[1], 128):
        total = total + values[:, start : start + 128]
    return total


def project_kernel(
    clean_ref, corrupt_ref, cot_ref, mask_ref, wq_ref, wk_ref, wv_ref,
    msg_ref, patched_ref, up_ref, down_ref, hidden_ref, mask_col,
):
    spread_mask = jnp.broadcast_to(mask_ref[...].astype(F32), (ROWS, ROWS))
    mask_col[...] = spread_mask.T

    def rows(i, carry):
        at = pl.ds(pl.multiple_of(i * 16, 16), 16)
        below = pl.ds(pl.multiple_of(ROWS + i * 16, 16), 16)
        clean = clean_ref[at, :].astype(F32)
        corrupt = corrupt_ref[at, :].astype(F32)
        patched = jnp.where(mask_col[at, 0:1] == 1.0, corrupt, clean)
        patched_ref[at, :] = patched.astype(BF16)
        for dest, source in ((at, clean), (below, patched)):
            centred, inverse = moments(source)
            hidden_ref[dest, :] = (centred * inverse).astype(BF16)
        return carry

    lax.fori_loop(0, ROWS // 16, rows, 0)
    half = RIM // 2
    up_ref[0:RIM, :] = clean_ref[ROWS - RIM : ROWS, :]
    up_ref[RIM : RIM + half, :] = patched_ref[ROWS - half : ROWS, :]
    up_ref[RIM + half :, :] = cot_ref[ROWS - half : ROWS, :]
    down_ref[0:RIM, :] = clean_ref[0:RIM, :]
    down_ref[RIM : RIM + half, :] = patched_ref[0:half, :]
    down_ref[RIM + half :, :] = cot_ref[0:half, :]

    low = lane_of(ROWS) < 64
    low_q = lane_of(32) < 64
    for pair in range(2):
        cols = slice(pair * 256, pair * 256 + 256)
        hidden = hidden_ref[...]
        query = dot(hidden, wq_ref[:, cols])
        keys = dot(hidden, wk_ref[:, cols])
        values = dot(hidden, wv_ref[:, cols])
        for sub in range(2):
            tile = slice(sub * 128, sub * 128 + 128)
            for run in range(2):
                part = slice(run * ROWS, run * ROWS + ROWS)
                k, v, q = keys[part, tile], values[part, tile], query[part, tile]
                base = run * 16 + (pair * 2 + sub) * 4
                even = jnp.where(low, k, swap(v)).astype(BF16)
                odd = jnp.where(low, swap(k), v).astype(BF16)
                for side in range(2):
                    msg_ref[base + side, 0:ROWS, :] = even
                    msg_ref[base + 2 + side, 0:ROWS, :] = odd
                    qa = q[side * 64 : side * 64 + 32]
                    qb = q[side * 64 + 32 : side * 64 + 64]
                    msg_ref[base + side, ROWS : ROWS + 32, :] = jnp.where(
                        low_q, qa, swap(qb)
                    ).astype(BF16)
                    msg_ref[base + 2 + side, ROWS : ROWS + 32, :] = jnp.where(
                        low_q, swap(qa), qb
                    ).astype(BF16)


def attend_kernel(scal_ref, recv_ref, out_ref, kt_ref, v_ref, s0_ref, s1_ref, m0_ref, m1_ref, c_ref):
    length = scal_ref[1]
    side = scal_ref[3]
    sources = recv_ref.shape[0]
    count = sources * ROWS
    lane = lane_of(ROWS)

    def load(s, carry):
        kv = recv_ref[s, 0:ROWS, :].astype(F32)
        frame = s * ROWS + lax.broadcasted_iota(jnp.int32, (ROWS, 128), 0)
        bias = jnp.where(frame < length, 0.0, FLOOR)
        keyed = jnp.where(lane < 64, kv, jnp.where(lane == 64, bias, 0.0))
        at = pl.ds(pl.multiple_of(s * ROWS, ROWS), ROWS)
        kt_ref[:, at] = keyed.T.astype(BF16)
        v_ref[at, :] = jnp.where(lane < 64, 1.0, kv).astype(BF16)
        return carry

    lax.fori_loop(0, sources, load, 0)

    chunk = 512
    pieces = count // chunk
    blocks = sources // 4
    scale = DH ** (-0.5) * LOG2E

    def queries(b):
        raw = recv_ref[pl.ds(b * 4, 4), ROWS : ROWS + 32, :].astype(F32).reshape(128, 128)
        fill = jnp.where(lane == 64, 1.0, 0.0)
        return jnp.concatenate(
            [jnp.where(lane < 64, raw, fill), jnp.where(lane < 64, swap(raw), fill)], axis=0
        ).astype(BF16)

    def score_piece(query, s_ref, k, top):
        scores = dot(query, kt_ref[:, k * chunk : (k + 1) * chunk])
        s_ref[:, k * chunk : (k + 1) * chunk] = scores
        for j in range(chunk // 128):
            tile = scores[:, j * 128 : (j + 1) * 128]
            top = tile if top is None else jnp.maximum(top, tile)
        return top

    def finish_top(m_ref, top):
        m_ref[...] = jnp.broadcast_to(jnp.max(top, axis=1, keepdims=True), (256, 128))

    def weigh_piece(s_ref, top, k, accum):
        scores = s_ref[:, k * chunk : (k + 1) * chunk]
        weights = jnp.exp2((scores - top) * scale).astype(BF16)
        addend = dot(weights, v_ref[k * chunk : (k + 1) * chunk, :])
        return addend if accum is None else accum + addend

    def store(b, accum):
        first, second = accum[:128], accum[128:]
        result = jnp.where(lane < 64, swap(first) / first, second / swap(second))
        c_ref[pl.ds(b * 128, 128), :] = result

    def step(b, s_ref, m_ref, next_b, next_s, next_m):
        query = None if next_s is None else queries(next_b)
        top, accum = None, None
        best = jnp.tile(m_ref[...], (1, chunk // 128))
        for k in range(pieces):
            if query is not None:
                top = score_piece(query, next_s, k, top)
            accum = weigh_piece(s_ref, best, k, accum)
        if query is not None:
            finish_top(next_m, top)
        store(b, accum)

    query, top = queries(0), None
    for k in range(pieces):
        top = score_piece(query, s0_ref, k, top)
    finish_top(m0_ref, top)

    def pair(i, carry):
        step(2 * i, s0_ref, m0_ref, 2 * i + 1, s1_ref, m1_ref)
        step(2 * i + 1, s1_ref, m1_ref, 2 * i + 2, s0_ref, m0_ref)
        return carry

    lax.fori_loop(0, blocks // 2 - 1, pair, 0)
    step(blocks - 2, s0_ref, m0_ref, blocks - 1, s1_ref, m1_ref)
    step(blocks - 1, s1_ref, m1_ref, None, None, None)

    low = lane_of(16) < 64

    def pack(d, carry):
        own = c_ref[pl.ds(pl.multiple_of(d * 32, 32), 32), :]
        after = lax.rem(d + 1, sources)
        before = lax.rem(d + sources - 1, sources)
        other = jnp.where(side == 0, after, before)
        rim = c_ref[pl.ds(pl.multiple_of(other * 32, 32), 32), :]
        first, second = rim[:16], rim[16:]
        rim_a = jnp.where(low, first, swap(second))
        rim_b = jnp.where(low, swap(first), second)
        out_ref[d, 0:32, :] = own.astype(BF16)
        out_ref[d, 32:48, :] = jnp.where(side == 0, rim_a, rim_b).astype(BF16)
        return carry

    lax.fori_loop(0, sources, pack, 0)


def depthwise(source, source_row, taps_ref, order, target, count):
    def rows(i, carry):
        first = source_row + i * 8
        taps = [taps_ref[t * 8 : t * 8 + 8, :] for t in order]
        sums = [None] * 8
        for s in range(KERNEL + 7):
            piece = source[pl.ds(pl.multiple_of((first + s) * 8, 8), 8), :]
            for o in range(8):
                if 0 <= s - o < KERNEL:
                    term = taps[s - o] * piece
                    sums[o] = term if sums[o] is None else sums[o] + term
        for o in range(8):
            target[pl.ds(pl.multiple_of((i * 8 + o) * 8, 8), 8), :] = sums[o]
        return carry

    lax.fori_loop(0, count // 8, rows, 0)


def put_rows(ref, row, tile, values):
    for r in range(0, values.shape[0], 8):
        ref[pl.ds((row + r) * 8 + tile, 8, stride=8), :] = values[r : r + 8]


def get_rows(ref, row, count):
    groups = []
    for r in range(0, count, 8):
        tiles = [ref[pl.ds((row + r) * 8 + t, 8, stride=8), :] for t in range(8)]
        groups.append(jnp.concatenate(tiles, axis=1))
    return jnp.concatenate(groups, axis=0) if len(groups) > 1 else groups[0]


def block_kernel(
    scal_ref, site_ref, ctx_in, clean_ref, patched_ref, cot_ref, up_ref, down_ref,
    wao_ref, win_ref, depth_ref, wout_ref,
    attr_ref, own_ref, send_ref, gm_ref, go_ref,
    ctx_ref, x_ref, resid_ref, low_ref, mv_ref, sg_ref, g2_ref, s2_ref, zed_ref, zinv_ref,
    sw_ref, gox_ref, gs_ref, gsp2_ref, gg2_ref, gl_ref, t0_ref, t1_ref, t2_ref, taps_ref,
):
    first_frame, length, core = scal_ref[0], scal_ref[1], scal_ref[2]
    half = RIM // 2

    for run in range(2):
        for t in range(HEADS // 2):
            at = slice(t * 128, t * 128 + 128)
            base = run * 16 + t * 4
            halves = {}
            for side in range(2):
                even = ctx_in[base + side].astype(F32)
                odd = ctx_in[base + 2 + side].astype(F32)
                low = lane_of(48) < 64
                halves[side] = (
                    jnp.where(low, even, swap(odd)).astype(BF16),
                    jnp.where(low, swap(even), odd).astype(BF16),
                )
            (lo0, hi0), (lo1, hi1) = halves[0], halves[1]
            parts = [lo1[32:48], hi1[32:48], lo0[:32], hi0[:32], lo1[:32], hi1[:32], lo0[32:48], hi0[32:48]]
            row = 0
            if run == 1:
                parts = parts[1:-1]
                row = CLEAN
            for part in parts:
                ctx_ref[row : row + part.shape[0], at] = part
                row += part.shape[0]

    x_ref[0:RIM, :] = up_ref[0:RIM, :]
    x_ref[RIM : RIM + ROWS, :] = clean_ref[...]
    x_ref[RIM + ROWS : CLEAN, :] = down_ref[0:RIM, :]
    x_ref[CLEAN : CLEAN + half, :] = up_ref[RIM : RIM + half, :]
    x_ref[CLEAN + half : CLEAN + half + ROWS, :] = patched_ref[...]
    x_ref[CLEAN + half + ROWS : BOTH, :] = down_ref[RIM : RIM + half, :]

    for r in range(0, KERNEL + 1, 8):
        got = min(8, KERNEL - r)
        block = depth_ref[r : r + got, :].astype(F32)
        if got < 8:
            block = jnp.concatenate([block, jnp.zeros((8 - got, WIDTH), F32)], axis=0)
        for t in range(8):
            put_rows(taps_ref, r, t, block[:, t * 128 : t * 128 + 128])

    frame0 = first_frame - half
    for piece, row, offset in (
        (up_ref[RIM + half :, :], 0, -half),
        (cot_ref[...], half, 0),
        (down_ref[RIM + half :, :], half + ROWS, ROWS),
    ):
        n = piece.shape[0]
        frame = first_frame + offset + lax.broadcasted_iota(jnp.int32, (n, 1), 0)
        keep = jnp.where(frame < length, 1.0, 0.0)
        gox_ref[row : row + n, :] = (piece.astype(F32) * keep).astype(BF16)
    go_ref[...] = gox_ref[half : half + ROWS, :]

    for j in range(4):
        at = slice(j * 256, j * 256 + 256)
        joined = x_ref[:, at].astype(F32) + dot(ctx_ref[...], wao_ref[:, at])
        resid_ref[:, at] = joined.astype(BF16)

    def lower(i, carry):
        at = pl.ds(pl.multiple_of(i * 16, 16), 16)
        centred, inverse = moments(resid_ref[at, :].astype(F32))
        low_ref[at, :] = (centred * inverse).astype(BF16)
        return carry

    lax.fori_loop(0, BOTH // 16, lower, 0)

    row = lax.broadcasted_iota(jnp.int32, (BOTH, 1), 0)
    frame = first_frame + jnp.where(row < CLEAN, row - RIM, row - CLEAN - half)
    live = jnp.where((frame >= 0) & (frame < length), 1.0, 0.0)
    for j in range(4):
        at = slice(j * 256, j * 256 + 256)
        gate_at = slice(WIDTH + j * 256, WIDTH + j * 256 + 256)
        value = dot(low_ref[...], win_ref[:, at])
        gate = sigmoid(dot(low_ref[...], win_ref[:, gate_at]))
        mv_ref[:, at] = value[RIM : RIM + ROWS]
        sg_ref[:, at] = gate[RIM : RIM + ROWS]
        gated = (value * gate * live).astype(BF16).astype(F32)
        for t in range(2):
            put_rows(g2_ref, 0, j * 2 + t, gated[:, t * 128 : t * 128 + 128])

    forward = list(range(KERNEL))
    edge = half - KERNEL // 2
    depthwise(g2_ref, edge, taps_ref, forward, s2_ref, INNER)

    def clean_rows(i, carry):
        r = pl.multiple_of(i * 16, 16)
        centred, inverse = moments(get_rows(s2_ref, r, 16))
        zed = centred * inverse
        zed_ref[pl.ds(r, 16), :] = zed
        zinv_ref[pl.ds(r, 16), :] = jnp.broadcast_to(inverse, (16, 128))
        sw_ref[pl.ds(r, 16), :] = (zed * sigmoid(zed)).astype(BF16)
        return carry

    lax.fori_loop(0, INNER // 16, clean_rows, 0)
    depthwise(g2_ref, CLEAN + edge, taps_ref, forward, s2_ref, ROWS)

    def patch_rows(i, carry):
        r = pl.multiple_of(i * 16, 16)
        centred, inverse = moments(get_rows(s2_ref, r, 16))
        zed = centred * inverse
        sw_ref[pl.ds(pl.multiple_of(INNER + r, 16), 16), :] = (zed * sigmoid(zed)).astype(BF16)
        return carry

    lax.fori_loop(0, ROWS // 16, patch_rows, 0)

    t3 = jnp.zeros((ROWS, 128), F32)
    for j in range(4):
        at = slice(j * 256, j * 256 + 256)
        out = dot(sw_ref[half : INNER + ROWS, :], wout_ref[:, at])
        out_clean = resid_ref[RIM : RIM + ROWS, at].astype(F32) + out[:ROWS]
        out_patch = resid_ref[CLEAN + half : CLEAN + half + ROWS, at].astype(F32) + out[ROWS + half :]
        gap = out_patch.astype(BF16).astype(F32) - out_clean.astype(BF16).astype(F32)
        t3 = t3 + lane_sum(gap * go_ref[:, at].astype(F32))

    for j in range(4):
        at = slice(j * 256, j * 256 + 256)
        gs_ref[:, at] = dot_nt(gox_ref[...], wout_ref[at, :])

    def back_rows(i, carry):
        r = pl.multiple_of(i * 16, 16)
        zed = zed_ref[pl.ds(r, 16), :]
        grad = gs_ref[pl.ds(r, 16), :]
        gate = sigmoid(zed)
        grad_zed = grad * (gate * (1.0 + zed * (1.0 - gate)))
        mean = jnp.mean(grad_zed, axis=-1, keepdims=True)
        along = jnp.mean(grad_zed * zed, axis=-1, keepdims=True)
        result = (grad_zed - mean - zed * along) * zinv_ref[pl.ds(r, 16), 0:1]
        for g in range(0, 16, 8):
            for t in range(8):
                gsp2_ref[pl.ds((r + g) * 8 + t, 8, stride=8), :] = result[
                    g : g + 8, t * 128 : t * 128 + 128
                ]
        return carry

    lax.fori_loop(0, INNER // 16, back_rows, 0)

    def swished_rows(i, carry):
        r = pl.multiple_of(i * 16, 16)
        inner = pl.ds(pl.multiple_of(half + r, 16), 16)
        other = pl.ds(pl.multiple_of(INNER + r, 16), 16)
        gap = sw_ref[other, :].astype(F32) - sw_ref[inner, :].astype(F32)
        t2_ref[pl.ds(r, 16), :] = lane_sum(gap * gs_ref[inner, :])
        return carry

    lax.fori_loop(0, ROWS // 16, swished_rows, 0)
    depthwise(gsp2_ref, edge, taps_ref, forward[::-1], gg2_ref, ROWS)

    def mixed_rows(i, carry):
        r = pl.multiple_of(i * 16, 16)
        at = pl.ds(r, 16)
        frame = first_frame + r + lax.broadcasted_iota(jnp.int32, (16, 1), 0)
        grad = get_rows(gg2_ref, r, 16) * jnp.where(frame < length, 1.0, 0.0)
        gap = get_rows(g2_ref, CLEAN + half + r, 16) - get_rows(g2_ref, RIM + r, 16)
        t1_ref[at, :] = lane_sum(gap * grad)
        gate = sg_ref[at, :]
        gm_ref[at, 0:WIDTH] = (grad * gate).astype(BF16)
        gm_ref[at, WIDTH:] = (grad * mv_ref[at, :] * gate * (1.0 - gate)).astype(BF16)
        return carry

    lax.fori_loop(0, ROWS // 16, mixed_rows, 0)
    for j in range(4):
        at = slice(j * 256, j * 256 + 256)
        gl_ref[:, at] = dot_nt(gm_ref[...], win_ref[at, :])

    def resid_rows(i, carry):
        r = pl.multiple_of(i * 16, 16)
        at = pl.ds(r, 16)
        clean = resid_ref[pl.ds(pl.multiple_of(RIM + r, 16), 16), :].astype(F32)
        patch = resid_ref[pl.ds(pl.multiple_of(CLEAN + half + r, 16), 16), :].astype(F32)
        centred, inverse = moments(clean)
        normed = centred * inverse
        grad = gl_ref[at, :]
        mean = jnp.mean(grad, axis=-1, keepdims=True)
        along = jnp.mean(grad * normed, axis=-1, keepdims=True)
        grad_resid = go_ref[at, :].astype(F32) + (grad - mean - normed * along) * inverse
        t0_ref[at, :] = lane_sum((patch - clean) * grad_resid)
        return carry

    lax.fori_loop(0, ROWS // 16, resid_rows, 0)

    columns = [
        jnp.sum(part, axis=1, keepdims=True) for part in (t0_ref[...], t1_ref[...], t2_ref[...], t3)
    ]
    lane = lane_of(ROWS)
    chosen = jnp.zeros((ROWS, 128), F32)
    for i in range(attr_ref.shape[0]):
        site = site_ref[i]
        column = columns[0]
        for k in range(1, 4):
            column = jnp.where(site == k, columns[k], column)
        chosen = jnp.where(lane == i, column, chosen)
    attr_ref[...] = chosen.T[: attr_ref.shape[0]]

    for part in range(4):
        lo = (part // 2) * 512
        dest = part * 256
        source = low_ref if part < 2 else sw_ref
        row = RIM if part < 2 else half
        lo = (part % 2) * 512
        first = source[row : row + ROWS, lo : lo + 256].astype(F32)
        second = source[row : row + ROWS, lo + 256 : lo + 512].astype(F32)
        own_ref[:, dest : dest + 256] = jnp.where(core == 0, first, second).astype(BF16)
        send_ref[:, dest : dest + 256] = jnp.where(core == 0, second, first).astype(BF16)


def weight_kernel(own_ref, other_ref, gm_ref, gm_other, go_ref, go_other, out_ref):
    low = jnp.concatenate([own_ref[:, 0:512], other_ref[:, 0:512]], axis=0)
    swished = jnp.concatenate([own_ref[:, 512:1024], other_ref[:, 512:1024]], axis=0)
    for j in range(0, 2 * WIDTH, 256):
        grads = jnp.concatenate([gm_ref[:, j : j + 256], gm_other[:, j : j + 256]], axis=0)
        out_ref[:, j : j + 256] = dot_tn(low, grads).astype(BF16)
    for j in range(0, WIDTH, 256):
        grads = jnp.concatenate([go_ref[:, j : j + 256], go_other[:, j : j + 256]], axis=0)
        out_ref[:, 2 * WIDTH + j : 2 * WIDTH + j + 256] = dot_tn(swished, grads).astype(BF16)


VMEM = pl.BlockSpec(memory_space=pltpu.VMEM)
SMEM = pl.BlockSpec(memory_space=pltpu.SMEM)


def kernel_call(body, out_shape, in_specs, scratch, limit, flops, moved):
    return pl.pallas_call(
        body,
        out_shape=out_shape,
        in_specs=in_specs,
        out_specs=[VMEM] * len(out_shape),
        scratch_shapes=scratch,
        compiler_params=pltpu.CompilerParams(vmem_limit_bytes=limit << 20),
        cost_estimate=pl.CostEstimate(flops=flops, bytes_accessed=moved, transcendentals=0),
    )


def shape(dims, dtype):
    return jax.ShapeDtypeStruct(dims, dtype)


def per_device(
    clean_input, corrupt_input, patch_mask, lengths, site_ids, w_query, w_key, w_value,
    w_attn_out, w_pointwise_in, depth_kernel, w_pointwise_out, cotangent,
):
    frames = lax.axis_size("frames")
    position = lax.axis_index("frames")
    core = lax.rem(lax.axis_index("dp"), 2)
    scalars = jnp.stack(
        [position * ROWS, lengths[0], core, lax.rem(position, 2)]
    ).astype(jnp.int32)
    clean, corrupt, cot = clean_input[0], corrupt_input[0], cotangent[0]

    msg, patched, up, down = kernel_call(
        project_kernel,
        [shape((frames, ROWS + 32, 128), BF16), shape((ROWS, WIDTH), BF16),
         shape((2 * RIM, WIDTH), BF16), shape((2 * RIM, WIDTH), BF16)],
        [VMEM] * 7,
        [pltpu.VMEM((2 * ROWS, WIDTH), BF16), pltpu.VMEM((ROWS, ROWS), F32)],
        24, 8 * 10**8, 6 * 10**6,
    )(clean, corrupt, cot, patch_mask, w_query, w_key, w_value)
    forward = [(i, i + 1) for i in range(frames - 1)]
    backward = [(i + 1, i) for i in range(frames - 1)]
    from_left = lax.ppermute(up, "frames", forward)
    from_right = lax.ppermute(down, "frames", backward)
    recv = lax.all_to_all(msg, "frames", 0, 0, tiled=True)
    count = frames * ROWS
    (context,) = kernel_call(
        attend_kernel,
        [shape((frames, 48, 128), BF16)],
        [SMEM, VMEM],
        [pltpu.VMEM((128, count), BF16), pltpu.VMEM((count, 128), BF16),
         pltpu.VMEM((256, count), F32), pltpu.VMEM((256, count), F32),
         pltpu.VMEM((256, 128), F32), pltpu.VMEM((256, 128), F32),
         pltpu.VMEM((frames * 32, 128), F32)],
        40, 8 * 10**9, 10**6,
    )(scalars, recv)
    contexts = lax.all_to_all(context, "frames", 0, 0, tiled=True)
    attribution, own, send, grad_mixed, grad_output = kernel_call(
        block_kernel,
        [shape((site_ids.shape[0], ROWS), F32), shape((ROWS, 1024), BF16), shape((ROWS, 1024), BF16),
         shape((ROWS, 2 * WIDTH), BF16), shape((ROWS, WIDTH), BF16)],
        [SMEM, SMEM] + [VMEM] * 10,
        [pltpu.VMEM((BOTH, 512), BF16), pltpu.VMEM((BOTH, WIDTH), BF16),
         pltpu.VMEM((BOTH, WIDTH), BF16), pltpu.VMEM((BOTH, WIDTH), BF16),
         pltpu.VMEM((ROWS, WIDTH), F32), pltpu.VMEM((ROWS, WIDTH), F32),
         pltpu.VMEM((BOTH * 8, 128), F32), pltpu.VMEM((INNER * 8, 128), F32),
         pltpu.VMEM((INNER, WIDTH), F32), pltpu.VMEM((INNER, 128), F32),
         pltpu.VMEM((INNER + ROWS, WIDTH), BF16), pltpu.VMEM((INNER, WIDTH), BF16),
         pltpu.VMEM((INNER, WIDTH), F32), pltpu.VMEM((INNER * 8, 128), F32),
         pltpu.VMEM((ROWS * 8, 128), F32), pltpu.VMEM((ROWS, WIDTH), F32),
         pltpu.VMEM((ROWS, 128), F32), pltpu.VMEM((ROWS, 128), F32), pltpu.VMEM((ROWS, 128), F32),
         pltpu.VMEM((32 * 8, 128), F32)],
        48, 4 * 10**9, 10**7,
    )(scalars, site_ids, contexts, clean, patched, cot, from_left, from_right,
      w_attn_out, w_pointwise_in, depth_kernel, w_pointwise_out)

    cores = [(i, i ^ 1) for i in range(lax.axis_size("dp"))]
    other, gm_other, go_other = (
        lax.ppermute(part, "dp", cores) for part in (send, grad_mixed, grad_output)
    )
    (partial,) = kernel_call(
        weight_kernel,
        [shape((512, 3 * WIDTH), BF16)],
        [VMEM] * 6,
        [],
        32, 8 * 10**8, 10**7,
    )(own, other, grad_mixed, gm_other, grad_output, go_other)
    groups = [
        [(2 * y + c) * frames + f for y in range(2) for f in range(frames)] for c in range(2)
    ]
    pieces = lax.all_to_all(
        partial.reshape(2 * frames, 8, 3 * WIDTH), ("dp", "frames"), 0, 0,
        axis_index_groups=groups, tiled=True,
    )
    summed = jnp.sum(pieces.astype(F32), axis=0)
    return attribution[None], summed[:, : 2 * WIDTH], summed[:, 2 * WIDTH :]


def solution(mesh):
    placed = (
        P("dp", "frames", None), P("dp", "frames", None), P("dp", "frames"), P("dp"), P(), P(), P(),
        P(), P(), P(), P(), P(), P("dp", "frames", None),
    )
    return jax.shard_map(
        per_device,
        mesh=mesh,
        in_specs=placed,
        out_specs=(P("dp", None, "frames"), P(("dp", "frames"), None), P(("dp", "frames"), None)),
        check_vma=False,
    )
```

```python
import jax
import jax.numpy as jnp
from jax import lax
from jax.experimental import pallas as pl
from jax.experimental.pallas import tpu as pltpu
from jax.sharding import PartitionSpec as P

HEADS = 8
DH = 64
KERNEL = 31
RIM = 32
EPSILON = 1e-05
FLOOR = -1e30
LOG2E = 1.4426950408889634
F32 = jnp.float32
BF16 = jnp.bfloat16
ROWS = 128
WIDTH = 1024
CLEAN = ROWS + 2 * RIM
PATCH = ROWS + RIM
BOTH = CLEAN + PATCH
INNER = ROWS + RIM


def lane_of(rows):
    return lax.broadcasted_iota(jnp.int32, (rows, 128), 1)


def swap(tile):
    return pltpu.roll(tile, 64, 1)


def moments(values):
    mean = jnp.mean(values, axis=-1, keepdims=True)
    centred = values - mean
    variance = jnp.mean(centred * centred, axis=-1, keepdims=True)
    return centred, lax.rsqrt(variance + EPSILON)


def dot(left, right):
    return jnp.dot(left, right, preferred_element_type=F32)


def dot_nt(left, right):
    return lax.dot_general(left, right, (((1,), (1,)), ((), ())), preferred_element_type=F32)


def dot_tn(left, right):
    return lax.dot_general(left, right, (((0,), (0,)), ((), ())), preferred_element_type=F32)


def sigmoid(values):
    return 1.0 / (1.0 + jnp.exp(-values))


def lane_sum(values):
    total = values[:, :128]
    for start in range(128, values.shape[1], 128):
        total = total + values[:, start : start + 128]
    return total


def project_kernel(
    clean_hbm, corrupt_hbm, cot_hbm, mask_ref, wq_hbm, wk_hbm, wv_hbm,
    msg_ref, patched_ref, up_ref, down_ref,
    hidden_ref, mask_col, clean_ref, corrupt_ref, wq_ref, wk_ref, wv_ref, sems,
):
    half = RIM // 2
    copies = [
        pltpu.make_async_copy(source, target, sems.at[i])
        for i, (source, target) in enumerate((
            (clean_hbm, clean_ref),
            (corrupt_hbm, corrupt_ref),
            (wk_hbm, wk_ref),
            (wv_hbm, wv_ref),
            (wq_hbm, wq_ref),
            (cot_hbm.at[pl.ds(ROWS - half, half)], up_ref.at[pl.ds(RIM + half, half)]),
            (cot_hbm.at[pl.ds(0, half)], down_ref.at[pl.ds(RIM + half, half)]),
        ))
    ]
    for copy in copies:
        copy.start()
    spread_mask = jnp.broadcast_to(mask_ref[...].astype(F32), (ROWS, ROWS))
    mask_col[...] = spread_mask.T
    copies[0].wait()
    copies[1].wait()

    def rows(i, carry):
        at = pl.ds(pl.multiple_of(i * 16, 16), 16)
        below = pl.ds(pl.multiple_of(ROWS + i * 16, 16), 16)
        clean = clean_ref[at, :].astype(F32)
        corrupt = corrupt_ref[at, :].astype(F32)
        patched = jnp.where(mask_col[at, 0:1] == 1.0, corrupt, clean)
        patched_ref[at, :] = patched.astype(BF16)
        for dest, source in ((at, clean), (below, patched)):
            centred, inverse = moments(source)
            hidden_ref[dest, :] = (centred * inverse).astype(BF16)
        return carry

    lax.fori_loop(0, ROWS // 16, rows, 0)
    up_ref[0:RIM, :] = clean_ref[ROWS - RIM : ROWS, :]
    up_ref[RIM : RIM + half, :] = patched_ref[ROWS - half : ROWS, :]
    down_ref[0:RIM, :] = clean_ref[0:RIM, :]
    down_ref[RIM : RIM + half, :] = patched_ref[0:half, :]
    for copy in copies[2:]:
        copy.wait()

    low = lane_of(ROWS) < 64
    low_q = lane_of(32) < 64
    for pair in range(2):
        cols = slice(pair * 256, pair * 256 + 256)
        hidden = hidden_ref[...]
        query = dot(hidden, wq_ref[:, cols])
        keys = dot(hidden, wk_ref[:, cols])
        values = dot(hidden, wv_ref[:, cols])
        for sub in range(2):
            tile = slice(sub * 128, sub * 128 + 128)
            for run in range(2):
                part = slice(run * ROWS, run * ROWS + ROWS)
                k, v, q = keys[part, tile], values[part, tile], query[part, tile]
                base = run * 16 + (pair * 2 + sub) * 4
                even = jnp.where(low, k, swap(v)).astype(BF16)
                odd = jnp.where(low, swap(k), v).astype(BF16)
                for side in range(2):
                    msg_ref[base + side, 0:ROWS, :] = even
                    msg_ref[base + 2 + side, 0:ROWS, :] = odd
                    qa = q[side * 64 : side * 64 + 32]
                    qb = q[side * 64 + 32 : side * 64 + 64]
                    msg_ref[base + side, ROWS : ROWS + 32, :] = jnp.where(
                        low_q, qa, swap(qb)
                    ).astype(BF16)
                    msg_ref[base + 2 + side, ROWS : ROWS + 32, :] = jnp.where(
                        low_q, swap(qa), qb
                    ).astype(BF16)


def attend_kernel(scal_ref, recv_ref, out_ref, kt_ref, v_ref, s0_ref, s1_ref, m0_ref, m1_ref, c_ref):
    length = scal_ref[1]
    side = scal_ref[3]
    sources = recv_ref.shape[0]
    count = sources * ROWS
    lane = lane_of(ROWS)

    def load(s, carry):
        kv = recv_ref[s, 0:ROWS, :].astype(F32)
        frame = s * ROWS + lax.broadcasted_iota(jnp.int32, (ROWS, 128), 0)
        bias = jnp.where(frame < length, 0.0, FLOOR)
        keyed = jnp.where(lane < 64, kv, jnp.where(lane == 64, bias, 0.0))
        at = pl.ds(pl.multiple_of(s * ROWS, ROWS), ROWS)
        kt_ref[:, at] = keyed.T.astype(BF16)
        v_ref[at, :] = jnp.where(lane < 64, 1.0, kv).astype(BF16)
        return carry

    lax.fori_loop(0, sources, load, 0)

    chunk = 512
    pieces = count // chunk
    blocks = sources // 4
    scale = DH ** (-0.5) * LOG2E

    def queries(b):
        raw = recv_ref[pl.ds(b * 4, 4), ROWS : ROWS + 32, :].astype(F32).reshape(128, 128)
        fill = jnp.where(lane == 64, 1.0, 0.0)
        return jnp.concatenate(
            [jnp.where(lane < 64, raw, fill), jnp.where(lane < 64, swap(raw), fill)], axis=0
        ).astype(BF16)

    def score_piece(query, s_ref, k, top):
        scores = dot(query, kt_ref[:, k * chunk : (k + 1) * chunk])
        s_ref[:, k * chunk : (k + 1) * chunk] = scores
        for j in range(chunk // 128):
            tile = scores[:, j * 128 : (j + 1) * 128]
            top = tile if top is None else jnp.maximum(top, tile)
        return top

    def finish_top(m_ref, top):
        m_ref[...] = jnp.broadcast_to(jnp.max(top, axis=1, keepdims=True), (256, 128))

    def weigh_piece(s_ref, top, k, accum):
        scores = s_ref[:, k * chunk : (k + 1) * chunk]
        weights = jnp.exp2((scores - top) * scale).astype(BF16)
        addend = dot(weights, v_ref[k * chunk : (k + 1) * chunk, :])
        return addend if accum is None else accum + addend

    def store(b, accum):
        first, second = accum[:128], accum[128:]
        result = jnp.where(lane < 64, swap(first) / first, second / swap(second))
        c_ref[pl.ds(b * 128, 128), :] = result

    def step(b, s_ref, m_ref, next_b, next_s, next_m):
        query = None if next_s is None else queries(next_b)
        top, accum = None, None
        best = jnp.tile(m_ref[...], (1, chunk // 128))
        for k in range(pieces):
            if query is not None:
                top = score_piece(query, next_s, k, top)
            accum = weigh_piece(s_ref, best, k, accum)
        if query is not None:
            finish_top(next_m, top)
        store(b, accum)

    query, top = queries(0), None
    for k in range(pieces):
        top = score_piece(query, s0_ref, k, top)
    finish_top(m0_ref, top)

    def pair(i, carry):
        step(2 * i, s0_ref, m0_ref, 2 * i + 1, s1_ref, m1_ref)
        step(2 * i + 1, s1_ref, m1_ref, 2 * i + 2, s0_ref, m0_ref)
        return carry

    lax.fori_loop(0, blocks // 2 - 1, pair, 0)
    step(blocks - 2, s0_ref, m0_ref, blocks - 1, s1_ref, m1_ref)
    step(blocks - 1, s1_ref, m1_ref, None, None, None)

    low = lane_of(16) < 64

    def pack(d, carry):
        own = c_ref[pl.ds(pl.multiple_of(d * 32, 32), 32), :]
        after = lax.rem(d + 1, sources)
        before = lax.rem(d + sources - 1, sources)
        other = jnp.where(side == 0, after, before)
        rim = c_ref[pl.ds(pl.multiple_of(other * 32, 32), 32), :]
        first, second = rim[:16], rim[16:]
        rim_a = jnp.where(low, first, swap(second))
        rim_b = jnp.where(low, swap(first), second)
        out_ref[d, 0:32, :] = own.astype(BF16)
        out_ref[d, 32:48, :] = jnp.where(side == 0, rim_a, rim_b).astype(BF16)
        return carry

    lax.fori_loop(0, sources, pack, 0)


def depthwise(source, source_row, taps_ref, order, target, count):
    def rows(i, carry):
        first = source_row + i * 8
        taps = [taps_ref[t * 8 : t * 8 + 8, :] for t in order]
        sums = [None] * 8
        for s in range(KERNEL + 7):
            piece = source[pl.ds(pl.multiple_of((first + s) * 8, 8), 8), :]
            for o in range(8):
                if 0 <= s - o < KERNEL:
                    term = taps[s - o] * piece
                    sums[o] = term if sums[o] is None else sums[o] + term
        for o in range(8):
            target[pl.ds(pl.multiple_of((i * 8 + o) * 8, 8), 8), :] = sums[o]
        return carry

    lax.fori_loop(0, count // 8, rows, 0)


def put_rows(ref, row, tile, values):
    for r in range(0, values.shape[0], 8):
        ref[pl.ds((row + r) * 8 + tile, 8, stride=8), :] = values[r : r + 8]


def get_rows(ref, row, count):
    groups = []
    for r in range(0, count, 8):
        tiles = [ref[pl.ds((row + r) * 8 + t, 8, stride=8), :] for t in range(8)]
        groups.append(jnp.concatenate(tiles, axis=1))
    return jnp.concatenate(groups, axis=0) if len(groups) > 1 else groups[0]


def place_context(ctx_in, ctx_ref, run, trimmed):
    low = lane_of(48) < 64
    for t in range(HEADS // 2):
        at = slice(t * 128, t * 128 + 128)
        base = run * 16 + t * 4
        halves = []
        for side in range(2):
            even = ctx_in[base + side].astype(F32)
            odd = ctx_in[base + 2 + side].astype(F32)
            halves.append((
                jnp.where(low, even, swap(odd)).astype(BF16),
                jnp.where(low, swap(even), odd).astype(BF16),
            ))
        (lo0, hi0), (lo1, hi1) = halves
        parts = [lo1[32:48], hi1[32:48], lo0[:32], hi0[:32], lo1[:32], hi1[:32], lo0[32:48], hi0[32:48]]
        row = 0
        for part in parts[1:-1] if trimmed else parts:
            ctx_ref[row : row + part.shape[0], at] = part
            row += part.shape[0]


def place_taps(depth_ref, taps_ref):
    for r in range(0, KERNEL + 1, 8):
        got = min(8, KERNEL - r)
        block = depth_ref[r : r + got, :].astype(F32)
        if got < 8:
            block = jnp.concatenate([block, jnp.zeros((8 - got, WIDTH), F32)], axis=0)
        for t in range(8):
            put_rows(taps_ref, r, t, block[:, t * 128 : t * 128 + 128])


def to_lowered(x_ref, ctx_ref, wao_ref, resid_ref, low_ref):
    for j in range(4):
        at = slice(j * 256, j * 256 + 256)
        joined = x_ref[:, at].astype(F32) + dot(ctx_ref[...], wao_ref[:, at])
        resid_ref[:, at] = joined.astype(BF16)

    def lower(i, carry):
        at = pl.ds(pl.multiple_of(i * 16, 16), 16)
        centred, inverse = moments(resid_ref[at, :].astype(F32))
        low_ref[at, :] = (centred * inverse).astype(BF16)
        return carry

    lax.fori_loop(0, x_ref.shape[0] // 16, lower, 0)


def to_gated(low_ref, win_ref, g2_ref, frame, length, keep):
    live = jnp.where((frame >= 0) & (frame < length), 1.0, 0.0)
    for j in range(4):
        at = slice(j * 256, j * 256 + 256)
        gate_at = slice(WIDTH + j * 256, WIDTH + j * 256 + 256)
        value = dot(low_ref[...], win_ref[:, at])
        gate = sigmoid(dot(low_ref[...], win_ref[:, gate_at]))
        if keep is not None:
            mv_ref, sg_ref = keep
            mv_ref[:, at] = value[RIM : RIM + ROWS]
            sg_ref[:, at] = gate[RIM : RIM + ROWS]
        gated = (value * gate * live).astype(BF16).astype(F32)
        for t in range(2):
            put_rows(g2_ref, 0, j * 2 + t, gated[:, t * 128 : t * 128 + 128])


def clean_kernel(
    scal_ref, ctx_in, clean_ref, cot_ref, up_ref, down_ref,
    wao_ref, win_ref, depth_ref, wout_ref,
    own_ref, send_ref, gm_ref, go_ref, sw_ref, gs_ref, gg2_ref, g2_ref, resid_ref,
    ctx_ref, x_ref, low_ref, mv_ref, sg_ref, s2_ref, zed_ref, zinv_ref, gox_ref, gsp2_ref, taps_ref,
):
    first_frame, length, core = scal_ref[0], scal_ref[1], scal_ref[2]
    half = RIM // 2
    place_context(ctx_in, ctx_ref, 0, False)
    x_ref[0:RIM, :] = up_ref[0:RIM, :]
    x_ref[RIM : RIM + ROWS, :] = clean_ref[...]
    x_ref[RIM + ROWS : CLEAN, :] = down_ref[0:RIM, :]
    place_taps(depth_ref, taps_ref)
    for piece, row, offset in (
        (up_ref[RIM + half :, :], 0, -half),
        (cot_ref[...], half, 0),
        (down_ref[RIM + half :, :], half + ROWS, ROWS),
    ):
        n = piece.shape[0]
        frame = first_frame + offset + lax.broadcasted_iota(jnp.int32, (n, 1), 0)
        keep = jnp.where(frame < length, 1.0, 0.0)
        gox_ref[row : row + n, :] = (piece.astype(F32) * keep).astype(BF16)
    go_ref[...] = gox_ref[half : half + ROWS, :]

    to_lowered(x_ref, ctx_ref, wao_ref, resid_ref, low_ref)
    frame = first_frame - RIM + lax.broadcasted_iota(jnp.int32, (CLEAN, 1), 0)
    to_gated(low_ref, win_ref, g2_ref, frame, length, (mv_ref, sg_ref))
    forward = list(range(KERNEL))
    edge = half - KERNEL // 2
    depthwise(g2_ref, edge, taps_ref, forward, s2_ref, INNER)

    def clean_rows(i, carry):
        r = pl.multiple_of(i * 16, 16)
        centred, inverse = moments(get_rows(s2_ref, r, 16))
        zed = centred * inverse
        zed_ref[pl.ds(r, 16), :] = zed
        zinv_ref[pl.ds(r, 16), :] = jnp.broadcast_to(inverse, (16, 128))
        sw_ref[pl.ds(r, 16), :] = (zed * sigmoid(zed)).astype(BF16)
        return carry

    lax.fori_loop(0, INNER // 16, clean_rows, 0)

    for j in range(4):
        at = slice(j * 256, j * 256 + 256)
        gs_ref[:, at] = dot_nt(gox_ref[...], wout_ref[at, :])

    def back_rows(i, carry):
        r = pl.multiple_of(i * 16, 16)
        zed = zed_ref[pl.ds(r, 16), :]
        grad = gs_ref[pl.ds(r, 16), :]
        gate = sigmoid(zed)
        grad_zed = grad * (gate * (1.0 + zed * (1.0 - gate)))
        mean = jnp.mean(grad_zed, axis=-1, keepdims=True)
        along = jnp.mean(grad_zed * zed, axis=-1, keepdims=True)
        result = (grad_zed - mean - zed * along) * zinv_ref[pl.ds(r, 16), 0:1]
        for g in range(0, 16, 8):
            for t in range(8):
                gsp2_ref[pl.ds((r + g) * 8 + t, 8, stride=8), :] = result[
                    g : g + 8, t * 128 : t * 128 + 128
                ]
        return carry

    lax.fori_loop(0, INNER // 16, back_rows, 0)
    depthwise(gsp2_ref, edge, taps_ref, forward[::-1], gg2_ref, ROWS)

    def mixed_rows(i, carry):
        r = pl.multiple_of(i * 16, 16)
        at = pl.ds(r, 16)
        frame = first_frame + r + lax.broadcasted_iota(jnp.int32, (16, 1), 0)
        grad = get_rows(gg2_ref, r, 16) * jnp.where(frame < length, 1.0, 0.0)
        gate = sg_ref[at, :]
        gm_ref[at, 0:WIDTH] = (grad * gate).astype(BF16)
        gm_ref[at, WIDTH:] = (grad * mv_ref[at, :] * gate * (1.0 - gate)).astype(BF16)
        return carry

    lax.fori_loop(0, ROWS // 16, mixed_rows, 0)

    for part in range(4):
        dest = part * 256
        source, row = (low_ref, RIM) if part < 2 else (sw_ref, half)
        lo = (part % 2) * 512
        first = source[row : row + ROWS, lo : lo + 256].astype(F32)
        second = source[row : row + ROWS, lo + 256 : lo + 512].astype(F32)
        own_ref[:, dest : dest + 256] = jnp.where(core == 0, first, second).astype(BF16)
        send_ref[:, dest : dest + 256] = jnp.where(core == 0, second, first).astype(BF16)


def patch_kernel(
    scal_ref, site_ref, ctx_in, patched_ref, up_ref, down_ref,
    wao_ref, win_ref, depth_ref, wout_ref,
    gm_ref, go_ref, swc_ref, gs_ref, gg2_ref, g2c_ref, residc_ref,
    attr_ref,
    ctx_ref, x_ref, resid_ref, low_ref, g2_ref, s2_ref, sw_ref, gl_ref, t0_ref, t1_ref, t2_ref, taps_ref,
):
    first_frame, length = scal_ref[0], scal_ref[1]
    half = RIM // 2
    place_context(ctx_in, ctx_ref, 1, True)
    x_ref[0:half, :] = up_ref[RIM : RIM + half, :]
    x_ref[half : half + ROWS, :] = patched_ref[...]
    x_ref[half + ROWS : PATCH, :] = down_ref[RIM : RIM + half, :]
    place_taps(depth_ref, taps_ref)
    to_lowered(x_ref, ctx_ref, wao_ref, resid_ref, low_ref)
    frame = first_frame - half + lax.broadcasted_iota(jnp.int32, (PATCH, 1), 0)
    to_gated(low_ref, win_ref, g2_ref, frame, length, None)
    depthwise(g2_ref, half - KERNEL // 2, taps_ref, list(range(KERNEL)), s2_ref, ROWS)
    sw_ref[0:ROWS, :] = swc_ref[half : half + ROWS, :]

    def patch_rows(i, carry):
        r = pl.multiple_of(i * 16, 16)
        at = pl.ds(r, 16)
        inner = pl.ds(pl.multiple_of(half + r, 16), 16)
        centred, inverse = moments(get_rows(s2_ref, r, 16))
        zed = centred * inverse
        swished = (zed * sigmoid(zed)).astype(BF16)
        sw_ref[pl.ds(pl.multiple_of(ROWS + r, 16), 16), :] = swished
        gap = swished.astype(F32) - sw_ref[at, :].astype(F32)
        t2_ref[at, :] = lane_sum(gap * gs_ref[inner, :])
        frame = first_frame + r + lax.broadcasted_iota(jnp.int32, (16, 1), 0)
        grad = get_rows(gg2_ref, r, 16) * jnp.where(frame < length, 1.0, 0.0)
        gap = get_rows(g2_ref, half + r, 16) - get_rows(g2c_ref, RIM + r, 16)
        t1_ref[at, :] = lane_sum(gap * grad)
        return carry

    lax.fori_loop(0, ROWS // 16, patch_rows, 0)

    t3 = jnp.zeros((ROWS, 128), F32)
    for j in range(4):
        at = slice(j * 256, j * 256 + 256)
        out = dot(sw_ref[...], wout_ref[:, at])
        out_clean = residc_ref[RIM : RIM + ROWS, at].astype(F32) + out[:ROWS]
        out_patch = resid_ref[half : half + ROWS, at].astype(F32) + out[ROWS:]
        gap = out_patch.astype(BF16).astype(F32) - out_clean.astype(BF16).astype(F32)
        t3 = t3 + lane_sum(gap * go_ref[:, at].astype(F32))
    for j in range(4):
        at = slice(j * 256, j * 256 + 256)
        gl_ref[:, at] = dot_nt(gm_ref[...], win_ref[at, :])

    def resid_rows(i, carry):
        r = pl.multiple_of(i * 16, 16)
        at = pl.ds(r, 16)
        clean = residc_ref[pl.ds(pl.multiple_of(RIM + r, 16), 16), :].astype(F32)
        patch = resid_ref[pl.ds(pl.multiple_of(half + r, 16), 16), :].astype(F32)
        centred, inverse = moments(clean)
        normed = centred * inverse
        grad = gl_ref[at, :]
        mean = jnp.mean(grad, axis=-1, keepdims=True)
        along = jnp.mean(grad * normed, axis=-1, keepdims=True)
        grad_resid = go_ref[at, :].astype(F32) + (grad - mean - normed * along) * inverse
        t0_ref[at, :] = lane_sum((patch - clean) * grad_resid)
        return carry

    lax.fori_loop(0, ROWS // 16, resid_rows, 0)

    columns = [
        jnp.sum(part, axis=1, keepdims=True) for part in (t0_ref[...], t1_ref[...], t2_ref[...], t3)
    ]
    lane = lane_of(ROWS)
    chosen = jnp.zeros((ROWS, 128), F32)
    for i in range(attr_ref.shape[0]):
        site = site_ref[i]
        column = columns[0]
        for k in range(1, 4):
            column = jnp.where(site == k, columns[k], column)
        chosen = jnp.where(lane == i, column, chosen)
    attr_ref[...] = chosen.T[: attr_ref.shape[0]]


def weight_kernel(own_ref, other_ref, gm_ref, gm_other, go_ref, go_other, out_ref):
    low = jnp.concatenate([own_ref[:, 0:512], other_ref[:, 0:512]], axis=0)
    swished = jnp.concatenate([own_ref[:, 512:1024], other_ref[:, 512:1024]], axis=0)
    def put(at, product):
        half = product.shape[0] // 2
        lower = product[:half].reshape(half // 8, 8, 256)
        upper = product[half:].reshape(half // 8, 8, 256)
        out_ref[:, :, at : at + 256] = jnp.concatenate([lower, upper], axis=1).astype(BF16)

    for j in range(0, 2 * WIDTH, 256):
        grads = jnp.concatenate([gm_ref[:, j : j + 256], gm_other[:, j : j + 256]], axis=0)
        put(j, dot_tn(low, grads))
    for j in range(0, WIDTH, 256):
        grads = jnp.concatenate([go_ref[:, j : j + 256], go_other[:, j : j + 256]], axis=0)
        put(2 * WIDTH + j, dot_tn(swished, grads))


VMEM = pl.BlockSpec(memory_space=pltpu.VMEM)
SMEM = pl.BlockSpec(memory_space=pltpu.SMEM)
HBM = pl.BlockSpec(memory_space=pltpu.HBM)


def kernel_call(body, out_shape, in_specs, scratch, limit, flops, moved):
    return pl.pallas_call(
        body,
        out_shape=out_shape,
        in_specs=in_specs,
        out_specs=[VMEM] * len(out_shape),
        scratch_shapes=scratch,
        compiler_params=pltpu.CompilerParams(vmem_limit_bytes=limit << 20),
        cost_estimate=pl.CostEstimate(flops=flops, bytes_accessed=moved, transcendentals=0),
    )


def shape(dims, dtype):
    return jax.ShapeDtypeStruct(dims, dtype)


def per_device(
    clean_input, corrupt_input, patch_mask, lengths, site_ids, w_query, w_key, w_value,
    w_attn_out, w_pointwise_in, depth_kernel, w_pointwise_out, cotangent,
):
    frames = lax.axis_size("frames")
    position = lax.axis_index("frames")
    core = lax.rem(lax.axis_index("dp"), 2)
    scalars = jnp.stack(
        [position * ROWS, lengths[0], core, lax.rem(position, 2)]
    ).astype(jnp.int32)
    clean, corrupt, cot = clean_input[0], corrupt_input[0], cotangent[0]

    msg, patched, up, down = kernel_call(
        project_kernel,
        [shape((frames, ROWS + 32, 128), BF16), shape((ROWS, WIDTH), BF16),
         shape((2 * RIM, WIDTH), BF16), shape((2 * RIM, WIDTH), BF16)],
        [HBM] * 3 + [VMEM] + [HBM] * 3,
        [pltpu.VMEM((2 * ROWS, WIDTH), BF16), pltpu.VMEM((ROWS, ROWS), F32),
         pltpu.VMEM((ROWS, WIDTH), BF16), pltpu.VMEM((ROWS, WIDTH), BF16),
         pltpu.VMEM((WIDTH, 512), BF16), pltpu.VMEM((WIDTH, 512), BF16),
         pltpu.VMEM((WIDTH, 512), BF16), pltpu.SemaphoreType.DMA((7,))],
        62, 8 * 10**8, 6 * 10**6,
    )(clean, corrupt, cot, patch_mask, w_query, w_key, w_value)
    forward = [(i, i + 1) for i in range(frames - 1)]
    backward = [(i + 1, i) for i in range(frames - 1)]
    from_left = lax.ppermute(up, "frames", forward)
    from_right = lax.ppermute(down, "frames", backward)
    recv = lax.all_to_all(msg, "frames", 0, 0, tiled=True)
    recv, from_left, from_right = lax.optimization_barrier((recv, from_left, from_right))
    count = frames * ROWS
    (context,) = kernel_call(
        attend_kernel,
        [shape((frames, 48, 128), BF16)],
        [SMEM, VMEM],
        [pltpu.VMEM((128, count), BF16), pltpu.VMEM((count, 128), BF16),
         pltpu.VMEM((256, count), F32), pltpu.VMEM((256, count), F32),
         pltpu.VMEM((256, 128), F32), pltpu.VMEM((256, 128), F32),
         pltpu.VMEM((frames * 32, 128), F32)],
        20, 8 * 10**9, 10**6,
    )(scalars, recv)
    contexts = lax.all_to_all(context, "frames", 0, 0, tiled=True)
    own, send, grad_mixed, grad_output, swished, grad_swished, grad_gated, gated, resid = kernel_call(
        clean_kernel,
        [shape((ROWS, 1024), BF16), shape((ROWS, 1024), BF16), shape((ROWS, 2 * WIDTH), BF16),
         shape((ROWS, WIDTH), BF16), shape((INNER, WIDTH), BF16), shape((INNER, WIDTH), F32),
         shape((ROWS * 8, 128), F32), shape((CLEAN * 8, 128), F32), shape((CLEAN, WIDTH), BF16)],
        [SMEM] + [VMEM] * 9,
        [pltpu.VMEM((CLEAN, 512), BF16), pltpu.VMEM((CLEAN, WIDTH), BF16),
         pltpu.VMEM((CLEAN, WIDTH), BF16),
         pltpu.VMEM((ROWS, WIDTH), F32), pltpu.VMEM((ROWS, WIDTH), F32),
         pltpu.VMEM((INNER * 8, 128), F32), pltpu.VMEM((INNER, WIDTH), F32),
         pltpu.VMEM((INNER, 128), F32), pltpu.VMEM((INNER, WIDTH), BF16),
         pltpu.VMEM((INNER * 8, 128), F32), pltpu.VMEM((32 * 8, 128), F32)],
        28, 3 * 10**9, 10**7,
    )(scalars, contexts, clean, cot, from_left, from_right,
      w_attn_out, w_pointwise_in, depth_kernel, w_pointwise_out)

    cores = [(i, i ^ 1) for i in range(lax.axis_size("dp"))]
    other, gm_other, go_other = (
        lax.ppermute(part, "dp", cores) for part in (send, grad_mixed, grad_output)
    )
    (partial,) = kernel_call(
        weight_kernel,
        [shape((frames, 16, 3 * WIDTH), BF16)],
        [VMEM] * 6,
        [],
        32, 8 * 10**8, 10**7,
    )(own, other, grad_mixed, gm_other, grad_output, go_other)
    pieces = lax.all_to_all(partial, "frames", 0, 0, tiled=True)
    (attribution,) = kernel_call(
        patch_kernel,
        [shape((site_ids.shape[0], ROWS), F32)],
        [SMEM, SMEM] + [VMEM] * 15,
        [pltpu.VMEM((PATCH, 512), BF16), pltpu.VMEM((PATCH, WIDTH), BF16),
         pltpu.VMEM((PATCH, WIDTH), BF16), pltpu.VMEM((PATCH, WIDTH), BF16),
         pltpu.VMEM((PATCH * 8, 128), F32), pltpu.VMEM((ROWS * 8, 128), F32),
         pltpu.VMEM((2 * ROWS, WIDTH), BF16), pltpu.VMEM((ROWS, WIDTH), F32),
         pltpu.VMEM((ROWS, 128), F32), pltpu.VMEM((ROWS, 128), F32), pltpu.VMEM((ROWS, 128), F32),
         pltpu.VMEM((32 * 8, 128), F32)],
        28, 3 * 10**9, 10**7,
    )(scalars, site_ids, contexts, patched, from_left, from_right,
      w_attn_out, w_pointwise_in, depth_kernel, w_pointwise_out,
      grad_mixed, grad_output, swished, grad_swished, grad_gated, gated, resid)
    pieces, attribution = lax.optimization_barrier((pieces, attribution))
    summed = jnp.sum(pieces.astype(F32), axis=0)
    upper = lax.axis_index("dp") // 2
    mine = jnp.where(upper == 0, summed[:8], summed[8:])
    theirs = jnp.where(upper == 0, summed[8:], summed[:8])
    half_dp = lax.axis_size("dp") // 2
    theirs = lax.ppermute(theirs, "dp", [(i, i ^ half_dp) for i in range(2 * half_dp)])
    return (
        attribution[None],
        mine[:, : 2 * WIDTH] + theirs[:, : 2 * WIDTH],
        mine[:, 2 * WIDTH :] + theirs[:, 2 * WIDTH :],
    )


def solution(mesh):
    placed = (
        P("dp", "frames", None), P("dp", "frames", None), P("dp", "frames"), P("dp"), P(), P(), P(),
        P(), P(), P(), P(), P(), P("dp", "frames", None),
    )
    return jax.shard_map(
        per_device,
        mesh=mesh,
        in_specs=placed,
        out_specs=(P("dp", None, "frames"), P(("dp", "frames"), None), P(("dp", "frames"), None)),
        check_vma=False,
    )
```

```python
import jax
import jax.numpy as jnp
from jax import lax
from jax.experimental import pallas as pl
from jax.experimental.pallas import tpu as pltpu
from jax.sharding import PartitionSpec as P

HEADS = 8
DH = 64
KERNEL = 31
RIM = 32
EPSILON = 1e-05
FLOOR = -1e30
LOG2E = 1.4426950408889634
F32 = jnp.float32
BF16 = jnp.bfloat16
ROWS = 128
WIDTH = 1024
CLEAN = ROWS + 2 * RIM
PATCH = ROWS + RIM
BOTH = CLEAN + PATCH
INNER = ROWS + RIM


def lane_of(rows):
    return lax.broadcasted_iota(jnp.int32, (rows, 128), 1)


def swap(tile):
    return pltpu.roll(tile, 64, 1)


def moments(values):
    mean = jnp.mean(values, axis=-1, keepdims=True)
    centred = values - mean
    variance = jnp.mean(centred * centred, axis=-1, keepdims=True)
    return centred, lax.rsqrt(variance + EPSILON)


def dot(left, right):
    return jnp.dot(left, right, preferred_element_type=F32)


def dot_nt(left, right):
    return lax.dot_general(left, right, (((1,), (1,)), ((), ())), preferred_element_type=F32)


def dot_tn(left, right):
    return lax.dot_general(left, right, (((0,), (0,)), ((), ())), preferred_element_type=F32)


def sigmoid(values):
    return 1.0 / (1.0 + jnp.exp(-values))


def lane_sum(values):
    total = values[:, :128]
    for start in range(128, values.shape[1], 128):
        total = total + values[:, start : start + 128]
    return total


def project_kernel(
    clean_hbm, corrupt_hbm, cot_hbm, mask_ref, wq_hbm, wk_hbm, wv_hbm,
    msg_ref, patched_ref, up_ref, down_ref,
    hidden_ref, mask_col, clean_ref, corrupt_ref, wq_ref, wk_ref, wv_ref, sems,
):
    half = RIM // 2
    copies = [
        pltpu.make_async_copy(source, target, sems.at[i])
        for i, (source, target) in enumerate((
            (clean_hbm, clean_ref),
            (corrupt_hbm, corrupt_ref),
            (wk_hbm, wk_ref),
            (wv_hbm, wv_ref),
            (wq_hbm, wq_ref),
            (cot_hbm.at[pl.ds(ROWS - half, half)], up_ref.at[pl.ds(RIM + half, half)]),
            (cot_hbm.at[pl.ds(0, half)], down_ref.at[pl.ds(RIM + half, half)]),
        ))
    ]
    for copy in copies:
        copy.start()
    spread_mask = jnp.broadcast_to(mask_ref[...].astype(F32), (ROWS, ROWS))
    mask_col[...] = spread_mask.T
    copies[0].wait()
    copies[1].wait()

    def rows(i, carry):
        at = pl.ds(pl.multiple_of(i * 16, 16), 16)
        below = pl.ds(pl.multiple_of(ROWS + i * 16, 16), 16)
        clean = clean_ref[at, :].astype(F32)
        corrupt = corrupt_ref[at, :].astype(F32)
        patched = jnp.where(mask_col[at, 0:1] == 1.0, corrupt, clean)
        patched_ref[at, :] = patched.astype(BF16)
        for dest, source in ((at, clean), (below, patched)):
            centred, inverse = moments(source)
            hidden_ref[dest, :] = (centred * inverse).astype(BF16)
        return carry

    lax.fori_loop(0, ROWS // 16, rows, 0)
    up_ref[0:RIM, :] = clean_ref[ROWS - RIM : ROWS, :]
    up_ref[RIM : RIM + half, :] = patched_ref[ROWS - half : ROWS, :]
    down_ref[0:RIM, :] = clean_ref[0:RIM, :]
    down_ref[RIM : RIM + half, :] = patched_ref[0:half, :]
    for copy in copies[2:]:
        copy.wait()

    low = lane_of(ROWS) < 64
    low_q = lane_of(64) < 64
    for pair in range(2):
        cols = slice(pair * 256, pair * 256 + 256)
        hidden = hidden_ref[...]
        query = dot(hidden, wq_ref[:, cols])
        keys = dot(hidden, wk_ref[:, cols])
        values = dot(hidden, wv_ref[:, cols])
        for sub in range(2):
            tile = slice(sub * 128, sub * 128 + 128)
            for run in range(2):
                part = slice(run * ROWS, run * ROWS + ROWS)
                k, v, q = keys[part, tile], values[part, tile], query[part, tile]
                base = run * 16 + (pair * 2 + sub) * 4
                kv = (jnp.where(low, k, swap(v)).astype(BF16), jnp.where(low, swap(k), v).astype(BF16))
                early, late = q[:64], q[64:]
                asked = (
                    jnp.where(low_q, early, swap(late)).astype(BF16),
                    jnp.where(low_q, swap(early), late).astype(BF16),
                )
                for odd in range(2):
                    for side in range(2):
                        dest = base + odd * 2 + side
                        msg_ref[dest, 0:64, :] = kv[odd][side * 64 : side * 64 + 64]
                        msg_ref[dest, 64:128, :] = asked[odd]


def attend_kernel(
    scal_ref, recv_ref, out_ref, k_ref, vt_ref, qt_ref, s0_ref, s1_ref, c_ref, r_ref
):
    length, side = scal_ref[1], scal_ref[3]
    sources = recv_ref.shape[0]
    lane = lane_of(128)
    row = lax.broadcasted_iota(jnp.int32, (128, 128), 0)
    scale = DH ** (-0.5) * LOG2E

    def load(s, carry):
        at = pl.multiple_of(s * 128, 128)
        kv = recv_ref[pl.ds(2 * s, 2), 0:64, :].astype(F32).reshape(128, 128)
        frame = (2 * s + row // 64) * ROWS + side * 64 + row % 64
        bias = jnp.where(frame < length, 0.0, FLOOR)
        keyed = jnp.where(lane < 64, kv, jnp.where(lane == 64, bias, 0.0))
        k_ref[pl.ds(at, 128), :] = keyed.astype(BF16)
        vt_ref[:, pl.ds(at, 128)] = jnp.where(lane < 64, 1.0, kv).T.astype(BF16)
        raw = recv_ref[pl.ds(2 * s, 2), 64:128, :].astype(F32).reshape(128, 128).T
        fill = jnp.where(row == 64, 1.0, 0.0)
        other = jnp.concatenate([raw[64:], raw[:64]], axis=0)
        at = pl.multiple_of(s * 256, 256)
        qt_ref[:, pl.ds(at, 128)] = jnp.where(row < 64, raw, fill).astype(BF16)
        qt_ref[:, pl.ds(at + 128, 128)] = jnp.where(row < 64, other, fill).astype(BF16)
        return carry

    lax.fori_loop(0, sources // 2, load, 0, unroll=4)

    many = s0_ref.shape[1]
    chunk = 256
    pieces = k_ref.shape[0] // chunk
    blocks = sources * ROWS // many

    def score_piece(query, s_ref, k, top):
        at = slice(k * chunk, k * chunk + chunk)
        scores = dot(k_ref[at, :], query)
        s_ref[at, :] = scores
        best = jnp.max(scores.reshape(chunk // 8, 8, many), axis=0)
        return best if top is None else jnp.maximum(top, best)

    def weigh_piece(s_ref, best, k, accum):
        at = slice(k * chunk, k * chunk + chunk)
        weights = jnp.exp2((s_ref[at, :] - best) * scale).astype(BF16)
        addend = dot(vt_ref[:, at], weights)
        return addend if accum is None else accum + addend

    def finish(top):
        return jnp.max(top, axis=0, keepdims=True)

    def queries(b):
        return qt_ref[:, pl.ds(pl.multiple_of(b * many, many), many)]

    low8 = lane_of(8) < 64

    def store(b, accum, best):
        total = accum[0:1, :]
        result = accum[64:128, :] / total
        level = jnp.broadcast_to(best * scale + jnp.log2(total), (8, many))
        for g in range(many // 256):
            first = slice(g * 256, g * 256 + 128)
            second = slice(g * 256 + 128, g * 256 + 256)
            both = jnp.concatenate([result[:, first], result[:, second]], axis=0)
            at = b * (many // 256) + g
            c_ref[pl.ds(pl.multiple_of(at * 128, 128), 128), :] = both.T
            early, late = level[:, first], level[:, second]
            r_ref[pl.ds(pl.multiple_of(at * 16, 16), 8), :] = jnp.where(low8, early, swap(late))
            r_ref[pl.ds(pl.multiple_of(at * 16 + 8, 8), 8), :] = jnp.where(low8, swap(early), late)

    def step(b, s_ref, best, next_b, next_s):
        query = None if next_s is None else queries(next_b)
        top, accum = None, None
        for k in range(pieces):
            if query is not None:
                top = score_piece(query, next_s, k, top)
            accum = weigh_piece(s_ref, best, k, accum)
        store(b, accum, best)
        return None if query is None else finish(top)

    query, top = queries(0), None
    for k in range(pieces):
        top = score_piece(query, s0_ref, k, top)

    def pair(i, best):
        best = step(2 * i, s0_ref, best, 2 * i + 1, s1_ref)
        return step(2 * i + 1, s1_ref, best, 2 * i + 2, s0_ref)

    best = lax.fori_loop(0, blocks // 2 - 1, pair, finish(top))
    best = step(blocks - 2, s0_ref, best, blocks - 1, s1_ref)
    step(blocks - 1, s1_ref, best, None, None)

    low32 = lane_of(32) < 64
    row8 = lax.broadcasted_iota(jnp.int32, (8, 128), 0)

    def pack(d, carry):
        after = lax.rem(d + 1, sources)
        before = lax.rem(d + sources - 1, sources)
        out_ref[d, 0:64, :] = c_ref[pl.ds(pl.multiple_of(d * 64, 64), 64), :].astype(BF16)
        right = c_ref[pl.ds(pl.multiple_of(after * 64, 64), 32), :]
        left = c_ref[pl.ds(pl.multiple_of(before * 64 + 32, 32), 32), :]
        out_ref[d, 64:96, :] = jnp.where(low32, right, left).astype(BF16)
        own = r_ref[pl.ds(pl.multiple_of(d * 8, 8), 8), :]
        rim = jnp.where(
            low8,
            r_ref[pl.ds(pl.multiple_of(after * 8, 8), 8), :],
            r_ref[pl.ds(pl.multiple_of(before * 8, 8), 8), :],
        )
        rows = jnp.where(row8 < 3, own, rim)
        high = rows.astype(BF16).astype(F32)
        rest = rows - high
        middle = rest.astype(BF16).astype(F32)
        last = rest - middle
        level = row8 % 3
        rows = jnp.where(level == 0, high, jnp.where(level == 1, middle, last))
        out_ref[d, 96:112, :] = jnp.concatenate([rows, rows], axis=0).astype(BF16)
        return carry

    lax.fori_loop(0, sources, pack, 0, unroll=2)


def depthwise(source, source_row, taps_ref, order, target, count):
    def rows(i, carry):
        first = source_row + i * 8
        taps = [taps_ref[t * 8 : t * 8 + 8, :] for t in order]
        sums = [None] * 8
        for s in range(KERNEL + 7):
            piece = source[pl.ds(pl.multiple_of((first + s) * 8, 8), 8), :]
            for o in range(8):
                if 0 <= s - o < KERNEL:
                    term = taps[s - o] * piece
                    sums[o] = term if sums[o] is None else sums[o] + term
        for o in range(8):
            target[pl.ds(pl.multiple_of((i * 8 + o) * 8, 8), 8), :] = sums[o]
        return carry

    lax.fori_loop(0, count // 8, rows, 0)


def put_rows(ref, row, tile, values):
    for r in range(0, values.shape[0], 8):
        ref[pl.ds((row + r) * 8 + tile, 8, stride=8), :] = values[r : r + 8]


def get_rows(ref, row, count):
    groups = []
    for r in range(0, count, 8):
        tiles = [ref[pl.ds((row + r) * 8 + t, 8, stride=8), :] for t in range(8)]
        groups.append(jnp.concatenate(tiles, axis=1))
    return jnp.concatenate(groups, axis=0) if len(groups) > 1 else groups[0]


def place_context(ctx_in, base, ctx_ref, rim):
    row8 = lax.broadcasted_iota(jnp.int32, (8, 128), 0)
    zero = jnp.zeros((8, 128), F32)
    levels = [[zero, zero], [zero, zero]]
    for h in range(HEADS):
        for side in range(2):
            block = ctx_in[base + h * 2 + side, 96:112, :].astype(F32)
            for kind in range(2):
                at = kind * 3
                level = block[at : at + 1] + block[at + 1 : at + 2] + block[at + 2 : at + 3]
                levels[kind][side] = jnp.where(row8 == h, level, levels[kind][side])
    shares = []
    for first, second in levels:
        shares.append(1.0 / (1.0 + jnp.exp2(second - first)))
        shares.append(1.0 / (1.0 + jnp.exp2(first - second)))
    share = jnp.concatenate(shares + [jnp.zeros((96, 128), F32)], axis=0).T
    low = lane_of(96) < 64
    low_rows = lane_of(ROWS) < 64
    for t in range(HEADS // 2):
        at = slice(t * 128, t * 128 + 128)
        own = left = right = None
        for side in range(2):
            even = ctx_in[base + t * 4 + side, 0:96, :].astype(F32)
            odd = ctx_in[base + t * 4 + 2 + side, 0:96, :].astype(F32)
            first = jnp.where(low, even, swap(odd))
            second = jnp.where(low, swap(even), odd)
            scale = []
            for kind in range(2):
                column = kind * 16 + side * 8 + 2 * t
                scale.append(jnp.where(
                    low_rows, share[:, column : column + 1], share[:, column + 1 : column + 2]
                ))
            part = jnp.concatenate([first[:64], second[:64]], axis=0) * scale[0]
            after = first[64:96] * scale[1][0:32]
            before = second[64:96] * scale[1][96:128]
            own = part if own is None else own + part
            left = before if left is None else left + before
            right = after if right is None else right + after
        ctx_ref[0:rim, at] = left[RIM - rim :].astype(BF16)
        ctx_ref[rim : rim + ROWS, at] = own.astype(BF16)
        ctx_ref[rim + ROWS :, at] = right[:rim].astype(BF16)


def place_taps(depth_ref, taps_ref):
    for r in range(0, KERNEL + 1, 8):
        got = min(8, KERNEL - r)
        block = depth_ref[r : r + got, :].astype(F32)
        if got < 8:
            block = jnp.concatenate([block, jnp.zeros((8 - got, WIDTH), F32)], axis=0)
        for t in range(8):
            put_rows(taps_ref, r, t, block[:, t * 128 : t * 128 + 128])


def to_lowered(x_ref, ctx_ref, wao_ref, resid_ref, low_ref):
    for j in range(4):
        at = slice(j * 256, j * 256 + 256)
        joined = x_ref[:, at].astype(F32) + dot(ctx_ref[...], wao_ref[:, at])
        resid_ref[:, at] = joined.astype(BF16)

    def lower(i, carry):
        at = pl.ds(pl.multiple_of(i * 16, 16), 16)
        centred, inverse = moments(resid_ref[at, :].astype(F32))
        low_ref[at, :] = (centred * inverse).astype(BF16)
        return carry

    lax.fori_loop(0, x_ref.shape[0] // 16, lower, 0)


def to_gated(low_ref, win_ref, g2_ref, frame, length, keep):
    live = jnp.where((frame >= 0) & (frame < length), 1.0, 0.0)
    for j in range(4):
        at = slice(j * 256, j * 256 + 256)
        gate_at = slice(WIDTH + j * 256, WIDTH + j * 256 + 256)
        value = dot(low_ref[...], win_ref[:, at])
        gate = sigmoid(dot(low_ref[...], win_ref[:, gate_at]))
        if keep is not None:
            mv_ref, sg_ref = keep
            mv_ref[:, at] = value[RIM : RIM + ROWS]
            sg_ref[:, at] = gate[RIM : RIM + ROWS]
        gated = (value * gate * live).astype(BF16).astype(F32)
        for t in range(2):
            put_rows(g2_ref, 0, j * 2 + t, gated[:, t * 128 : t * 128 + 128])


def clean_kernel(
    scal_ref, ctx_hbm, clean_hbm, cot_hbm, up_hbm, down_hbm,
    wao_hbm, win_hbm, depth_hbm, wout_hbm,
    own_out, send_out, gm_out, go_out, sw_out, gs_out, gg2_out, g2_out, resid_out,
    ctx_in, wao_ref, win_ref, depth_ref, wout_ref,
    own_ref, send_ref, gm_ref, go_ref, sw_ref, gs_ref, gg2_ref, g2_ref, resid_ref,
    ctx_ref, x_ref, low_ref, mv_ref, sg_ref, s2_ref, zed_ref, zinv_ref, gox_ref, gsp2_ref, taps_ref,
    in_sems, out_sems,
):
    first_frame, length, core = scal_ref[0], scal_ref[1], scal_ref[2]
    half = RIM // 2
    copies = [
        pltpu.make_async_copy(source, target, in_sems.at[i])
        for i, (source, target) in enumerate((
            (ctx_hbm.at[pl.ds(0, 16)], ctx_in),
            (up_hbm.at[pl.ds(0, RIM)], x_ref.at[pl.ds(0, RIM)]),
            (clean_hbm, x_ref.at[pl.ds(RIM, ROWS)]),
            (down_hbm.at[pl.ds(0, RIM)], x_ref.at[pl.ds(RIM + ROWS, RIM)]),
            (wao_hbm, wao_ref),
            (depth_hbm, depth_ref),
            (up_hbm.at[pl.ds(RIM + half, half)], gox_ref.at[pl.ds(0, half)]),
            (cot_hbm, gox_ref.at[pl.ds(half, ROWS)]),
            (down_hbm.at[pl.ds(RIM + half, half)], gox_ref.at[pl.ds(half + ROWS, half)]),
            (win_hbm, win_ref),
            (wout_hbm, wout_ref),
        ))
    ]
    for copy in copies:
        copy.start()
    results = [
        pltpu.make_async_copy(source, target, out_sems.at[i])
        for i, (source, target) in enumerate((
            (own_ref, own_out), (send_ref, send_out), (gm_ref, gm_out), (go_ref, go_out),
            (sw_ref, sw_out), (gs_ref, gs_out), (gg2_ref, gg2_out), (g2_ref, g2_out),
            (resid_ref, resid_out),
        ))
    ]
    own_copy, send_copy, gm_copy, go_copy, sw_copy, gs_copy, gg2_copy, g2_copy, resid_copy = results
    copies[0].wait()
    place_context(ctx_in, 0, ctx_ref, RIM)
    for copy in copies[1:9]:
        copy.wait()
    place_taps(depth_ref, taps_ref)
    for row in range(0, INNER, 16):
        at = slice(row, row + 16)
        frame = first_frame - half + row + lax.broadcasted_iota(jnp.int32, (16, 1), 0)
        gox_ref[at, :] = (gox_ref[at, :].astype(F32) * jnp.where(frame < length, 1.0, 0.0)).astype(BF16)
    go_ref[...] = gox_ref[half : half + ROWS, :]
    go_copy.start()

    to_lowered(x_ref, ctx_ref, wao_ref, resid_ref, low_ref)
    resid_copy.start()
    frame = first_frame - RIM + lax.broadcasted_iota(jnp.int32, (CLEAN, 1), 0)
    copies[9].wait()
    to_gated(low_ref, win_ref, g2_ref, frame, length, (mv_ref, sg_ref))
    g2_copy.start()
    forward = list(range(KERNEL))
    edge = half - KERNEL // 2
    depthwise(g2_ref, edge, taps_ref, forward, s2_ref, INNER)

    def clean_rows(i, carry):
        r = pl.multiple_of(i * 16, 16)
        centred, inverse = moments(get_rows(s2_ref, r, 16))
        zed = centred * inverse
        zed_ref[pl.ds(r, 16), :] = zed
        zinv_ref[pl.ds(r, 16), :] = jnp.broadcast_to(inverse, (16, 128))
        sw_ref[pl.ds(r, 16), :] = (zed * sigmoid(zed)).astype(BF16)
        return carry

    lax.fori_loop(0, INNER // 16, clean_rows, 0)
    sw_copy.start()

    for part in range(4):
        dest = part * 256
        source, row = (low_ref, RIM) if part < 2 else (sw_ref, half)
        lo = (part % 2) * 512
        first = source[row : row + ROWS, lo : lo + 256].astype(F32)
        second = source[row : row + ROWS, lo + 256 : lo + 512].astype(F32)
        own_ref[:, dest : dest + 256] = jnp.where(core == 0, first, second).astype(BF16)
        send_ref[:, dest : dest + 256] = jnp.where(core == 0, second, first).astype(BF16)
    own_copy.start()
    send_copy.start()

    copies[10].wait()
    for j in range(4):
        at = slice(j * 256, j * 256 + 256)
        gs_ref[:, at] = dot_nt(gox_ref[...], wout_ref[at, :])
    gs_copy.start()

    def back_rows(i, carry):
        r = pl.multiple_of(i * 16, 16)
        zed = zed_ref[pl.ds(r, 16), :]
        grad = gs_ref[pl.ds(r, 16), :]
        gate = sigmoid(zed)
        grad_zed = grad * (gate * (1.0 + zed * (1.0 - gate)))
        mean = jnp.mean(grad_zed, axis=-1, keepdims=True)
        along = jnp.mean(grad_zed * zed, axis=-1, keepdims=True)
        result = (grad_zed - mean - zed * along) * zinv_ref[pl.ds(r, 16), 0:1]
        for g in range(0, 16, 8):
            for t in range(8):
                gsp2_ref[pl.ds((r + g) * 8 + t, 8, stride=8), :] = result[
                    g : g + 8, t * 128 : t * 128 + 128
                ]
        return carry

    lax.fori_loop(0, INNER // 16, back_rows, 0)
    depthwise(gsp2_ref, edge, taps_ref, forward[::-1], gg2_ref, ROWS)
    gg2_copy.start()

    def mixed_rows(i, carry):
        r = pl.multiple_of(i * 16, 16)
        at = pl.ds(r, 16)
        frame = first_frame + r + lax.broadcasted_iota(jnp.int32, (16, 1), 0)
        grad = get_rows(gg2_ref, r, 16) * jnp.where(frame < length, 1.0, 0.0)
        gate = sg_ref[at, :]
        gm_ref[at, 0:WIDTH] = (grad * gate).astype(BF16)
        gm_ref[at, WIDTH:] = (grad * mv_ref[at, :] * gate * (1.0 - gate)).astype(BF16)
        return carry

    lax.fori_loop(0, ROWS // 16, mixed_rows, 0)

    gm_copy.start()
    for copy in results:
        copy.wait()


def patch_kernel(
    scal_ref, site_ref, ctx_in, patched_ref, up_ref, down_ref,
    wao_ref, win_ref, depth_ref, wout_ref,
    gm_ref, go_ref, swc_ref, gs_ref, gg2_ref, g2c_ref, residc_ref,
    attr_ref,
    ctx_ref, x_ref, resid_ref, low_ref, g2_ref, s2_ref, sw_ref, gl_ref, t0_ref, t1_ref, t2_ref, taps_ref,
):
    first_frame, length = scal_ref[0], scal_ref[1]
    half = RIM // 2
    place_context(ctx_in, 16, ctx_ref, half)
    x_ref[0:half, :] = up_ref[RIM : RIM + half, :]
    x_ref[half : half + ROWS, :] = patched_ref[...]
    x_ref[half + ROWS : PATCH, :] = down_ref[RIM : RIM + half, :]
    place_taps(depth_ref, taps_ref)
    to_lowered(x_ref, ctx_ref, wao_ref, resid_ref, low_ref)
    frame = first_frame - half + lax.broadcasted_iota(jnp.int32, (PATCH, 1), 0)
    to_gated(low_ref, win_ref, g2_ref, frame, length, None)
    depthwise(g2_ref, half - KERNEL // 2, taps_ref, list(range(KERNEL)), s2_ref, ROWS)
    sw_ref[0:ROWS, :] = swc_ref[half : half + ROWS, :]

    def patch_rows(i, carry):
        r = pl.multiple_of(i * 16, 16)
        at = pl.ds(r, 16)
        inner = pl.ds(pl.multiple_of(half + r, 16), 16)
        centred, inverse = moments(get_rows(s2_ref, r, 16))
        zed = centred * inverse
        swished = (zed * sigmoid(zed)).astype(BF16)
        sw_ref[pl.ds(pl.multiple_of(ROWS + r, 16), 16), :] = swished
        gap = swished.astype(F32) - sw_ref[at, :].astype(F32)
        t2_ref[at, :] = lane_sum(gap * gs_ref[inner, :])
        frame = first_frame + r + lax.broadcasted_iota(jnp.int32, (16, 1), 0)
        grad = get_rows(gg2_ref, r, 16) * jnp.where(frame < length, 1.0, 0.0)
        gap = get_rows(g2_ref, half + r, 16) - get_rows(g2c_ref, RIM + r, 16)
        t1_ref[at, :] = lane_sum(gap * grad)
        return carry

    lax.fori_loop(0, ROWS // 16, patch_rows, 0)

    t3 = jnp.zeros((ROWS, 128), F32)
    for j in range(4):
        at = slice(j * 256, j * 256 + 256)
        out = dot(sw_ref[...], wout_ref[:, at])
        out_clean = residc_ref[RIM : RIM + ROWS, at].astype(F32) + out[:ROWS]
        out_patch = resid_ref[half : half + ROWS, at].astype(F32) + out[ROWS:]
        gap = out_patch.astype(BF16).astype(F32) - out_clean.astype(BF16).astype(F32)
        t3 = t3 + lane_sum(gap * go_ref[:, at].astype(F32))
    for j in range(4):
        at = slice(j * 256, j * 256 + 256)
        gl_ref[:, at] = dot_nt(gm_ref[...], win_ref[at, :])

    def resid_rows(i, carry):
        r = pl.multiple_of(i * 16, 16)
        at = pl.ds(r, 16)
        clean = residc_ref[pl.ds(pl.multiple_of(RIM + r, 16), 16), :].astype(F32)
        patch = resid_ref[pl.ds(pl.multiple_of(half + r, 16), 16), :].astype(F32)
        centred, inverse = moments(clean)
        normed = centred * inverse
        grad = gl_ref[at, :]
        mean = jnp.mean(grad, axis=-1, keepdims=True)
        along = jnp.mean(grad * normed, axis=-1, keepdims=True)
        grad_resid = go_ref[at, :].astype(F32) + (grad - mean - normed * along) * inverse
        t0_ref[at, :] = lane_sum((patch - clean) * grad_resid)
        return carry

    lax.fori_loop(0, ROWS // 16, resid_rows, 0)

    columns = [
        jnp.sum(part, axis=1, keepdims=True) for part in (t0_ref[...], t1_ref[...], t2_ref[...], t3)
    ]
    lane = lane_of(ROWS)
    chosen = jnp.zeros((ROWS, 128), F32)
    for i in range(attr_ref.shape[0]):
        site = site_ref[i]
        column = columns[0]
        for k in range(1, 4):
            column = jnp.where(site == k, columns[k], column)
        chosen = jnp.where(lane == i, column, chosen)
    attr_ref[...] = chosen.T[: attr_ref.shape[0]]


def weight_kernel(own_ref, other_ref, gm_ref, gm_other, go_ref, go_other, out_ref):
    low = jnp.concatenate([own_ref[:, 0:512], other_ref[:, 0:512]], axis=0)
    swished = jnp.concatenate([own_ref[:, 512:1024], other_ref[:, 512:1024]], axis=0)
    def put(at, product):
        half = product.shape[0] // 2
        lower = product[:half].reshape(half // 8, 8, 256)
        upper = product[half:].reshape(half // 8, 8, 256)
        out_ref[:, :, at : at + 256] = jnp.concatenate([lower, upper], axis=1).astype(BF16)

    for j in range(0, 2 * WIDTH, 256):
        grads = jnp.concatenate([gm_ref[:, j : j + 256], gm_other[:, j : j + 256]], axis=0)
        put(j, dot_tn(low, grads))
    for j in range(0, WIDTH, 256):
        grads = jnp.concatenate([go_ref[:, j : j + 256], go_other[:, j : j + 256]], axis=0)
        put(2 * WIDTH + j, dot_tn(swished, grads))


VMEM = pl.BlockSpec(memory_space=pltpu.VMEM)
SMEM = pl.BlockSpec(memory_space=pltpu.SMEM)
HBM = pl.BlockSpec(memory_space=pltpu.HBM)


def kernel_call(body, out_shape, in_specs, scratch, limit, flops, moved, out_spec=VMEM):
    return pl.pallas_call(
        body,
        out_shape=out_shape,
        in_specs=in_specs,
        out_specs=[out_spec] * len(out_shape),
        scratch_shapes=scratch,
        compiler_params=pltpu.CompilerParams(vmem_limit_bytes=limit << 20),
        cost_estimate=pl.CostEstimate(flops=flops, bytes_accessed=moved, transcendentals=0),
    )


def shape(dims, dtype):
    return jax.ShapeDtypeStruct(dims, dtype)


def per_device(
    clean_input, corrupt_input, patch_mask, lengths, site_ids, w_query, w_key, w_value,
    w_attn_out, w_pointwise_in, depth_kernel, w_pointwise_out, cotangent,
):
    frames = lax.axis_size("frames")
    position = lax.axis_index("frames")
    core = lax.rem(lax.axis_index("dp"), 2)
    scalars = jnp.stack(
        [position * ROWS, lengths[0], core, lax.rem(position, 2)]
    ).astype(jnp.int32)
    clean, corrupt, cot = clean_input[0], corrupt_input[0], cotangent[0]

    msg, patched, up, down = kernel_call(
        project_kernel,
        [shape((frames, ROWS, 128), BF16), shape((ROWS, WIDTH), BF16),
         shape((2 * RIM, WIDTH), BF16), shape((2 * RIM, WIDTH), BF16)],
        [HBM] * 3 + [VMEM] + [HBM] * 3,
        [pltpu.VMEM((2 * ROWS, WIDTH), BF16), pltpu.VMEM((ROWS, ROWS), F32),
         pltpu.VMEM((ROWS, WIDTH), BF16), pltpu.VMEM((ROWS, WIDTH), BF16),
         pltpu.VMEM((WIDTH, 512), BF16), pltpu.VMEM((WIDTH, 512), BF16),
         pltpu.VMEM((WIDTH, 512), BF16), pltpu.SemaphoreType.DMA((7,))],
        62, 8 * 10**8, 6 * 10**6,
    )(clean, corrupt, cot, patch_mask, w_query, w_key, w_value)
    forward = [(i, i + 1) for i in range(frames - 1)]
    backward = [(i + 1, i) for i in range(frames - 1)]
    from_left = lax.ppermute(up, "frames", forward)
    from_right = lax.ppermute(down, "frames", backward)
    recv = lax.all_to_all(msg, "frames", 0, 0, tiled=True)
    recv, from_left, from_right = lax.optimization_barrier((recv, from_left, from_right))
    keys = frames * ROWS // 2
    (context,) = kernel_call(
        attend_kernel,
        [shape((frames, 112, 128), BF16)],
        [SMEM, VMEM],
        [pltpu.VMEM((keys, 128), BF16), pltpu.VMEM((128, keys), BF16),
         pltpu.VMEM((128, 2 * keys), BF16),
         pltpu.VMEM((keys, 512), F32), pltpu.VMEM((keys, 512), F32),
         pltpu.VMEM((frames * 64, 128), F32), pltpu.VMEM((frames * 8, 128), F32)],
        20, 8 * 10**9, 10**6,
    )(scalars, recv)
    contexts = lax.all_to_all(context, "frames", 0, 0, tiled=True)
    own, send, grad_mixed, grad_output, swished, grad_swished, grad_gated, gated, resid = kernel_call(
        clean_kernel,
        [shape((ROWS, 1024), BF16), shape((ROWS, 1024), BF16), shape((ROWS, 2 * WIDTH), BF16),
         shape((ROWS, WIDTH), BF16), shape((INNER, WIDTH), BF16), shape((INNER, WIDTH), F32),
         shape((ROWS * 8, 128), F32), shape((CLEAN * 8, 128), F32), shape((CLEAN, WIDTH), BF16)],
        [SMEM] + [HBM] * 9,
        [pltpu.VMEM((16, 112, 128), BF16), pltpu.VMEM((512, WIDTH), BF16),
         pltpu.VMEM((WIDTH, 2 * WIDTH), BF16), pltpu.VMEM((KERNEL, WIDTH), BF16),
         pltpu.VMEM((WIDTH, WIDTH), BF16),
         pltpu.VMEM((ROWS, 1024), BF16), pltpu.VMEM((ROWS, 1024), BF16),
         pltpu.VMEM((ROWS, 2 * WIDTH), BF16), pltpu.VMEM((ROWS, WIDTH), BF16),
         pltpu.VMEM((INNER, WIDTH), BF16), pltpu.VMEM((INNER, WIDTH), F32),
         pltpu.VMEM((ROWS * 8, 128), F32), pltpu.VMEM((CLEAN * 8, 128), F32),
         pltpu.VMEM((CLEAN, WIDTH), BF16),
         pltpu.VMEM((CLEAN, 512), BF16), pltpu.VMEM((CLEAN, WIDTH), BF16),
         pltpu.VMEM((CLEAN, WIDTH), BF16),
         pltpu.VMEM((ROWS, WIDTH), F32), pltpu.VMEM((ROWS, WIDTH), F32),
         pltpu.VMEM((INNER * 8, 128), F32), pltpu.VMEM((INNER, WIDTH), F32),
         pltpu.VMEM((INNER, 128), F32), pltpu.VMEM((INNER, WIDTH), BF16),
         pltpu.VMEM((INNER * 8, 128), F32), pltpu.VMEM((32 * 8, 128), F32),
         pltpu.SemaphoreType.DMA((11,)), pltpu.SemaphoreType.DMA((9,))],
        62, 3 * 10**9, 10**7, HBM,
    )(scalars, contexts, clean, cot, from_left, from_right,
      w_attn_out, w_pointwise_in, depth_kernel, w_pointwise_out)

    cores = [(i, i ^ 1) for i in range(lax.axis_size("dp"))]
    other, gm_other, go_other = (
        lax.ppermute(part, "dp", cores) for part in (send, grad_mixed, grad_output)
    )
    (partial,) = kernel_call(
        weight_kernel,
        [shape((frames, 16, 3 * WIDTH), BF16)],
        [VMEM] * 6,
        [],
        32, 8 * 10**8, 10**7,
    )(own, other, grad_mixed, gm_other, grad_output, go_other)
    pieces = lax.all_to_all(partial, "frames", 0, 0, tiled=True)
    (attribution,) = kernel_call(
        patch_kernel,
        [shape((site_ids.shape[0], ROWS), F32)],
        [SMEM, SMEM] + [VMEM] * 15,
        [pltpu.VMEM((PATCH, 512), BF16), pltpu.VMEM((PATCH, WIDTH), BF16),
         pltpu.VMEM((PATCH, WIDTH), BF16), pltpu.VMEM((PATCH, WIDTH), BF16),
         pltpu.VMEM((PATCH * 8, 128), F32), pltpu.VMEM((ROWS * 8, 128), F32),
         pltpu.VMEM((2 * ROWS, WIDTH), BF16), pltpu.VMEM((ROWS, WIDTH), F32),
         pltpu.VMEM((ROWS, 128), F32), pltpu.VMEM((ROWS, 128), F32), pltpu.VMEM((ROWS, 128), F32),
         pltpu.VMEM((32 * 8, 128), F32)],
        28, 3 * 10**9, 10**7,
    )(scalars, site_ids, contexts, patched, from_left, from_right,
      w_attn_out, w_pointwise_in, depth_kernel, w_pointwise_out,
      grad_mixed, grad_output, swished, grad_swished, grad_gated, gated, resid)
    pieces, attribution = lax.optimization_barrier((pieces, attribution))
    summed = jnp.sum(pieces.astype(F32), axis=0)
    upper = lax.axis_index("dp") // 2
    mine = jnp.where(upper == 0, summed[:8], summed[8:])
    theirs = jnp.where(upper == 0, summed[8:], summed[:8])
    half_dp = lax.axis_size("dp") // 2
    theirs = lax.ppermute(
        theirs.astype(BF16), "dp", [(i, i ^ half_dp) for i in range(2 * half_dp)]
    ).astype(F32)
    return (
        attribution[None],
        mine[:, : 2 * WIDTH] + theirs[:, : 2 * WIDTH],
        mine[:, 2 * WIDTH :] + theirs[:, 2 * WIDTH :],
    )


def solution(mesh):
    placed = (
        P("dp", "frames", None), P("dp", "frames", None), P("dp", "frames"), P("dp"), P(), P(), P(),
        P(), P(), P(), P(), P(), P("dp", "frames", None),
    )
    return jax.shard_map(
        per_device,
        mesh=mesh,
        in_specs=placed,
        out_specs=(P("dp", None, "frames"), P(("dp", "frames"), None), P(("dp", "frames"), None)),
        check_vma=False,
    )
```

```python
import jax
import jax.numpy as jnp
from jax import lax
from jax.experimental import pallas as pl
from jax.experimental.pallas import tpu as pltpu
from jax.sharding import PartitionSpec as P

HEADS = 8
DH = 64
KERNEL = 31
RIM = 32
EPSILON = 1e-05
FLOOR = -1e30
LOG2E = 1.4426950408889634
F32 = jnp.float32
BF16 = jnp.bfloat16
ROWS = 128
WIDTH = 1024
CLEAN = ROWS + 2 * RIM
PATCH = ROWS + RIM
BOTH = CLEAN + PATCH
INNER = ROWS + RIM
UNROLL = 5
TAP_UNROLL = 2


def lane_of(rows):
    return lax.broadcasted_iota(jnp.int32, (rows, 128), 1)


def swap(tile):
    return pltpu.roll(tile, 64, 1)


def moments(values):
    mean = jnp.mean(values, axis=-1, keepdims=True)
    centred = values - mean
    variance = jnp.mean(centred * centred, axis=-1, keepdims=True)
    return centred, lax.rsqrt(variance + EPSILON)


def dot(left, right):
    return jnp.dot(left, right, preferred_element_type=F32)


def dot_nt(left, right):
    return lax.dot_general(left, right, (((1,), (1,)), ((), ())), preferred_element_type=F32)


def dot_tn(left, right):
    return lax.dot_general(left, right, (((0,), (0,)), ((), ())), preferred_element_type=F32)


def sigmoid(values):
    return 1.0 / (1.0 + jnp.exp(-values))


def lane_sum(values):
    total = values[:, :128]
    for start in range(128, values.shape[1], 128):
        total = total + values[:, start : start + 128]
    return total


def project_kernel(
    clean_hbm, corrupt_hbm, cot_hbm, mask_ref, wq_hbm, wk_hbm, wv_hbm,
    msg_ref, patched_ref, up_ref, down_ref,
    hidden_ref, mask_col, clean_ref, corrupt_ref, wq_ref, wk_ref, wv_ref, sems,
):
    half = RIM // 2
    copies = [
        pltpu.make_async_copy(source, target, sems.at[i])
        for i, (source, target) in enumerate((
            (clean_hbm, clean_ref),
            (corrupt_hbm, corrupt_ref),
            (wk_hbm, wk_ref),
            (wv_hbm, wv_ref),
            (wq_hbm, wq_ref),
            (cot_hbm.at[pl.ds(ROWS - half, half)], up_ref.at[pl.ds(RIM + half, half)]),
            (cot_hbm.at[pl.ds(0, half)], down_ref.at[pl.ds(RIM + half, half)]),
        ))
    ]
    for copy in copies:
        copy.start()
    spread_mask = jnp.broadcast_to(mask_ref[...].astype(F32), (ROWS, ROWS))
    mask_col[...] = spread_mask.T
    copies[0].wait()
    copies[1].wait()

    def rows(i, carry):
        at = pl.ds(pl.multiple_of(i * 16, 16), 16)
        below = pl.ds(pl.multiple_of(ROWS + i * 16, 16), 16)
        clean = clean_ref[at, :].astype(F32)
        corrupt = corrupt_ref[at, :].astype(F32)
        patched = jnp.where(mask_col[at, 0:1] == 1.0, corrupt, clean)
        patched_ref[at, :] = patched.astype(BF16)
        for dest, source in ((at, clean), (below, patched)):
            centred, inverse = moments(source)
            hidden_ref[dest, :] = (centred * inverse).astype(BF16)
        return carry

    lax.fori_loop(0, ROWS // 16, rows, 0, unroll=UNROLL)
    up_ref[0:RIM, :] = clean_ref[ROWS - RIM : ROWS, :]
    up_ref[RIM : RIM + half, :] = patched_ref[ROWS - half : ROWS, :]
    down_ref[0:RIM, :] = clean_ref[0:RIM, :]
    down_ref[RIM : RIM + half, :] = patched_ref[0:half, :]
    for copy in copies[2:]:
        copy.wait()

    low = lane_of(ROWS) < 64
    low_q = lane_of(64) < 64
    for pair in range(2):
        cols = slice(pair * 256, pair * 256 + 256)
        hidden = hidden_ref[...]
        query = dot(hidden, wq_ref[:, cols])
        keys = dot(hidden, wk_ref[:, cols])
        values = dot(hidden, wv_ref[:, cols])
        for sub in range(2):
            tile = slice(sub * 128, sub * 128 + 128)
            for run in range(2):
                part = slice(run * ROWS, run * ROWS + ROWS)
                k, v, q = keys[part, tile], values[part, tile], query[part, tile]
                base = run * 16 + (pair * 2 + sub) * 4
                kv = (jnp.where(low, k, swap(v)).astype(BF16), jnp.where(low, swap(k), v).astype(BF16))
                early, late = q[:64], q[64:]
                asked = (
                    jnp.where(low_q, early, swap(late)).astype(BF16),
                    jnp.where(low_q, swap(early), late).astype(BF16),
                )
                for odd in range(2):
                    for side in range(2):
                        dest = base + odd * 2 + side
                        msg_ref[dest, 0:64, :] = kv[odd][side * 64 : side * 64 + 64]
                        msg_ref[dest, 64:128, :] = asked[odd]


def attend_kernel(
    scal_ref, recv_ref, out_ref, k_ref, vt_ref, qt_ref, s0_ref, s1_ref, c_ref, r_ref
):
    length, side = scal_ref[1], scal_ref[3]
    sources = recv_ref.shape[0]
    lane = lane_of(128)
    row = lax.broadcasted_iota(jnp.int32, (128, 128), 0)
    scale = DH ** (-0.5) * LOG2E

    def load(s, carry):
        at = pl.multiple_of(s * 128, 128)
        kv = recv_ref[pl.ds(2 * s, 2), 0:64, :].astype(F32).reshape(128, 128)
        frame = (2 * s + row // 64) * ROWS + side * 64 + row % 64
        bias = jnp.where(frame < length, 0.0, FLOOR)
        keyed = jnp.where(lane < 64, kv, jnp.where(lane == 64, bias, 0.0))
        k_ref[pl.ds(at, 128), :] = keyed.astype(BF16)
        vt_ref[:, pl.ds(at, 128)] = jnp.where(lane < 64, 1.0, kv).T.astype(BF16)
        raw = recv_ref[pl.ds(2 * s, 2), 64:128, :].astype(F32).reshape(128, 128).T
        fill = jnp.where(row == 64, 1.0, 0.0)
        other = jnp.concatenate([raw[64:], raw[:64]], axis=0)
        at = pl.multiple_of(s * 256, 256)
        qt_ref[:, pl.ds(at, 128)] = jnp.where(row < 64, raw, fill).astype(BF16)
        qt_ref[:, pl.ds(at + 128, 128)] = jnp.where(row < 64, other, fill).astype(BF16)
        return carry

    lax.fori_loop(0, sources // 2, load, 0, unroll=4)

    many = s0_ref.shape[1]
    chunk = 256
    pieces = k_ref.shape[0] // chunk
    blocks = sources * ROWS // many

    def score_piece(query, s_ref, k, top):
        at = slice(k * chunk, k * chunk + chunk)
        scores = dot(k_ref[at, :], query)
        s_ref[at, :] = scores
        best = jnp.max(scores.reshape(chunk // 8, 8, many), axis=0)
        return best if top is None else jnp.maximum(top, best)

    def weigh_piece(s_ref, best, k, accum):
        at = slice(k * chunk, k * chunk + chunk)
        weights = jnp.exp2((s_ref[at, :] - best) * scale).astype(BF16)
        addend = dot(vt_ref[:, at], weights)
        return addend if accum is None else accum + addend

    def finish(top):
        return jnp.max(top, axis=0, keepdims=True)

    def queries(b):
        return qt_ref[:, pl.ds(pl.multiple_of(b * many, many), many)]

    low8 = lane_of(8) < 64

    def store(b, accum, best):
        total = accum[0:1, :]
        result = accum[64:128, :] / total
        level = jnp.broadcast_to(best * scale + jnp.log2(total), (8, many))
        for g in range(many // 256):
            first = slice(g * 256, g * 256 + 128)
            second = slice(g * 256 + 128, g * 256 + 256)
            both = jnp.concatenate([result[:, first], result[:, second]], axis=0)
            at = b * (many // 256) + g
            c_ref[pl.ds(pl.multiple_of(at * 128, 128), 128), :] = both.T
            early, late = level[:, first], level[:, second]
            r_ref[pl.ds(pl.multiple_of(at * 16, 16), 8), :] = jnp.where(low8, early, swap(late))
            r_ref[pl.ds(pl.multiple_of(at * 16 + 8, 8), 8), :] = jnp.where(low8, swap(early), late)

    def step(b, s_ref, best, next_b, next_s):
        query = None if next_s is None else queries(next_b)
        top, accum = None, None
        for k in range(pieces):
            if query is not None:
                top = score_piece(query, next_s, k, top)
            accum = weigh_piece(s_ref, best, k, accum)
        store(b, accum, best)
        return None if query is None else finish(top)

    query, top = queries(0), None
    for k in range(pieces):
        top = score_piece(query, s0_ref, k, top)

    def pair(i, best):
        best = step(2 * i, s0_ref, best, 2 * i + 1, s1_ref)
        return step(2 * i + 1, s1_ref, best, 2 * i + 2, s0_ref)

    best = lax.fori_loop(0, blocks // 2 - 1, pair, finish(top))
    best = step(blocks - 2, s0_ref, best, blocks - 1, s1_ref)
    step(blocks - 1, s1_ref, best, None, None)

    low32 = lane_of(32) < 64
    row8 = lax.broadcasted_iota(jnp.int32, (8, 128), 0)

    def pack(d, carry):
        after = lax.rem(d + 1, sources)
        before = lax.rem(d + sources - 1, sources)
        out_ref[d, 0:64, :] = c_ref[pl.ds(pl.multiple_of(d * 64, 64), 64), :].astype(BF16)
        right = c_ref[pl.ds(pl.multiple_of(after * 64, 64), 32), :]
        left = c_ref[pl.ds(pl.multiple_of(before * 64 + 32, 32), 32), :]
        out_ref[d, 64:96, :] = jnp.where(low32, right, left).astype(BF16)
        own = r_ref[pl.ds(pl.multiple_of(d * 8, 8), 8), :]
        rim = jnp.where(
            low8,
            r_ref[pl.ds(pl.multiple_of(after * 8, 8), 8), :],
            r_ref[pl.ds(pl.multiple_of(before * 8, 8), 8), :],
        )
        rows = jnp.where(row8 < 3, own, rim)
        high = rows.astype(BF16).astype(F32)
        rest = rows - high
        middle = rest.astype(BF16).astype(F32)
        last = rest - middle
        level = row8 % 3
        rows = jnp.where(level == 0, high, jnp.where(level == 1, middle, last))
        out_ref[d, 96:112, :] = jnp.concatenate([rows, rows], axis=0).astype(BF16)
        return carry

    lax.fori_loop(0, sources, pack, 0, unroll=2)


def depthwise(source, source_row, taps_ref, order, target, count):
    def rows(i, carry):
        first = source_row + i * 8
        taps = [taps_ref[t * 8 : t * 8 + 8, :] for t in order]
        sums = [None] * 8
        for s in range(KERNEL + 7):
            piece = source[pl.ds(pl.multiple_of((first + s) * 8, 8), 8), :]
            for o in range(8):
                if 0 <= s - o < KERNEL:
                    term = taps[s - o] * piece
                    sums[o] = term if sums[o] is None else sums[o] + term
        for o in range(8):
            target[pl.ds(pl.multiple_of((i * 8 + o) * 8, 8), 8), :] = sums[o]
        return carry

    lax.fori_loop(0, count // 8, rows, 0, unroll=TAP_UNROLL)


def put_rows(ref, row, tile, values):
    for r in range(0, values.shape[0], 8):
        ref[pl.ds((row + r) * 8 + tile, 8, stride=8), :] = values[r : r + 8]


def get_rows(ref, row, count):
    groups = []
    for r in range(0, count, 8):
        tiles = [ref[pl.ds((row + r) * 8 + t, 8, stride=8), :] for t in range(8)]
        groups.append(jnp.concatenate(tiles, axis=1))
    return jnp.concatenate(groups, axis=0) if len(groups) > 1 else groups[0]


def place_context(ctx_in, base, ctx_ref, rim):
    row8 = lax.broadcasted_iota(jnp.int32, (8, 128), 0)
    zero = jnp.zeros((8, 128), F32)
    levels = [[zero, zero], [zero, zero]]
    for h in range(HEADS):
        for side in range(2):
            block = ctx_in[base + h * 2 + side, 96:112, :].astype(F32)
            for kind in range(2):
                at = kind * 3
                level = block[at : at + 1] + block[at + 1 : at + 2] + block[at + 2 : at + 3]
                levels[kind][side] = jnp.where(row8 == h, level, levels[kind][side])
    shares = []
    for first, second in levels:
        shares.append(1.0 / (1.0 + jnp.exp2(second - first)))
        shares.append(1.0 / (1.0 + jnp.exp2(first - second)))
    share = jnp.concatenate(shares + [jnp.zeros((96, 128), F32)], axis=0).T
    low = lane_of(96) < 64
    low_rows = lane_of(ROWS) < 64
    for t in range(HEADS // 2):
        at = slice(t * 128, t * 128 + 128)
        own = left = right = None
        for side in range(2):
            even = ctx_in[base + t * 4 + side, 0:96, :].astype(F32)
            odd = ctx_in[base + t * 4 + 2 + side, 0:96, :].astype(F32)
            first = jnp.where(low, even, swap(odd))
            second = jnp.where(low, swap(even), odd)
            scale = []
            for kind in range(2):
                column = kind * 16 + side * 8 + 2 * t
                scale.append(jnp.where(
                    low_rows, share[:, column : column + 1], share[:, column + 1 : column + 2]
                ))
            part = jnp.concatenate([first[:64], second[:64]], axis=0) * scale[0]
            after = first[64:96] * scale[1][0:32]
            before = second[64:96] * scale[1][96:128]
            own = part if own is None else own + part
            left = before if left is None else left + before
            right = after if right is None else right + after
        ctx_ref[0:rim, at] = left[RIM - rim :].astype(BF16)
        ctx_ref[rim : rim + ROWS, at] = own.astype(BF16)
        ctx_ref[rim + ROWS :, at] = right[:rim].astype(BF16)


def place_taps(depth_ref, taps_ref):
    for r in range(0, KERNEL + 1, 8):
        got = min(8, KERNEL - r)
        block = depth_ref[r : r + got, :].astype(F32)
        if got < 8:
            block = jnp.concatenate([block, jnp.zeros((8 - got, WIDTH), F32)], axis=0)
        for t in range(8):
            put_rows(taps_ref, r, t, block[:, t * 128 : t * 128 + 128])


def to_lowered(x_ref, ctx_ref, wao_ref, resid_ref, low_ref):
    for j in range(4):
        at = slice(j * 256, j * 256 + 256)
        joined = x_ref[:, at].astype(F32) + dot(ctx_ref[...], wao_ref[:, at])
        resid_ref[:, at] = joined.astype(BF16)

    def lower(i, carry):
        at = pl.ds(pl.multiple_of(i * 16, 16), 16)
        centred, inverse = moments(resid_ref[at, :].astype(F32))
        low_ref[at, :] = (centred * inverse).astype(BF16)
        return carry

    lax.fori_loop(0, x_ref.shape[0] // 16, lower, 0, unroll=UNROLL)


def to_gated(low_ref, win_ref, g2_ref, frame, length, keep):
    live = jnp.where((frame >= 0) & (frame < length), 1.0, 0.0)
    for j in range(4):
        at = slice(j * 256, j * 256 + 256)
        gate_at = slice(WIDTH + j * 256, WIDTH + j * 256 + 256)
        value = dot(low_ref[...], win_ref[:, at])
        gate = sigmoid(dot(low_ref[...], win_ref[:, gate_at]))
        if keep is not None:
            mv_ref, sg_ref = keep
            mv_ref[:, at] = value[RIM : RIM + ROWS]
            sg_ref[:, at] = gate[RIM : RIM + ROWS]
        gated = (value * gate * live).astype(BF16).astype(F32)
        for t in range(2):
            put_rows(g2_ref, 0, j * 2 + t, gated[:, t * 128 : t * 128 + 128])


def clean_kernel(
    scal_ref, ctx_hbm, clean_hbm, cot_hbm, up_hbm, down_hbm,
    wao_hbm, win_hbm, depth_hbm, wout_hbm,
    own_out, send_out, gm_out, go_out, sw_out, gs_out, gg2_out, g2_out, resid_out,
    ctx_in, wao_ref, win_ref, depth_ref, wout_ref,
    own_ref, send_ref, gm_ref, go_ref, sw_ref, gs_ref, gg2_ref, g2_ref, resid_ref,
    ctx_ref, x_ref, low_ref, mv_ref, sg_ref, s2_ref, zed_ref, zinv_ref, gox_ref, gsp2_ref, taps_ref,
    in_sems, out_sems,
):
    first_frame, length, core = scal_ref[0], scal_ref[1], scal_ref[2]
    half = RIM // 2
    copies = [
        pltpu.make_async_copy(source, target, in_sems.at[i])
        for i, (source, target) in enumerate((
            (ctx_hbm.at[pl.ds(0, 16)], ctx_in),
            (up_hbm.at[pl.ds(0, RIM)], x_ref.at[pl.ds(0, RIM)]),
            (clean_hbm, x_ref.at[pl.ds(RIM, ROWS)]),
            (down_hbm.at[pl.ds(0, RIM)], x_ref.at[pl.ds(RIM + ROWS, RIM)]),
            (wao_hbm, wao_ref),
            (depth_hbm, depth_ref),
            (up_hbm.at[pl.ds(RIM + half, half)], gox_ref.at[pl.ds(0, half)]),
            (cot_hbm, gox_ref.at[pl.ds(half, ROWS)]),
            (down_hbm.at[pl.ds(RIM + half, half)], gox_ref.at[pl.ds(half + ROWS, half)]),
            (win_hbm, win_ref),
            (wout_hbm, wout_ref),
        ))
    ]
    for copy in copies:
        copy.start()
    results = [
        pltpu.make_async_copy(source, target, out_sems.at[i])
        for i, (source, target) in enumerate((
            (own_ref, own_out), (send_ref, send_out), (gm_ref, gm_out), (go_ref, go_out),
            (sw_ref, sw_out), (gs_ref, gs_out), (gg2_ref, gg2_out), (g2_ref, g2_out),
            (resid_ref, resid_out),
        ))
    ]
    own_copy, send_copy, gm_copy, go_copy, sw_copy, gs_copy, gg2_copy, g2_copy, resid_copy = results
    copies[0].wait()
    place_context(ctx_in, 0, ctx_ref, RIM)
    for copy in copies[1:9]:
        copy.wait()
    place_taps(depth_ref, taps_ref)
    for row in range(0, INNER, 16):
        at = slice(row, row + 16)
        frame = first_frame - half + row + lax.broadcasted_iota(jnp.int32, (16, 1), 0)
        gox_ref[at, :] = (gox_ref[at, :].astype(F32) * jnp.where(frame < length, 1.0, 0.0)).astype(BF16)
    go_ref[...] = gox_ref[half : half + ROWS, :]
    go_copy.start()

    to_lowered(x_ref, ctx_ref, wao_ref, resid_ref, low_ref)
    resid_copy.start()
    frame = first_frame - RIM + lax.broadcasted_iota(jnp.int32, (CLEAN, 1), 0)
    copies[9].wait()
    to_gated(low_ref, win_ref, g2_ref, frame, length, (mv_ref, sg_ref))
    g2_copy.start()
    forward = list(range(KERNEL))
    edge = half - KERNEL // 2
    depthwise(g2_ref, edge, taps_ref, forward, s2_ref, INNER)

    def clean_rows(i, carry):
        r = pl.multiple_of(i * 16, 16)
        centred, inverse = moments(get_rows(s2_ref, r, 16))
        zed = centred * inverse
        zed_ref[pl.ds(r, 16), :] = zed
        zinv_ref[pl.ds(r, 16), :] = jnp.broadcast_to(inverse, (16, 128))
        sw_ref[pl.ds(r, 16), :] = (zed * sigmoid(zed)).astype(BF16)
        return carry

    lax.fori_loop(0, INNER // 16, clean_rows, 0, unroll=UNROLL)
    sw_copy.start()

    for part in range(4):
        dest = part * 256
        source, row = (low_ref, RIM) if part < 2 else (sw_ref, half)
        lo = (part % 2) * 512
        first = source[row : row + ROWS, lo : lo + 256].astype(F32)
        second = source[row : row + ROWS, lo + 256 : lo + 512].astype(F32)
        own_ref[:, dest : dest + 256] = jnp.where(core == 0, first, second).astype(BF16)
        send_ref[:, dest : dest + 256] = jnp.where(core == 0, second, first).astype(BF16)
    own_copy.start()
    send_copy.start()

    copies[10].wait()
    for j in range(4):
        at = slice(j * 256, j * 256 + 256)
        gs_ref[:, at] = dot_nt(gox_ref[...], wout_ref[at, :])
    gs_copy.start()

    def back_rows(i, carry):
        r = pl.multiple_of(i * 16, 16)
        zed = zed_ref[pl.ds(r, 16), :]
        grad = gs_ref[pl.ds(r, 16), :]
        gate = sigmoid(zed)
        grad_zed = grad * (gate * (1.0 + zed * (1.0 - gate)))
        mean = jnp.mean(grad_zed, axis=-1, keepdims=True)
        along = jnp.mean(grad_zed * zed, axis=-1, keepdims=True)
        result = (grad_zed - mean - zed * along) * zinv_ref[pl.ds(r, 16), 0:1]
        for g in range(0, 16, 8):
            for t in range(8):
                gsp2_ref[pl.ds((r + g) * 8 + t, 8, stride=8), :] = result[
                    g : g + 8, t * 128 : t * 128 + 128
                ]
        return carry

    lax.fori_loop(0, INNER // 16, back_rows, 0, unroll=UNROLL)
    depthwise(gsp2_ref, edge, taps_ref, forward[::-1], gg2_ref, ROWS)
    gg2_copy.start()

    def mixed_rows(i, carry):
        r = pl.multiple_of(i * 16, 16)
        at = pl.ds(r, 16)
        frame = first_frame + r + lax.broadcasted_iota(jnp.int32, (16, 1), 0)
        grad = get_rows(gg2_ref, r, 16) * jnp.where(frame < length, 1.0, 0.0)
        gate = sg_ref[at, :]
        gm_ref[at, 0:WIDTH] = (grad * gate).astype(BF16)
        gm_ref[at, WIDTH:] = (grad * mv_ref[at, :] * gate * (1.0 - gate)).astype(BF16)
        return carry

    lax.fori_loop(0, ROWS // 16, mixed_rows, 0, unroll=UNROLL)

    gm_copy.start()
    for copy in results:
        copy.wait()


def patch_kernel(
    scal_ref, site_ref, ctx_in, patched_ref, up_ref, down_ref,
    wao_ref, win_ref, depth_ref, wout_ref,
    gm_ref, go_ref, swc_ref, gs_ref, gg2_ref, g2c_ref, residc_ref,
    attr_ref,
    ctx_ref, x_ref, resid_ref, low_ref, g2_ref, s2_ref, sw_ref, gl_ref, t0_ref, t1_ref, t2_ref, taps_ref,
):
    first_frame, length = scal_ref[0], scal_ref[1]
    half = RIM // 2
    place_context(ctx_in, 16, ctx_ref, half)
    x_ref[0:half, :] = up_ref[RIM : RIM + half, :]
    x_ref[half : half + ROWS, :] = patched_ref[...]
    x_ref[half + ROWS : PATCH, :] = down_ref[RIM : RIM + half, :]
    place_taps(depth_ref, taps_ref)
    to_lowered(x_ref, ctx_ref, wao_ref, resid_ref, low_ref)
    frame = first_frame - half + lax.broadcasted_iota(jnp.int32, (PATCH, 1), 0)
    to_gated(low_ref, win_ref, g2_ref, frame, length, None)
    depthwise(g2_ref, half - KERNEL // 2, taps_ref, list(range(KERNEL)), s2_ref, ROWS)
    sw_ref[0:ROWS, :] = swc_ref[half : half + ROWS, :]

    def patch_rows(i, carry):
        r = pl.multiple_of(i * 16, 16)
        at = pl.ds(r, 16)
        inner = pl.ds(pl.multiple_of(half + r, 16), 16)
        centred, inverse = moments(get_rows(s2_ref, r, 16))
        zed = centred * inverse
        swished = (zed * sigmoid(zed)).astype(BF16)
        sw_ref[pl.ds(pl.multiple_of(ROWS + r, 16), 16), :] = swished
        gap = swished.astype(F32) - sw_ref[at, :].astype(F32)
        t2_ref[at, :] = lane_sum(gap * gs_ref[inner, :])
        frame = first_frame + r + lax.broadcasted_iota(jnp.int32, (16, 1), 0)
        grad = get_rows(gg2_ref, r, 16) * jnp.where(frame < length, 1.0, 0.0)
        gap = get_rows(g2_ref, half + r, 16) - get_rows(g2c_ref, RIM + r, 16)
        t1_ref[at, :] = lane_sum(gap * grad)
        return carry

    lax.fori_loop(0, ROWS // 16, patch_rows, 0, unroll=UNROLL)

    t3 = jnp.zeros((ROWS, 128), F32)
    for j in range(4):
        at = slice(j * 256, j * 256 + 256)
        out = dot(sw_ref[...], wout_ref[:, at])
        out_clean = residc_ref[RIM : RIM + ROWS, at].astype(F32) + out[:ROWS]
        out_patch = resid_ref[half : half + ROWS, at].astype(F32) + out[ROWS:]
        gap = out_patch.astype(BF16).astype(F32) - out_clean.astype(BF16).astype(F32)
        t3 = t3 + lane_sum(gap * go_ref[:, at].astype(F32))
    for j in range(4):
        at = slice(j * 256, j * 256 + 256)
        gl_ref[:, at] = dot_nt(gm_ref[...], win_ref[at, :])

    def resid_rows(i, carry):
        r = pl.multiple_of(i * 16, 16)
        at = pl.ds(r, 16)
        clean = residc_ref[pl.ds(pl.multiple_of(RIM + r, 16), 16), :].astype(F32)
        patch = resid_ref[pl.ds(pl.multiple_of(half + r, 16), 16), :].astype(F32)
        centred, inverse = moments(clean)
        normed = centred * inverse
        grad = gl_ref[at, :]
        mean = jnp.mean(grad, axis=-1, keepdims=True)
        along = jnp.mean(grad * normed, axis=-1, keepdims=True)
        grad_resid = go_ref[at, :].astype(F32) + (grad - mean - normed * along) * inverse
        t0_ref[at, :] = lane_sum((patch - clean) * grad_resid)
        return carry

    lax.fori_loop(0, ROWS // 16, resid_rows, 0, unroll=UNROLL)

    columns = [
        jnp.sum(part, axis=1, keepdims=True) for part in (t0_ref[...], t1_ref[...], t2_ref[...], t3)
    ]
    lane = lane_of(ROWS)
    chosen = jnp.zeros((ROWS, 128), F32)
    for i in range(attr_ref.shape[0]):
        site = site_ref[i]
        column = columns[0]
        for k in range(1, 4):
            column = jnp.where(site == k, columns[k], column)
        chosen = jnp.where(lane == i, column, chosen)
    attr_ref[...] = chosen.T[: attr_ref.shape[0]]


def weight_kernel(
    own_hbm, other_hbm, gm_hbm, gm_other_hbm, go_hbm, go_other_hbm, out_hbm,
    left_ref, gm_ref, go_ref, out_ref, in_sems, out_sems,
):
    pairs = (
        (own_hbm, left_ref, 0), (other_hbm, left_ref, ROWS), (go_hbm, go_ref, 0),
        (go_other_hbm, go_ref, ROWS), (gm_hbm, gm_ref, 0), (gm_other_hbm, gm_ref, ROWS),
    )
    copies = [
        pltpu.make_async_copy(source, target.at[pl.ds(row, ROWS)], in_sems.at[i])
        for i, (source, target, row) in enumerate(pairs)
    ]
    for copy in copies:
        copy.start()

    def send(i):
        at = pl.ds(i * WIDTH, WIDTH)
        return pltpu.make_async_copy(out_ref.at[:, :, at], out_hbm.at[:, :, at], out_sems.at[i])

    def put(at, product):
        half = product.shape[0] // 2
        lower = product[:half].reshape(half // 8, 8, 256)
        upper = product[half:].reshape(half // 8, 8, 256)
        out_ref[:, :, at : at + 256] = jnp.concatenate([lower, upper], axis=1).astype(BF16)

    for copy in copies[:4]:
        copy.wait()
    swished = left_ref[:, 512:1024].T
    for j in range(0, WIDTH, 256):
        put(2 * WIDTH + j, dot(swished, go_ref[:, j : j + 256]))
    send(2).start()
    for copy in copies[4:]:
        copy.wait()
    low = left_ref[:, 0:512].T
    for j in range(0, 2 * WIDTH, 256):
        put(j, dot(low, gm_ref[:, j : j + 256]))
        if j + 256 == WIDTH:
            send(0).start()
    send(1).start()
    for i in range(3):
        send(i).wait()


VMEM = pl.BlockSpec(memory_space=pltpu.VMEM)
SMEM = pl.BlockSpec(memory_space=pltpu.SMEM)
HBM = pl.BlockSpec(memory_space=pltpu.HBM)


def kernel_call(body, out_shape, in_specs, scratch, limit, flops, moved, out_spec=VMEM):
    return pl.pallas_call(
        body,
        out_shape=out_shape,
        in_specs=in_specs,
        out_specs=[out_spec] * len(out_shape),
        scratch_shapes=scratch,
        compiler_params=pltpu.CompilerParams(vmem_limit_bytes=limit << 20),
        cost_estimate=pl.CostEstimate(flops=flops, bytes_accessed=moved, transcendentals=0),
    )


def shape(dims, dtype):
    return jax.ShapeDtypeStruct(dims, dtype)


def per_device(
    clean_input, corrupt_input, patch_mask, lengths, site_ids, w_query, w_key, w_value,
    w_attn_out, w_pointwise_in, depth_kernel, w_pointwise_out, cotangent,
):
    frames = lax.axis_size("frames")
    position = lax.axis_index("frames")
    core = lax.rem(lax.axis_index("dp"), 2)
    scalars = jnp.stack(
        [position * ROWS, lengths[0], core, lax.rem(position, 2)]
    ).astype(jnp.int32)
    clean, corrupt, cot = clean_input[0], corrupt_input[0], cotangent[0]

    msg, patched, up, down = kernel_call(
        project_kernel,
        [shape((frames, ROWS, 128), BF16), shape((ROWS, WIDTH), BF16),
         shape((2 * RIM, WIDTH), BF16), shape((2 * RIM, WIDTH), BF16)],
        [HBM] * 3 + [VMEM] + [HBM] * 3,
        [pltpu.VMEM((2 * ROWS, WIDTH), BF16), pltpu.VMEM((ROWS, ROWS), F32),
         pltpu.VMEM((ROWS, WIDTH), BF16), pltpu.VMEM((ROWS, WIDTH), BF16),
         pltpu.VMEM((WIDTH, 512), BF16), pltpu.VMEM((WIDTH, 512), BF16),
         pltpu.VMEM((WIDTH, 512), BF16), pltpu.SemaphoreType.DMA((7,))],
        62, 8 * 10**8, 6 * 10**6,
    )(clean, corrupt, cot, patch_mask, w_query, w_key, w_value)
    forward = [(i, i + 1) for i in range(frames - 1)]
    backward = [(i + 1, i) for i in range(frames - 1)]
    from_left = lax.ppermute(up, "frames", forward)
    from_right = lax.ppermute(down, "frames", backward)
    recv = lax.all_to_all(msg, "frames", 0, 0, tiled=True)
    keys = frames * ROWS // 2
    (context,) = kernel_call(
        attend_kernel,
        [shape((frames, 112, 128), BF16)],
        [SMEM, VMEM],
        [pltpu.VMEM((keys, 128), BF16), pltpu.VMEM((128, keys), BF16),
         pltpu.VMEM((128, 2 * keys), BF16),
         pltpu.VMEM((keys, 512), F32), pltpu.VMEM((keys, 512), F32),
         pltpu.VMEM((frames * 64, 128), F32), pltpu.VMEM((frames * 8, 128), F32)],
        20, 8 * 10**9, 10**6,
    )(scalars, recv)
    contexts = lax.all_to_all(context, "frames", 0, 0, tiled=True)
    own, send, grad_mixed, grad_output, swished, grad_swished, grad_gated, gated, resid = kernel_call(
        clean_kernel,
        [shape((ROWS, 1024), BF16), shape((ROWS, 1024), BF16), shape((ROWS, 2 * WIDTH), BF16),
         shape((ROWS, WIDTH), BF16), shape((INNER, WIDTH), BF16), shape((INNER, WIDTH), F32),
         shape((ROWS * 8, 128), F32), shape((CLEAN * 8, 128), F32), shape((CLEAN, WIDTH), BF16)],
        [SMEM] + [HBM] * 9,
        [pltpu.VMEM((16, 112, 128), BF16), pltpu.VMEM((512, WIDTH), BF16),
         pltpu.VMEM((WIDTH, 2 * WIDTH), BF16), pltpu.VMEM((KERNEL, WIDTH), BF16),
         pltpu.VMEM((WIDTH, WIDTH), BF16),
         pltpu.VMEM((ROWS, 1024), BF16), pltpu.VMEM((ROWS, 1024), BF16),
         pltpu.VMEM((ROWS, 2 * WIDTH), BF16), pltpu.VMEM((ROWS, WIDTH), BF16),
         pltpu.VMEM((INNER, WIDTH), BF16), pltpu.VMEM((INNER, WIDTH), F32),
         pltpu.VMEM((ROWS * 8, 128), F32), pltpu.VMEM((CLEAN * 8, 128), F32),
         pltpu.VMEM((CLEAN, WIDTH), BF16),
         pltpu.VMEM((CLEAN, 512), BF16), pltpu.VMEM((CLEAN, WIDTH), BF16),
         pltpu.VMEM((CLEAN, WIDTH), BF16),
         pltpu.VMEM((ROWS, WIDTH), F32), pltpu.VMEM((ROWS, WIDTH), F32),
         pltpu.VMEM((INNER * 8, 128), F32), pltpu.VMEM((INNER, WIDTH), F32),
         pltpu.VMEM((INNER, 128), F32), pltpu.VMEM((INNER, WIDTH), BF16),
         pltpu.VMEM((INNER * 8, 128), F32), pltpu.VMEM((32 * 8, 128), F32),
         pltpu.SemaphoreType.DMA((11,)), pltpu.SemaphoreType.DMA((9,))],
        59, 3 * 10**9, 10**7, HBM,
    )(scalars, contexts, clean, cot, from_left, from_right,
      w_attn_out, w_pointwise_in, depth_kernel, w_pointwise_out)

    cores = [(i, i ^ 1) for i in range(lax.axis_size("dp"))]
    other, gm_other, go_other = (
        lax.ppermute(part, "dp", cores) for part in (send, grad_mixed, grad_output)
    )
    (partial,) = kernel_call(
        weight_kernel,
        [shape((frames, 16, 3 * WIDTH), BF16)],
        [HBM] * 6,
        [pltpu.VMEM((2 * ROWS, WIDTH), BF16), pltpu.VMEM((2 * ROWS, 2 * WIDTH), BF16),
         pltpu.VMEM((2 * ROWS, WIDTH), BF16), pltpu.VMEM((frames, 16, 3 * WIDTH), BF16),
         pltpu.SemaphoreType.DMA((6,)), pltpu.SemaphoreType.DMA((3,))],
        59, 8 * 10**8, 10**7, HBM,
    )(own, other, grad_mixed, gm_other, grad_output, go_other)
    pieces = lax.all_to_all(partial, "frames", 0, 0, tiled=True)
    (attribution,) = kernel_call(
        patch_kernel,
        [shape((site_ids.shape[0], ROWS), F32)],
        [SMEM, SMEM] + [VMEM] * 15,
        [pltpu.VMEM((PATCH, 512), BF16), pltpu.VMEM((PATCH, WIDTH), BF16),
         pltpu.VMEM((PATCH, WIDTH), BF16), pltpu.VMEM((PATCH, WIDTH), BF16),
         pltpu.VMEM((PATCH * 8, 128), F32), pltpu.VMEM((ROWS * 8, 128), F32),
         pltpu.VMEM((2 * ROWS, WIDTH), BF16), pltpu.VMEM((ROWS, WIDTH), F32),
         pltpu.VMEM((ROWS, 128), F32), pltpu.VMEM((ROWS, 128), F32), pltpu.VMEM((ROWS, 128), F32),
         pltpu.VMEM((32 * 8, 128), F32)],
        28, 3 * 10**9, 10**7,
    )(scalars, site_ids, contexts, patched, from_left, from_right,
      w_attn_out, w_pointwise_in, depth_kernel, w_pointwise_out,
      grad_mixed, grad_output, swished, grad_swished, grad_gated, gated, resid)
    pieces, attribution = lax.optimization_barrier((pieces, attribution))
    summed = jnp.sum(pieces.astype(F32), axis=0)
    upper = lax.axis_index("dp") // 2
    mine = jnp.where(upper == 0, summed[:8], summed[8:])
    theirs = jnp.where(upper == 0, summed[8:], summed[:8])
    half_dp = lax.axis_size("dp") // 2
    theirs = lax.ppermute(
        theirs.astype(BF16), "dp", [(i, i ^ half_dp) for i in range(2 * half_dp)]
    ).astype(F32)
    return (
        attribution[None],
        mine[:, : 2 * WIDTH] + theirs[:, : 2 * WIDTH],
        mine[:, 2 * WIDTH :] + theirs[:, 2 * WIDTH :],
    )


def solution(mesh):
    placed = (
        P("dp", "frames", None), P("dp", "frames", None), P("dp", "frames"), P("dp"), P(), P(), P(),
        P(), P(), P(), P(), P(), P("dp", "frames", None),
    )
    return jax.shard_map(
        per_device,
        mesh=mesh,
        in_specs=placed,
        out_specs=(P("dp", None, "frames"), P(("dp", "frames"), None), P(("dp", "frames"), None)),
        check_vma=False,
    )
```

```python
import jax
import jax.numpy as jnp
from jax import lax
from jax.experimental import pallas as pl
from jax.experimental.pallas import tpu as pltpu
from jax.sharding import PartitionSpec as P

HEADS = 8
DH = 64
KERNEL = 31
RIM = 32
EPSILON = 1e-05
FLOOR = -1e30
LOG2E = 1.4426950408889634
F32 = jnp.float32
BF16 = jnp.bfloat16
ROWS = 128
WIDTH = 1024
CLEAN = ROWS + 2 * RIM
PATCH = ROWS + RIM
BOTH = CLEAN + PATCH
INNER = ROWS + RIM
UNROLL = True
TAP_UNROLL = 4
LOAD_UNROLL = 4
PACK_UNROLL = 4
CHUNK = 256


def lane_of(rows):
    return lax.broadcasted_iota(jnp.int32, (rows, 128), 1)


def swap(tile):
    return pltpu.roll(tile, 64, 1)


def moments(values):
    mean = jnp.mean(values, axis=-1, keepdims=True)
    centred = values - mean
    variance = jnp.mean(centred * centred, axis=-1, keepdims=True)
    return centred, lax.rsqrt(variance + EPSILON)


def dot(left, right):
    return jnp.dot(left, right, preferred_element_type=F32)


def dot_nt(left, right):
    return lax.dot_general(left, right, (((1,), (1,)), ((), ())), preferred_element_type=F32)


def dot_tn(left, right):
    return lax.dot_general(left, right, (((0,), (0,)), ((), ())), preferred_element_type=F32)


def sigmoid(values):
    return 1.0 / (1.0 + jnp.exp(-values))


def lane_sum(values):
    total = values[:, :128]
    for start in range(128, values.shape[1], 128):
        total = total + values[:, start : start + 128]
    return total


def project_kernel(
    clean_hbm, corrupt_hbm, cot_hbm, mask_ref, wq_hbm, wk_hbm, wv_hbm,
    msg_ref, patched_ref, up_ref, down_ref,
    hidden_ref, mask_col, clean_ref, corrupt_ref, wq_ref, wk_ref, wv_ref, sems,
):
    half = RIM // 2
    copies = [
        pltpu.make_async_copy(source, target, sems.at[i])
        for i, (source, target) in enumerate((
            (clean_hbm, clean_ref),
            (corrupt_hbm, corrupt_ref),
            (wk_hbm, wk_ref),
            (wv_hbm, wv_ref),
            (wq_hbm, wq_ref),
            (cot_hbm.at[pl.ds(ROWS - half, half)], up_ref.at[pl.ds(RIM + half, half)]),
            (cot_hbm.at[pl.ds(0, half)], down_ref.at[pl.ds(RIM + half, half)]),
        ))
    ]
    for copy in copies:
        copy.start()
    spread_mask = jnp.broadcast_to(mask_ref[...].astype(F32), (ROWS, ROWS))
    mask_col[...] = spread_mask.T
    copies[0].wait()
    copies[1].wait()

    def rows(i, carry):
        at = pl.ds(pl.multiple_of(i * 16, 16), 16)
        below = pl.ds(pl.multiple_of(ROWS + i * 16, 16), 16)
        clean = clean_ref[at, :].astype(F32)
        corrupt = corrupt_ref[at, :].astype(F32)
        patched = jnp.where(mask_col[at, 0:1] == 1.0, corrupt, clean)
        patched_ref[at, :] = patched.astype(BF16)
        for dest, source in ((at, clean), (below, patched)):
            centred, inverse = moments(source)
            hidden_ref[dest, :] = (centred * inverse).astype(BF16)
        return carry

    lax.fori_loop(0, ROWS // 16, rows, 0, unroll=UNROLL)
    up_ref[0:RIM, :] = clean_ref[ROWS - RIM : ROWS, :]
    up_ref[RIM : RIM + half, :] = patched_ref[ROWS - half : ROWS, :]
    down_ref[0:RIM, :] = clean_ref[0:RIM, :]
    down_ref[RIM : RIM + half, :] = patched_ref[0:half, :]
    for copy in copies[2:]:
        copy.wait()

    low = lane_of(ROWS) < 64
    low_q = lane_of(64) < 64
    for pair in range(2):
        cols = slice(pair * 256, pair * 256 + 256)
        hidden = hidden_ref[...]
        query = dot(hidden, wq_ref[:, cols])
        keys = dot(hidden, wk_ref[:, cols])
        values = dot(hidden, wv_ref[:, cols])
        for sub in range(2):
            tile = slice(sub * 128, sub * 128 + 128)
            for run in range(2):
                part = slice(run * ROWS, run * ROWS + ROWS)
                k, v, q = keys[part, tile], values[part, tile], query[part, tile]
                base = run * 16 + (pair * 2 + sub) * 4
                kv = (jnp.where(low, k, swap(v)).astype(BF16), jnp.where(low, swap(k), v).astype(BF16))
                early, late = q[:64], q[64:]
                asked = (
                    jnp.where(low_q, early, swap(late)).astype(BF16),
                    jnp.where(low_q, swap(early), late).astype(BF16),
                )
                for odd in range(2):
                    for side in range(2):
                        dest = base + odd * 2 + side
                        msg_ref[dest, 0:64, :] = kv[odd][side * 64 : side * 64 + 64]
                        msg_ref[dest, 64:128, :] = asked[odd]


def attend_kernel(
    scal_ref, recv_ref, out_ref, k_ref, vt_ref, qt_ref, s0_ref, s1_ref, c_ref, r_ref
):
    length, side = scal_ref[1], scal_ref[3]
    sources = recv_ref.shape[0]
    lane = lane_of(128)
    row = lax.broadcasted_iota(jnp.int32, (128, 128), 0)
    scale = DH ** (-0.5) * LOG2E

    def load(s, carry):
        at = pl.multiple_of(s * 128, 128)
        kv = recv_ref[pl.ds(2 * s, 2), 0:64, :].astype(F32).reshape(128, 128)
        frame = (2 * s + row // 64) * ROWS + side * 64 + row % 64
        bias = jnp.where(frame < length, 0.0, FLOOR)
        keyed = jnp.where(lane < 64, kv, jnp.where(lane == 64, bias, 0.0))
        k_ref[pl.ds(at, 128), :] = keyed.astype(BF16)
        vt_ref[:, pl.ds(at, 128)] = jnp.where(lane < 64, 1.0, kv).T.astype(BF16)
        raw = recv_ref[pl.ds(2 * s, 2), 64:128, :].astype(F32).reshape(128, 128).T
        fill = jnp.where(row == 64, 1.0, 0.0)
        other = jnp.concatenate([raw[64:], raw[:64]], axis=0)
        at = pl.multiple_of(s * 256, 256)
        qt_ref[:, pl.ds(at, 128)] = jnp.where(row < 64, raw, fill).astype(BF16)
        qt_ref[:, pl.ds(at + 128, 128)] = jnp.where(row < 64, other, fill).astype(BF16)
        return carry

    lax.fori_loop(0, sources // 2, load, 0, unroll=LOAD_UNROLL)

    many = s0_ref.shape[1]
    chunk = CHUNK
    pieces = k_ref.shape[0] // chunk
    blocks = sources * ROWS // many

    def score_piece(query, s_ref, k, top):
        at = slice(k * chunk, k * chunk + chunk)
        scores = dot(k_ref[at, :], query)
        s_ref[at, :] = scores
        best = jnp.max(scores.reshape(chunk // 8, 8, many), axis=0)
        return best if top is None else jnp.maximum(top, best)

    def weigh_piece(s_ref, best, k, accum):
        at = slice(k * chunk, k * chunk + chunk)
        weights = jnp.exp2((s_ref[at, :] - best) * scale).astype(BF16)
        addend = dot(vt_ref[:, at], weights)
        return addend if accum is None else accum + addend

    def finish(top):
        return jnp.max(top, axis=0, keepdims=True)

    def queries(b):
        return qt_ref[:, pl.ds(pl.multiple_of(b * many, many), many)]

    low8 = lane_of(8) < 64

    def store(b, accum, best):
        total = accum[0:1, :]
        result = accum[64:128, :] / total
        level = jnp.broadcast_to(best * scale + jnp.log2(total), (8, many))
        for g in range(many // 256):
            first = slice(g * 256, g * 256 + 128)
            second = slice(g * 256 + 128, g * 256 + 256)
            both = jnp.concatenate([result[:, first], result[:, second]], axis=0)
            at = b * (many // 256) + g
            c_ref[pl.ds(pl.multiple_of(at * 128, 128), 128), :] = both.T
            early, late = level[:, first], level[:, second]
            r_ref[pl.ds(pl.multiple_of(at * 16, 16), 8), :] = jnp.where(low8, early, swap(late))
            r_ref[pl.ds(pl.multiple_of(at * 16 + 8, 8), 8), :] = jnp.where(low8, swap(early), late)

    def step(b, s_ref, best, next_b, next_s):
        query = None if next_s is None else queries(next_b)
        top, accum = None, None
        for k in range(pieces):
            if query is not None:
                top = score_piece(query, next_s, k, top)
            accum = weigh_piece(s_ref, best, k, accum)
        store(b, accum, best)
        return None if query is None else finish(top)

    query, top = queries(0), None
    for k in range(pieces):
        top = score_piece(query, s0_ref, k, top)

    def pair(i, best):
        best = step(2 * i, s0_ref, best, 2 * i + 1, s1_ref)
        return step(2 * i + 1, s1_ref, best, 2 * i + 2, s0_ref)

    best = lax.fori_loop(0, blocks // 2 - 1, pair, finish(top))
    best = step(blocks - 2, s0_ref, best, blocks - 1, s1_ref)
    step(blocks - 1, s1_ref, best, None, None)

    low32 = lane_of(32) < 64
    row8 = lax.broadcasted_iota(jnp.int32, (8, 128), 0)

    def pack(d, carry):
        after = lax.rem(d + 1, sources)
        before = lax.rem(d + sources - 1, sources)
        out_ref[d, 0:64, :] = c_ref[pl.ds(pl.multiple_of(d * 64, 64), 64), :].astype(BF16)
        right = c_ref[pl.ds(pl.multiple_of(after * 64, 64), 32), :]
        left = c_ref[pl.ds(pl.multiple_of(before * 64 + 32, 32), 32), :]
        out_ref[d, 64:96, :] = jnp.where(low32, right, left).astype(BF16)
        own = r_ref[pl.ds(pl.multiple_of(d * 8, 8), 8), :]
        rim = jnp.where(
            low8,
            r_ref[pl.ds(pl.multiple_of(after * 8, 8), 8), :],
            r_ref[pl.ds(pl.multiple_of(before * 8, 8), 8), :],
        )
        rows = jnp.where(row8 < 3, own, rim)
        high = rows.astype(BF16).astype(F32)
        rest = rows - high
        middle = rest.astype(BF16).astype(F32)
        last = rest - middle
        level = row8 % 3
        rows = jnp.where(level == 0, high, jnp.where(level == 1, middle, last))
        out_ref[d, 96:112, :] = jnp.concatenate([rows, rows], axis=0).astype(BF16)
        return carry

    lax.fori_loop(0, sources, pack, 0, unroll=PACK_UNROLL)


def depthwise(source, source_row, taps_ref, order, target, count):
    def rows(i, carry):
        first = source_row + i * 8
        taps = [taps_ref[t * 8 : t * 8 + 8, :] for t in order]
        sums = [None] * 8
        for s in range(KERNEL + 7):
            piece = source[pl.ds(pl.multiple_of((first + s) * 8, 8), 8), :]
            for o in range(8):
                if 0 <= s - o < KERNEL:
                    term = taps[s - o] * piece
                    sums[o] = term if sums[o] is None else sums[o] + term
        for o in range(8):
            target[pl.ds(pl.multiple_of((i * 8 + o) * 8, 8), 8), :] = sums[o]
        return carry

    lax.fori_loop(0, count // 8, rows, 0, unroll=TAP_UNROLL)


def put_rows(ref, row, tile, values):
    for r in range(0, values.shape[0], 8):
        ref[pl.ds((row + r) * 8 + tile, 8, stride=8), :] = values[r : r + 8]


def get_rows(ref, row, count):
    groups = []
    for r in range(0, count, 8):
        tiles = [ref[pl.ds((row + r) * 8 + t, 8, stride=8), :] for t in range(8)]
        groups.append(jnp.concatenate(tiles, axis=1))
    return jnp.concatenate(groups, axis=0) if len(groups) > 1 else groups[0]


def place_context(ctx_in, base, ctx_ref, rim):
    row8 = lax.broadcasted_iota(jnp.int32, (8, 128), 0)
    zero = jnp.zeros((8, 128), F32)
    levels = [[zero, zero], [zero, zero]]
    for h in range(HEADS):
        for side in range(2):
            block = ctx_in[base + h * 2 + side, 96:112, :].astype(F32)
            for kind in range(2):
                at = kind * 3
                level = block[at : at + 1] + block[at + 1 : at + 2] + block[at + 2 : at + 3]
                levels[kind][side] = jnp.where(row8 == h, level, levels[kind][side])
    shares = []
    for first, second in levels:
        shares.append(1.0 / (1.0 + jnp.exp2(second - first)))
        shares.append(1.0 / (1.0 + jnp.exp2(first - second)))
    share = jnp.concatenate(shares + [jnp.zeros((96, 128), F32)], axis=0).T
    low = lane_of(96) < 64
    low_rows = lane_of(ROWS) < 64
    for t in range(HEADS // 2):
        at = slice(t * 128, t * 128 + 128)
        own = left = right = None
        for side in range(2):
            even = ctx_in[base + t * 4 + side, 0:96, :].astype(F32)
            odd = ctx_in[base + t * 4 + 2 + side, 0:96, :].astype(F32)
            first = jnp.where(low, even, swap(odd))
            second = jnp.where(low, swap(even), odd)
            scale = []
            for kind in range(2):
                column = kind * 16 + side * 8 + 2 * t
                scale.append(jnp.where(
                    low_rows, share[:, column : column + 1], share[:, column + 1 : column + 2]
                ))
            part = jnp.concatenate([first[:64], second[:64]], axis=0) * scale[0]
            after = first[64:96] * scale[1][0:32]
            before = second[64:96] * scale[1][96:128]
            own = part if own is None else own + part
            left = before if left is None else left + before
            right = after if right is None else right + after
        ctx_ref[0:rim, at] = left[RIM - rim :].astype(BF16)
        ctx_ref[rim : rim + ROWS, at] = own.astype(BF16)
        ctx_ref[rim + ROWS :, at] = right[:rim].astype(BF16)


def place_taps(depth_ref, taps_ref):
    for r in range(0, KERNEL + 1, 8):
        got = min(8, KERNEL - r)
        block = depth_ref[r : r + got, :].astype(F32)
        if got < 8:
            block = jnp.concatenate([block, jnp.zeros((8 - got, WIDTH), F32)], axis=0)
        for t in range(8):
            put_rows(taps_ref, r, t, block[:, t * 128 : t * 128 + 128])


def to_lowered(x_ref, ctx_ref, wao_ref, resid_ref, low_ref):
    for j in range(4):
        at = slice(j * 256, j * 256 + 256)
        joined = x_ref[:, at].astype(F32) + dot(ctx_ref[...], wao_ref[:, at])
        resid_ref[:, at] = joined.astype(BF16)

    def lower(i, carry):
        at = pl.ds(pl.multiple_of(i * 16, 16), 16)
        centred, inverse = moments(resid_ref[at, :].astype(F32))
        low_ref[at, :] = (centred * inverse).astype(BF16)
        return carry

    lax.fori_loop(0, x_ref.shape[0] // 16, lower, 0, unroll=UNROLL)


def to_gated(low_ref, win_ref, g2_ref, frame, length, keep, arrivals=None):
    live = jnp.where((frame >= 0) & (frame < length), 1.0, 0.0)
    for j in range(4):
        at = slice(j * 256, j * 256 + 256)
        gate_at = slice(WIDTH + j * 256, WIDTH + j * 256 + 256)
        if arrivals is not None:
            arrivals[2 * j].wait()
            arrivals[2 * j + 1].wait()
        value = dot(low_ref[...], win_ref[:, at])
        gate = sigmoid(dot(low_ref[...], win_ref[:, gate_at]))
        if keep is not None:
            mv_ref, sg_ref = keep
            mv_ref[:, at] = value[RIM : RIM + ROWS]
            sg_ref[:, at] = gate[RIM : RIM + ROWS]
        gated = (value * gate * live).astype(BF16).astype(F32)
        for t in range(2):
            put_rows(g2_ref, 0, j * 2 + t, gated[:, t * 128 : t * 128 + 128])


def clean_kernel(
    scal_ref, ctx_hbm, clean_hbm, cot_hbm, up_hbm, down_hbm,
    wao_hbm, win_hbm, depth_hbm, wout_hbm,
    own_out, send_out, gm_out, go_out, sw_out, gs_out, gg2_out, g2_out, resid_out,
    ctx_in, wao_ref, win_ref, depth_ref, wout_ref,
    own_ref, send_ref, gm_ref, go_ref, sw_ref, gs_ref, gg2_ref, g2_ref, resid_ref,
    ctx_ref, x_ref, low_ref, mv_ref, sg_ref, s2_ref, zed_ref, zinv_ref, gox_ref, gsp2_ref, taps_ref,
    in_sems, out_sems,
):
    first_frame, length, core = scal_ref[0], scal_ref[1], scal_ref[2]
    half = RIM // 2
    copies = [
        pltpu.make_async_copy(source, target, in_sems.at[i])
        for i, (source, target) in enumerate((
            (ctx_hbm.at[pl.ds(0, 16)], ctx_in),
            (up_hbm.at[pl.ds(0, RIM)], x_ref.at[pl.ds(0, RIM)]),
            (clean_hbm, x_ref.at[pl.ds(RIM, ROWS)]),
            (down_hbm.at[pl.ds(0, RIM)], x_ref.at[pl.ds(RIM + ROWS, RIM)]),
            (wao_hbm, wao_ref),
            (depth_hbm, depth_ref),
            (up_hbm.at[pl.ds(RIM + half, half)], gox_ref.at[pl.ds(0, half)]),
            (cot_hbm, gox_ref.at[pl.ds(half, ROWS)]),
            (down_hbm.at[pl.ds(RIM + half, half)], gox_ref.at[pl.ds(half + ROWS, half)]),
            *(
                (win_hbm.at[:, pl.ds(at, 256)], win_ref.at[:, pl.ds(at, 256)])
                for j in range(0, WIDTH, 256)
                for at in (j, WIDTH + j)
            ),
            (wout_hbm, wout_ref),
        ))
    ]
    for copy in copies:
        copy.start()
    results = [
        pltpu.make_async_copy(source, target, out_sems.at[i])
        for i, (source, target) in enumerate((
            (own_ref, own_out), (send_ref, send_out), (gm_ref, gm_out), (go_ref, go_out),
            (sw_ref, sw_out), (gs_ref, gs_out), (gg2_ref, gg2_out), (g2_ref, g2_out),
            (resid_ref, resid_out),
        ))
    ]
    own_copy, send_copy, gm_copy, go_copy, sw_copy, gs_copy, gg2_copy, g2_copy, resid_copy = results
    copies[0].wait()
    place_context(ctx_in, 0, ctx_ref, RIM)
    for copy in copies[1:9]:
        copy.wait()
    place_taps(depth_ref, taps_ref)
    for row in range(0, INNER, 16):
        at = slice(row, row + 16)
        frame = first_frame - half + row + lax.broadcasted_iota(jnp.int32, (16, 1), 0)
        gox_ref[at, :] = (gox_ref[at, :].astype(F32) * jnp.where(frame < length, 1.0, 0.0)).astype(BF16)
    go_ref[...] = gox_ref[half : half + ROWS, :]
    go_copy.start()

    to_lowered(x_ref, ctx_ref, wao_ref, resid_ref, low_ref)
    resid_copy.start()
    frame = first_frame - RIM + lax.broadcasted_iota(jnp.int32, (CLEAN, 1), 0)
    to_gated(low_ref, win_ref, g2_ref, frame, length, (mv_ref, sg_ref), copies[9:17])
    g2_copy.start()
    forward = list(range(KERNEL))
    edge = half - KERNEL // 2
    depthwise(g2_ref, edge, taps_ref, forward, s2_ref, INNER)

    def clean_rows(i, carry):
        r = pl.multiple_of(i * 16, 16)
        centred, inverse = moments(get_rows(s2_ref, r, 16))
        zed = centred * inverse
        zed_ref[pl.ds(r, 16), :] = zed
        zinv_ref[pl.ds(r, 16), :] = jnp.broadcast_to(inverse, (16, 128))
        sw_ref[pl.ds(r, 16), :] = (zed * sigmoid(zed)).astype(BF16)
        return carry

    lax.fori_loop(0, INNER // 16, clean_rows, 0, unroll=UNROLL)
    sw_copy.start()

    for part in range(4):
        dest = part * 256
        source, row = (low_ref, RIM) if part < 2 else (sw_ref, half)
        lo = (part % 2) * 512
        first = source[row : row + ROWS, lo : lo + 256].astype(F32)
        second = source[row : row + ROWS, lo + 256 : lo + 512].astype(F32)
        own_ref[:, dest : dest + 256] = jnp.where(core == 0, first, second).astype(BF16)
        send_ref[:, dest : dest + 256] = jnp.where(core == 0, second, first).astype(BF16)
    own_copy.start()
    send_copy.start()

    copies[17].wait()
    for j in range(4):
        at = slice(j * 256, j * 256 + 256)
        gs_ref[:, at] = dot_nt(gox_ref[...], wout_ref[at, :])
    gs_copy.start()

    def back_rows(i, carry):
        r = pl.multiple_of(i * 16, 16)
        zed = zed_ref[pl.ds(r, 16), :]
        grad = gs_ref[pl.ds(r, 16), :]
        gate = sigmoid(zed)
        grad_zed = grad * (gate * (1.0 + zed * (1.0 - gate)))
        mean = jnp.mean(grad_zed, axis=-1, keepdims=True)
        along = jnp.mean(grad_zed * zed, axis=-1, keepdims=True)
        result = (grad_zed - mean - zed * along) * zinv_ref[pl.ds(r, 16), 0:1]
        for g in range(0, 16, 8):
            for t in range(8):
                gsp2_ref[pl.ds((r + g) * 8 + t, 8, stride=8), :] = result[
                    g : g + 8, t * 128 : t * 128 + 128
                ]
        return carry

    lax.fori_loop(0, INNER // 16, back_rows, 0, unroll=UNROLL)
    depthwise(gsp2_ref, edge, taps_ref, forward[::-1], gg2_ref, ROWS)
    gg2_copy.start()

    def mixed_rows(i, carry):
        r = pl.multiple_of(i * 16, 16)
        at = pl.ds(r, 16)
        frame = first_frame + r + lax.broadcasted_iota(jnp.int32, (16, 1), 0)
        grad = get_rows(gg2_ref, r, 16) * jnp.where(frame < length, 1.0, 0.0)
        gate = sg_ref[at, :]
        gm_ref[at, 0:WIDTH] = (grad * gate).astype(BF16)
        gm_ref[at, WIDTH:] = (grad * mv_ref[at, :] * gate * (1.0 - gate)).astype(BF16)
        return carry

    lax.fori_loop(0, ROWS // 16, mixed_rows, 0, unroll=UNROLL)

    gm_copy.start()
    for copy in results:
        copy.wait()


def patch_kernel(
    scal_ref, site_ref, ctx_in, patched_ref, up_ref, down_ref,
    wao_ref, win_ref, depth_ref, wout_ref,
    gm_ref, go_ref, swc_ref, gs_ref, gg2_ref, g2c_ref, residc_ref,
    attr_ref,
    ctx_ref, x_ref, resid_ref, low_ref, g2_ref, s2_ref, sw_ref, gl_ref, t0_ref, t1_ref, t2_ref, taps_ref,
):
    first_frame, length = scal_ref[0], scal_ref[1]
    half = RIM // 2
    place_context(ctx_in, 16, ctx_ref, half)
    x_ref[0:half, :] = up_ref[RIM : RIM + half, :]
    x_ref[half : half + ROWS, :] = patched_ref[...]
    x_ref[half + ROWS : PATCH, :] = down_ref[RIM : RIM + half, :]
    place_taps(depth_ref, taps_ref)
    to_lowered(x_ref, ctx_ref, wao_ref, resid_ref, low_ref)
    frame = first_frame - half + lax.broadcasted_iota(jnp.int32, (PATCH, 1), 0)
    to_gated(low_ref, win_ref, g2_ref, frame, length, None)
    depthwise(g2_ref, half - KERNEL // 2, taps_ref, list(range(KERNEL)), s2_ref, ROWS)
    sw_ref[0:ROWS, :] = swc_ref[half : half + ROWS, :]

    def patch_rows(i, carry):
        r = pl.multiple_of(i * 16, 16)
        at = pl.ds(r, 16)
        inner = pl.ds(pl.multiple_of(half + r, 16), 16)
        centred, inverse = moments(get_rows(s2_ref, r, 16))
        zed = centred * inverse
        swished = (zed * sigmoid(zed)).astype(BF16)
        sw_ref[pl.ds(pl.multiple_of(ROWS + r, 16), 16), :] = swished
        gap = swished.astype(F32) - sw_ref[at, :].astype(F32)
        t2_ref[at, :] = lane_sum(gap * gs_ref[inner, :])
        frame = first_frame + r + lax.broadcasted_iota(jnp.int32, (16, 1), 0)
        grad = get_rows(gg2_ref, r, 16) * jnp.where(frame < length, 1.0, 0.0)
        gap = get_rows(g2_ref, half + r, 16) - get_rows(g2c_ref, RIM + r, 16)
        t1_ref[at, :] = lane_sum(gap * grad)
        return carry

    lax.fori_loop(0, ROWS // 16, patch_rows, 0, unroll=UNROLL)

    t3 = jnp.zeros((ROWS, 128), F32)
    for j in range(4):
        at = slice(j * 256, j * 256 + 256)
        out = dot(sw_ref[...], wout_ref[:, at])
        out_clean = residc_ref[RIM : RIM + ROWS, at].astype(F32) + out[:ROWS]
        out_patch = resid_ref[half : half + ROWS, at].astype(F32) + out[ROWS:]
        gap = out_patch.astype(BF16).astype(F32) - out_clean.astype(BF16).astype(F32)
        t3 = t3 + lane_sum(gap * go_ref[:, at].astype(F32))
    for j in range(4):
        at = slice(j * 256, j * 256 + 256)
        gl_ref[:, at] = dot_nt(gm_ref[...], win_ref[at, :])

    def resid_rows(i, carry):
        r = pl.multiple_of(i * 16, 16)
        at = pl.ds(r, 16)
        clean = residc_ref[pl.ds(pl.multiple_of(RIM + r, 16), 16), :].astype(F32)
        patch = resid_ref[pl.ds(pl.multiple_of(half + r, 16), 16), :].astype(F32)
        centred, inverse = moments(clean)
        normed = centred * inverse
        grad = gl_ref[at, :]
        mean = jnp.mean(grad, axis=-1, keepdims=True)
        along = jnp.mean(grad * normed, axis=-1, keepdims=True)
        grad_resid = go_ref[at, :].astype(F32) + (grad - mean - normed * along) * inverse
        t0_ref[at, :] = lane_sum((patch - clean) * grad_resid)
        return carry

    lax.fori_loop(0, ROWS // 16, resid_rows, 0, unroll=UNROLL)

    columns = [
        jnp.sum(part, axis=1, keepdims=True) for part in (t0_ref[...], t1_ref[...], t2_ref[...], t3)
    ]
    lane = lane_of(ROWS)
    chosen = jnp.zeros((ROWS, 128), F32)
    for i in range(attr_ref.shape[0]):
        site = site_ref[i]
        column = columns[0]
        for k in range(1, 4):
            column = jnp.where(site == k, columns[k], column)
        chosen = jnp.where(lane == i, column, chosen)
    attr_ref[...] = chosen.T[: attr_ref.shape[0]]


def weight_kernel(
    own_hbm, other_hbm, gm_hbm, gm_other_hbm, go_hbm, go_other_hbm, out_hbm,
    left_ref, gm_ref, go_ref, out_ref, in_sems, out_sems,
):
    pairs = (
        (own_hbm, left_ref, 0), (other_hbm, left_ref, ROWS), (go_hbm, go_ref, 0),
        (go_other_hbm, go_ref, ROWS), (gm_hbm, gm_ref, 0), (gm_other_hbm, gm_ref, ROWS),
    )
    copies = [
        pltpu.make_async_copy(source, target.at[pl.ds(row, ROWS)], in_sems.at[i])
        for i, (source, target, row) in enumerate(pairs)
    ]
    for copy in copies:
        copy.start()

    def send(i):
        at = pl.ds(i * WIDTH, WIDTH)
        return pltpu.make_async_copy(out_ref.at[:, :, at], out_hbm.at[:, :, at], out_sems.at[i])

    def put(at, product):
        half = product.shape[0] // 2
        lower = product[:half].reshape(half // 8, 8, 256)
        upper = product[half:].reshape(half // 8, 8, 256)
        out_ref[:, :, at : at + 256] = jnp.concatenate([lower, upper], axis=1).astype(BF16)

    for copy in copies[:4]:
        copy.wait()
    swished = left_ref[:, 512:1024].T
    for j in range(0, WIDTH, 256):
        put(2 * WIDTH + j, dot(swished, go_ref[:, j : j + 256]))
    send(2).start()
    for copy in copies[4:]:
        copy.wait()
    low = left_ref[:, 0:512].T
    for j in range(0, 2 * WIDTH, 256):
        put(j, dot(low, gm_ref[:, j : j + 256]))
        if j + 256 == WIDTH:
            send(0).start()
    send(1).start()
    for i in range(3):
        send(i).wait()


def fold_kernel(scal_ref, pieces_ref, mine_ref, theirs_ref):
    upper = scal_ref[4]

    def columns(j, carry):
        at = pl.ds(pl.multiple_of(j * 256, 256), 256)
        total = pieces_ref[0, :, at].astype(F32)
        for k in range(1, pieces_ref.shape[0]):
            total = total + pieces_ref[k, :, at].astype(F32)
        first, second = total[:8], total[8:]
        mine_ref[:, at] = jnp.where(upper == 0, first, second)
        theirs_ref[:, at] = jnp.where(upper == 0, second, first)
        return carry

    lax.fori_loop(0, mine_ref.shape[1] // 256, columns, 0, unroll=2)


def join_kernel(mine_ref, theirs_ref, in_ref, out_ref):
    whole = mine_ref[...] + theirs_ref[...]
    in_ref[...] = whole[:, : 2 * WIDTH]
    out_ref[...] = whole[:, 2 * WIDTH :]


VMEM = pl.BlockSpec(memory_space=pltpu.VMEM)
SMEM = pl.BlockSpec(memory_space=pltpu.SMEM)
HBM = pl.BlockSpec(memory_space=pltpu.HBM)


def kernel_call(body, out_shape, in_specs, scratch, limit, flops, moved, out_spec=VMEM):
    return pl.pallas_call(
        body,
        out_shape=out_shape,
        in_specs=in_specs,
        out_specs=[out_spec] * len(out_shape),
        scratch_shapes=scratch,
        compiler_params=pltpu.CompilerParams(vmem_limit_bytes=limit << 20),
        cost_estimate=pl.CostEstimate(flops=flops, bytes_accessed=moved, transcendentals=0),
    )


def shape(dims, dtype):
    return jax.ShapeDtypeStruct(dims, dtype)


def per_device(
    clean_input, corrupt_input, patch_mask, lengths, site_ids, w_query, w_key, w_value,
    w_attn_out, w_pointwise_in, depth_kernel, w_pointwise_out, cotangent,
):
    frames = lax.axis_size("frames")
    position = lax.axis_index("frames")
    core = lax.rem(lax.axis_index("dp"), 2)
    scalars = jnp.stack(
        [position * ROWS, lengths[0], core, lax.rem(position, 2), lax.axis_index("dp") // 2]
    ).astype(jnp.int32)
    clean, corrupt, cot = clean_input[0], corrupt_input[0], cotangent[0]

    msg, patched, up, down = kernel_call(
        project_kernel,
        [shape((frames, ROWS, 128), BF16), shape((ROWS, WIDTH), BF16),
         shape((2 * RIM, WIDTH), BF16), shape((2 * RIM, WIDTH), BF16)],
        [HBM] * 3 + [VMEM] + [HBM] * 3,
        [pltpu.VMEM((2 * ROWS, WIDTH), BF16), pltpu.VMEM((ROWS, ROWS), F32),
         pltpu.VMEM((ROWS, WIDTH), BF16), pltpu.VMEM((ROWS, WIDTH), BF16),
         pltpu.VMEM((WIDTH, 512), BF16), pltpu.VMEM((WIDTH, 512), BF16),
         pltpu.VMEM((WIDTH, 512), BF16), pltpu.SemaphoreType.DMA((7,))],
        62, 8 * 10**8, 6 * 10**6,
    )(clean, corrupt, cot, patch_mask, w_query, w_key, w_value)
    forward = [(i, i + 1) for i in range(frames - 1)]
    backward = [(i + 1, i) for i in range(frames - 1)]
    from_left = lax.ppermute(up, "frames", forward)
    from_right = lax.ppermute(down, "frames", backward)
    recv = lax.all_to_all(msg, "frames", 0, 0, tiled=True)
    recv, from_left, from_right = lax.optimization_barrier((recv, from_left, from_right))
    keys = frames * ROWS // 2
    (context,) = kernel_call(
        attend_kernel,
        [shape((frames, 112, 128), BF16)],
        [SMEM, VMEM],
        [pltpu.VMEM((keys, 128), BF16), pltpu.VMEM((128, keys), BF16),
         pltpu.VMEM((128, 2 * keys), BF16),
         pltpu.VMEM((keys, 512), F32), pltpu.VMEM((keys, 512), F32),
         pltpu.VMEM((frames * 64, 128), F32), pltpu.VMEM((frames * 8, 128), F32)],
        20, 8 * 10**9, 10**6,
    )(scalars, recv)
    contexts = lax.all_to_all(context, "frames", 0, 0, tiled=True)
    own, send, grad_mixed, grad_output, swished, grad_swished, grad_gated, gated, resid = kernel_call(
        clean_kernel,
        [shape((ROWS, 1024), BF16), shape((ROWS, 1024), BF16), shape((ROWS, 2 * WIDTH), BF16),
         shape((ROWS, WIDTH), BF16), shape((INNER, WIDTH), BF16), shape((INNER, WIDTH), F32),
         shape((ROWS * 8, 128), F32), shape((CLEAN * 8, 128), F32), shape((CLEAN, WIDTH), BF16)],
        [SMEM] + [HBM] * 9,
        [pltpu.VMEM((16, 112, 128), BF16), pltpu.VMEM((512, WIDTH), BF16),
         pltpu.VMEM((WIDTH, 2 * WIDTH), BF16), pltpu.VMEM((KERNEL, WIDTH), BF16),
         pltpu.VMEM((WIDTH, WIDTH), BF16),
         pltpu.VMEM((ROWS, 1024), BF16), pltpu.VMEM((ROWS, 1024), BF16),
         pltpu.VMEM((ROWS, 2 * WIDTH), BF16), pltpu.VMEM((ROWS, WIDTH), BF16),
         pltpu.VMEM((INNER, WIDTH), BF16), pltpu.VMEM((INNER, WIDTH), F32),
         pltpu.VMEM((ROWS * 8, 128), F32), pltpu.VMEM((CLEAN * 8, 128), F32),
         pltpu.VMEM((CLEAN, WIDTH), BF16),
         pltpu.VMEM((CLEAN, 512), BF16), pltpu.VMEM((CLEAN, WIDTH), BF16),
         pltpu.VMEM((CLEAN, WIDTH), BF16),
         pltpu.VMEM((ROWS, WIDTH), F32), pltpu.VMEM((ROWS, WIDTH), F32),
         pltpu.VMEM((INNER * 8, 128), F32), pltpu.VMEM((INNER, WIDTH), F32),
         pltpu.VMEM((INNER, 128), F32), pltpu.VMEM((INNER, WIDTH), BF16),
         pltpu.VMEM((INNER * 8, 128), F32), pltpu.VMEM((32 * 8, 128), F32),
         pltpu.SemaphoreType.DMA((18,)), pltpu.SemaphoreType.DMA((9,))],
        59, 3 * 10**9, 10**7, HBM,
    )(scalars, contexts, clean, cot, from_left, from_right,
      w_attn_out, w_pointwise_in, depth_kernel, w_pointwise_out)

    cores = [(i, i ^ 1) for i in range(lax.axis_size("dp"))]
    other, gm_other, go_other = (
        lax.ppermute(part, "dp", cores) for part in (send, grad_mixed, grad_output)
    )
    (partial,) = kernel_call(
        weight_kernel,
        [shape((frames, 16, 3 * WIDTH), BF16)],
        [HBM] * 6,
        [pltpu.VMEM((2 * ROWS, WIDTH), BF16), pltpu.VMEM((2 * ROWS, 2 * WIDTH), BF16),
         pltpu.VMEM((2 * ROWS, WIDTH), BF16), pltpu.VMEM((frames, 16, 3 * WIDTH), BF16),
         pltpu.SemaphoreType.DMA((6,)), pltpu.SemaphoreType.DMA((3,))],
        59, 8 * 10**8, 10**7, HBM,
    )(own, other, grad_mixed, gm_other, grad_output, go_other)
    pieces = lax.all_to_all(partial, "frames", 0, 0, tiled=True)
    (attribution,) = kernel_call(
        patch_kernel,
        [shape((site_ids.shape[0], ROWS), F32)],
        [SMEM, SMEM] + [VMEM] * 15,
        [pltpu.VMEM((PATCH, 512), BF16), pltpu.VMEM((PATCH, WIDTH), BF16),
         pltpu.VMEM((PATCH, WIDTH), BF16), pltpu.VMEM((PATCH, WIDTH), BF16),
         pltpu.VMEM((PATCH * 8, 128), F32), pltpu.VMEM((ROWS * 8, 128), F32),
         pltpu.VMEM((2 * ROWS, WIDTH), BF16), pltpu.VMEM((ROWS, WIDTH), F32),
         pltpu.VMEM((ROWS, 128), F32), pltpu.VMEM((ROWS, 128), F32), pltpu.VMEM((ROWS, 128), F32),
         pltpu.VMEM((32 * 8, 128), F32)],
        28, 3 * 10**9, 10**7,
    )(scalars, site_ids, contexts, patched, from_left, from_right,
      w_attn_out, w_pointwise_in, depth_kernel, w_pointwise_out,
      grad_mixed, grad_output, swished, grad_swished, grad_gated, gated, resid)
    pieces, attribution = lax.optimization_barrier((pieces, attribution))
    mine, theirs = kernel_call(
        fold_kernel,
        [shape((8, 3 * WIDTH), F32), shape((8, 3 * WIDTH), F32)],
        [SMEM, VMEM],
        [],
        16, 10**8, 3 * 10**6,
    )(scalars, pieces)
    half_dp = lax.axis_size("dp") // 2
    theirs = lax.ppermute(theirs, "dp", [(i, i ^ half_dp) for i in range(2 * half_dp)])
    grad_in, grad_out = kernel_call(
        join_kernel,
        [shape((8, 2 * WIDTH), F32), shape((8, WIDTH), F32)],
        [VMEM] * 2,
        [],
        16, 10**6, 10**6,
    )(mine, theirs)
    return attribution[None], grad_in, grad_out


def solution(mesh):
    placed = (
        P("dp", "frames", None), P("dp", "frames", None), P("dp", "frames"), P("dp"), P(), P(), P(),
        P(), P(), P(), P(), P(), P("dp", "frames", None),
    )
    return jax.shard_map(
        per_device,
        mesh=mesh,
        in_specs=placed,
        out_specs=(P("dp", None, "frames"), P(("dp", "frames"), None), P(("dp", "frames"), None)),
        check_vma=False,
    )
```

```python
import jax
import jax.numpy as jnp
from jax import lax
from jax.experimental import pallas as pl
from jax.experimental.pallas import tpu as pltpu
from jax.sharding import PartitionSpec as P

HEADS = 8
DH = 64
KERNEL = 31
RIM = 32
EPSILON = 1e-05
FLOOR = -1e30
LOG2E = 1.4426950408889634
F32 = jnp.float32
BF16 = jnp.bfloat16
ROWS = 128
WIDTH = 1024
CLEAN = ROWS + 2 * RIM
PATCH = ROWS + RIM
BOTH = CLEAN + PATCH
INNER = ROWS + RIM
GM = WIDTH
GO = 3 * WIDTH
UNROLL = True
TAP_UNROLL = 4
LOAD_UNROLL = 4
PACK_UNROLL = 4
CHUNK = 256


def lane_of(rows):
    return lax.broadcasted_iota(jnp.int32, (rows, 128), 1)


def swap(tile):
    return pltpu.roll(tile, 64, 1)


def moments(values):
    mean = jnp.mean(values, axis=-1, keepdims=True)
    centred = values - mean
    variance = jnp.mean(centred * centred, axis=-1, keepdims=True)
    return centred, lax.rsqrt(variance + EPSILON)


def dot(left, right):
    return jnp.dot(left, right, preferred_element_type=F32)


def dot_nt(left, right):
    return lax.dot_general(left, right, (((1,), (1,)), ((), ())), preferred_element_type=F32)


def dot_tn(left, right):
    return lax.dot_general(left, right, (((0,), (0,)), ((), ())), preferred_element_type=F32)


def sigmoid(values):
    return 1.0 / (1.0 + jnp.exp(-values))


def lane_sum(values):
    total = values[:, :128]
    for start in range(128, values.shape[1], 128):
        total = total + values[:, start : start + 128]
    return total


def project_kernel(
    clean_hbm, corrupt_hbm, cot_hbm, mask_ref, wq_hbm, wk_hbm, wv_hbm,
    msg_ref, patched_ref, up_ref, down_ref,
    hidden_ref, mask_col, clean_ref, corrupt_ref, wq_ref, wk_ref, wv_ref, sems,
):
    half = RIM // 2
    copies = [
        pltpu.make_async_copy(source, target, sems.at[i])
        for i, (source, target) in enumerate((
            (clean_hbm, clean_ref),
            (corrupt_hbm, corrupt_ref),
            (wk_hbm, wk_ref),
            (wv_hbm, wv_ref),
            (wq_hbm, wq_ref),
            (cot_hbm.at[pl.ds(ROWS - half, half)], up_ref.at[pl.ds(RIM + half, half)]),
            (cot_hbm.at[pl.ds(0, half)], down_ref.at[pl.ds(RIM + half, half)]),
        ))
    ]
    for copy in copies:
        copy.start()
    spread_mask = jnp.broadcast_to(mask_ref[...].astype(F32), (ROWS, ROWS))
    mask_col[...] = spread_mask.T
    copies[0].wait()
    copies[1].wait()

    def rows(i, carry):
        at = pl.ds(pl.multiple_of(i * 16, 16), 16)
        below = pl.ds(pl.multiple_of(ROWS + i * 16, 16), 16)
        clean = clean_ref[at, :].astype(F32)
        corrupt = corrupt_ref[at, :].astype(F32)
        patched = jnp.where(mask_col[at, 0:1] == 1.0, corrupt, clean)
        patched_ref[at, :] = patched.astype(BF16)
        for dest, source in ((at, clean), (below, patched)):
            centred, inverse = moments(source)
            hidden_ref[dest, :] = (centred * inverse).astype(BF16)
        return carry

    lax.fori_loop(0, ROWS // 16, rows, 0, unroll=UNROLL)
    up_ref[0:RIM, :] = clean_ref[ROWS - RIM : ROWS, :]
    up_ref[RIM : RIM + half, :] = patched_ref[ROWS - half : ROWS, :]
    down_ref[0:RIM, :] = clean_ref[0:RIM, :]
    down_ref[RIM : RIM + half, :] = patched_ref[0:half, :]
    for copy in copies[2:]:
        copy.wait()

    low = lane_of(ROWS) < 64
    low_q = lane_of(64) < 64
    for pair in range(2):
        cols = slice(pair * 256, pair * 256 + 256)
        hidden = hidden_ref[...]
        query = dot(hidden, wq_ref[:, cols])
        keys = dot(hidden, wk_ref[:, cols])
        values = dot(hidden, wv_ref[:, cols])
        for sub in range(2):
            tile = slice(sub * 128, sub * 128 + 128)
            for run in range(2):
                part = slice(run * ROWS, run * ROWS + ROWS)
                k, v, q = keys[part, tile], values[part, tile], query[part, tile]
                base = run * 16 + (pair * 2 + sub) * 4
                kv = (jnp.where(low, k, swap(v)).astype(BF16), jnp.where(low, swap(k), v).astype(BF16))
                early, late = q[:64], q[64:]
                asked = (
                    jnp.where(low_q, early, swap(late)).astype(BF16),
                    jnp.where(low_q, swap(early), late).astype(BF16),
                )
                for odd in range(2):
                    for side in range(2):
                        dest = base + odd * 2 + side
                        msg_ref[dest, 0:64, :] = kv[odd][side * 64 : side * 64 + 64]
                        msg_ref[dest, 64:128, :] = asked[odd]


def attend_kernel(
    scal_ref, recv_ref, out_ref, k_ref, vt_ref, qt_ref, s0_ref, s1_ref, c_ref, r_ref
):
    length, side = scal_ref[1], scal_ref[3]
    sources = recv_ref.shape[0]
    lane = lane_of(128)
    row = lax.broadcasted_iota(jnp.int32, (128, 128), 0)
    scale = DH ** (-0.5) * LOG2E

    def load(s, carry):
        at = pl.multiple_of(s * 128, 128)
        kv = recv_ref[pl.ds(2 * s, 2), 0:64, :].astype(F32).reshape(128, 128)
        frame = (2 * s + row // 64) * ROWS + side * 64 + row % 64
        bias = jnp.where(frame < length, 0.0, FLOOR)
        keyed = jnp.where(lane < 64, kv, jnp.where(lane == 64, bias, 0.0))
        k_ref[pl.ds(at, 128), :] = keyed.astype(BF16)
        vt_ref[0:64, pl.ds(at, 128)] = kv.T[64:128].astype(BF16)
        vt_ref[64:80, pl.ds(at, 128)] = jnp.ones((16, 128), BF16)
        raw = recv_ref[pl.ds(2 * s, 2), 64:128, :].astype(F32).reshape(128, 128).T
        fill = jnp.where(row == 64, 1.0, 0.0)
        other = jnp.concatenate([raw[64:], raw[:64]], axis=0)
        at = pl.multiple_of(s * 256, 256)
        qt_ref[:, pl.ds(at, 128)] = jnp.where(row < 64, raw, fill).astype(BF16)
        qt_ref[:, pl.ds(at + 128, 128)] = jnp.where(row < 64, other, fill).astype(BF16)
        return carry

    lax.fori_loop(0, sources // 2, load, 0, unroll=LOAD_UNROLL)

    many = s0_ref.shape[1]
    chunk = CHUNK
    pieces = k_ref.shape[0] // chunk
    blocks = sources * ROWS // many

    def score_piece(query, s_ref, k, top):
        at = slice(k * chunk, k * chunk + chunk)
        scores = dot(k_ref[at, :], query)
        s_ref[at, :] = scores
        best = jnp.max(scores.reshape(chunk // 8, 8, many), axis=0)
        return best if top is None else jnp.maximum(top, best)

    def weigh_piece(s_ref, best, k, accum):
        at = slice(k * chunk, k * chunk + chunk)
        weights = jnp.exp2((s_ref[at, :] - best) * scale).astype(BF16)
        addend = dot(vt_ref[:, at], weights)
        return addend if accum is None else accum + addend

    def finish(top):
        return jnp.max(top, axis=0, keepdims=True)

    def queries(b):
        return qt_ref[:, pl.ds(pl.multiple_of(b * many, many), many)]

    low8 = lane_of(8) < 64

    def store(b, accum, best):
        total = accum[64:65, :]
        result = accum[0:64, :] / total
        level = jnp.broadcast_to(best * scale + jnp.log2(total), (8, many))
        for g in range(many // 256):
            first = slice(g * 256, g * 256 + 128)
            second = slice(g * 256 + 128, g * 256 + 256)
            both = jnp.concatenate([result[:, first], result[:, second]], axis=0)
            at = b * (many // 256) + g
            c_ref[pl.ds(pl.multiple_of(at * 128, 128), 128), :] = both.T
            early, late = level[:, first], level[:, second]
            r_ref[pl.ds(pl.multiple_of(at * 16, 16), 8), :] = jnp.where(low8, early, swap(late))
            r_ref[pl.ds(pl.multiple_of(at * 16 + 8, 8), 8), :] = jnp.where(low8, swap(early), late)

    def step(b, s_ref, best, next_b, next_s):
        query = None if next_s is None else queries(next_b)
        top, accum = None, None
        for k in range(pieces):
            if query is not None:
                top = score_piece(query, next_s, k, top)
            accum = weigh_piece(s_ref, best, k, accum)
        store(b, accum, best)
        return None if query is None else finish(top)

    query, top = queries(0), None
    for k in range(pieces):
        top = score_piece(query, s0_ref, k, top)

    def pair(i, best):
        best = step(2 * i, s0_ref, best, 2 * i + 1, s1_ref)
        return step(2 * i + 1, s1_ref, best, 2 * i + 2, s0_ref)

    best = lax.fori_loop(0, blocks // 2 - 1, pair, finish(top))
    best = step(blocks - 2, s0_ref, best, blocks - 1, s1_ref)
    step(blocks - 1, s1_ref, best, None, None)

    low32 = lane_of(32) < 64
    row8 = lax.broadcasted_iota(jnp.int32, (8, 128), 0)

    def pack(d, carry):
        after = lax.rem(d + 1, sources)
        before = lax.rem(d + sources - 1, sources)
        out_ref[d, 0:64, :] = c_ref[pl.ds(pl.multiple_of(d * 64, 64), 64), :].astype(BF16)
        right = c_ref[pl.ds(pl.multiple_of(after * 64, 64), 32), :]
        left = c_ref[pl.ds(pl.multiple_of(before * 64 + 32, 32), 32), :]
        out_ref[d, 64:96, :] = jnp.where(low32, right, left).astype(BF16)
        own = r_ref[pl.ds(pl.multiple_of(d * 8, 8), 8), :]
        rim = jnp.where(
            low8,
            r_ref[pl.ds(pl.multiple_of(after * 8, 8), 8), :],
            r_ref[pl.ds(pl.multiple_of(before * 8, 8), 8), :],
        )
        rows = jnp.where(row8 < 3, own, rim)
        high = rows.astype(BF16).astype(F32)
        rest = rows - high
        middle = rest.astype(BF16).astype(F32)
        last = rest - middle
        level = row8 % 3
        rows = jnp.where(level == 0, high, jnp.where(level == 1, middle, last))
        out_ref[d, 96:112, :] = jnp.concatenate([rows, rows], axis=0).astype(BF16)
        return carry

    lax.fori_loop(0, sources, pack, 0, unroll=PACK_UNROLL)


def depthwise(source, source_row, taps_ref, order, target, count):
    def rows(i, carry):
        first = source_row + i * 8
        taps = [taps_ref[t * 8 : t * 8 + 8, :] for t in order]
        sums = [None] * 8
        for s in range(KERNEL + 7):
            piece = source[pl.ds(pl.multiple_of((first + s) * 8, 8), 8), :]
            for o in range(8):
                if 0 <= s - o < KERNEL:
                    term = taps[s - o] * piece
                    sums[o] = term if sums[o] is None else sums[o] + term
        for o in range(8):
            target[pl.ds(pl.multiple_of((i * 8 + o) * 8, 8), 8), :] = sums[o]
        return carry

    lax.fori_loop(0, count // 8, rows, 0, unroll=TAP_UNROLL)


def put_rows(ref, row, tile, values):
    for r in range(0, values.shape[0], 8):
        ref[pl.ds((row + r) * 8 + tile, 8, stride=8), :] = values[r : r + 8]


def get_rows(ref, row, count):
    groups = []
    for r in range(0, count, 8):
        tiles = [ref[pl.ds((row + r) * 8 + t, 8, stride=8), :] for t in range(8)]
        groups.append(jnp.concatenate(tiles, axis=1))
    return jnp.concatenate(groups, axis=0) if len(groups) > 1 else groups[0]


def place_context(ctx_in, base, ctx_ref, rim):
    row8 = lax.broadcasted_iota(jnp.int32, (8, 128), 0)
    zero = jnp.zeros((8, 128), F32)
    levels = [[zero, zero], [zero, zero]]
    for h in range(HEADS):
        for side in range(2):
            block = ctx_in[base + h * 2 + side, 96:112, :].astype(F32)
            for kind in range(2):
                at = kind * 3
                level = block[at : at + 1] + block[at + 1 : at + 2] + block[at + 2 : at + 3]
                levels[kind][side] = jnp.where(row8 == h, level, levels[kind][side])
    shares = []
    for first, second in levels:
        shares.append(1.0 / (1.0 + jnp.exp2(second - first)))
        shares.append(1.0 / (1.0 + jnp.exp2(first - second)))
    share = jnp.concatenate(shares + [jnp.zeros((96, 128), F32)], axis=0).T
    low = lane_of(96) < 64
    low_rows = lane_of(ROWS) < 64
    for t in range(HEADS // 2):
        at = slice(t * 128, t * 128 + 128)
        own = left = right = None
        for side in range(2):
            even = ctx_in[base + t * 4 + side, 0:96, :].astype(F32)
            odd = ctx_in[base + t * 4 + 2 + side, 0:96, :].astype(F32)
            first = jnp.where(low, even, swap(odd))
            second = jnp.where(low, swap(even), odd)
            scale = []
            for kind in range(2):
                column = kind * 16 + side * 8 + 2 * t
                scale.append(jnp.where(
                    low_rows, share[:, column : column + 1], share[:, column + 1 : column + 2]
                ))
            part = jnp.concatenate([first[:64], second[:64]], axis=0) * scale[0]
            after = first[64:96] * scale[1][0:32]
            before = second[64:96] * scale[1][96:128]
            own = part if own is None else own + part
            left = before if left is None else left + before
            right = after if right is None else right + after
        ctx_ref[0:rim, at] = left[RIM - rim :].astype(BF16)
        ctx_ref[rim : rim + ROWS, at] = own.astype(BF16)
        ctx_ref[rim + ROWS :, at] = right[:rim].astype(BF16)


def place_taps(depth_ref, taps_ref):
    for r in range(0, KERNEL + 1, 8):
        got = min(8, KERNEL - r)
        block = depth_ref[r : r + got, :].astype(F32)
        if got < 8:
            block = jnp.concatenate([block, jnp.zeros((8 - got, WIDTH), F32)], axis=0)
        for t in range(8):
            put_rows(taps_ref, r, t, block[:, t * 128 : t * 128 + 128])


def to_lowered(x_ref, ctx_ref, wao_ref, resid_ref, low_ref):
    for j in range(4):
        at = slice(j * 256, j * 256 + 256)
        joined = x_ref[:, at].astype(F32) + dot(ctx_ref[...], wao_ref[:, at])
        resid_ref[:, at] = joined.astype(BF16)

    def lower(i, carry):
        at = pl.ds(pl.multiple_of(i * 16, 16), 16)
        centred, inverse = moments(resid_ref[at, :].astype(F32))
        low_ref[at, :] = (centred * inverse).astype(BF16)
        return carry

    lax.fori_loop(0, x_ref.shape[0] // 16, lower, 0, unroll=UNROLL)


def to_gated(low_ref, win_ref, g2_ref, frame, length, keep, arrivals=None):
    live = jnp.where((frame >= 0) & (frame < length), 1.0, 0.0)
    for j in range(4):
        at = slice(j * 256, j * 256 + 256)
        gate_at = slice(WIDTH + j * 256, WIDTH + j * 256 + 256)
        if arrivals is not None:
            arrivals[2 * j].wait()
            arrivals[2 * j + 1].wait()
        value = dot(low_ref[...], win_ref[:, at])
        gate = sigmoid(dot(low_ref[...], win_ref[:, gate_at]))
        if keep is not None:
            mv_ref, sg_ref = keep
            mv_ref[:, at] = value[RIM : RIM + ROWS]
            sg_ref[:, at] = gate[RIM : RIM + ROWS]
        gated = (value * gate * live).astype(BF16).astype(F32)
        for t in range(2):
            put_rows(g2_ref, 0, j * 2 + t, gated[:, t * 128 : t * 128 + 128])


def clean_kernel(
    scal_ref, ctx_hbm, clean_hbm, cot_hbm, up_hbm, down_hbm,
    wao_hbm, win_hbm, depth_hbm, wout_hbm,
    own_out, pack_out, sw_out, gs_out, gg2_out, g2_out, resid_out,
    ctx_in, wao_ref, win_ref, depth_ref, wout_ref,
    own_ref, pack_ref, sw_ref, gs_ref, gg2_ref, g2_ref, resid_ref,
    ctx_ref, x_ref, low_ref, mv_ref, sg_ref, s2_ref, zed_ref, zinv_ref, gox_ref, gsp2_ref, taps_ref,
    in_sems, out_sems,
):
    first_frame, length, core = scal_ref[0], scal_ref[1], scal_ref[2]
    half = RIM // 2
    copies = [
        pltpu.make_async_copy(source, target, in_sems.at[i])
        for i, (source, target) in enumerate((
            (ctx_hbm.at[pl.ds(0, 16)], ctx_in),
            (up_hbm.at[pl.ds(0, RIM)], x_ref.at[pl.ds(0, RIM)]),
            (clean_hbm, x_ref.at[pl.ds(RIM, ROWS)]),
            (down_hbm.at[pl.ds(0, RIM)], x_ref.at[pl.ds(RIM + ROWS, RIM)]),
            (wao_hbm, wao_ref),
            (depth_hbm, depth_ref),
            (up_hbm.at[pl.ds(RIM + half, half)], gox_ref.at[pl.ds(0, half)]),
            (cot_hbm, gox_ref.at[pl.ds(half, ROWS)]),
            (down_hbm.at[pl.ds(RIM + half, half)], gox_ref.at[pl.ds(half + ROWS, half)]),
            *(
                (win_hbm.at[:, pl.ds(at, 256)], win_ref.at[:, pl.ds(at, 256)])
                for j in range(0, WIDTH, 256)
                for at in (j, WIDTH + j)
            ),
            (wout_hbm, wout_ref),
        ))
    ]
    for copy in copies:
        copy.start()
    results = [
        pltpu.make_async_copy(source, target, out_sems.at[i])
        for i, (source, target) in enumerate((
            (own_ref, own_out),
            *(
                (pack_ref.at[:, pl.ds(at, size)], pack_out.at[:, pl.ds(at, size)])
                for at, size in ((0, WIDTH), (GM, 2 * WIDTH), (GO, WIDTH))
            ),
            (sw_ref, sw_out), (gs_ref, gs_out), (gg2_ref, gg2_out), (g2_ref, g2_out),
            (resid_ref, resid_out),
        ))
    ]
    own_copy, send_copy, gm_copy, go_copy, sw_copy, gs_copy, gg2_copy, g2_copy, resid_copy = results
    copies[0].wait()
    place_context(ctx_in, 0, ctx_ref, RIM)
    for copy in copies[1:9]:
        copy.wait()
    place_taps(depth_ref, taps_ref)
    for row in range(0, INNER, 16):
        at = slice(row, row + 16)
        frame = first_frame - half + row + lax.broadcasted_iota(jnp.int32, (16, 1), 0)
        gox_ref[at, :] = (gox_ref[at, :].astype(F32) * jnp.where(frame < length, 1.0, 0.0)).astype(BF16)
    pack_ref[:, GO:] = gox_ref[half : half + ROWS, :]
    go_copy.start()

    to_lowered(x_ref, ctx_ref, wao_ref, resid_ref, low_ref)
    resid_copy.start()
    frame = first_frame - RIM + lax.broadcasted_iota(jnp.int32, (CLEAN, 1), 0)
    to_gated(low_ref, win_ref, g2_ref, frame, length, (mv_ref, sg_ref), copies[9:17])
    g2_copy.start()
    forward = list(range(KERNEL))
    edge = half - KERNEL // 2
    depthwise(g2_ref, edge, taps_ref, forward, s2_ref, INNER)

    def clean_rows(i, carry):
        r = pl.multiple_of(i * 16, 16)
        centred, inverse = moments(get_rows(s2_ref, r, 16))
        zed = centred * inverse
        zed_ref[pl.ds(r, 16), :] = zed
        zinv_ref[pl.ds(r, 16), :] = jnp.broadcast_to(inverse, (16, 128))
        sw_ref[pl.ds(r, 16), :] = (zed * sigmoid(zed)).astype(BF16)
        return carry

    lax.fori_loop(0, INNER // 16, clean_rows, 0, unroll=UNROLL)
    sw_copy.start()

    for part in range(4):
        dest = part * 256
        source, row = (low_ref, RIM) if part < 2 else (sw_ref, half)
        lo = (part % 2) * 512
        first = source[row : row + ROWS, lo : lo + 256].astype(F32)
        second = source[row : row + ROWS, lo + 256 : lo + 512].astype(F32)
        own_ref[:, dest : dest + 256] = jnp.where(core == 0, first, second).astype(BF16)
        pack_ref[:, dest : dest + 256] = jnp.where(core == 0, second, first).astype(BF16)
    own_copy.start()
    send_copy.start()

    copies[17].wait()
    for j in range(4):
        at = slice(j * 256, j * 256 + 256)
        gs_ref[:, at] = dot_nt(gox_ref[...], wout_ref[at, :])
    gs_copy.start()

    def back_rows(i, carry):
        r = pl.multiple_of(i * 16, 16)
        zed = zed_ref[pl.ds(r, 16), :]
        grad = gs_ref[pl.ds(r, 16), :]
        gate = sigmoid(zed)
        grad_zed = grad * (gate * (1.0 + zed * (1.0 - gate)))
        mean = jnp.mean(grad_zed, axis=-1, keepdims=True)
        along = jnp.mean(grad_zed * zed, axis=-1, keepdims=True)
        result = (grad_zed - mean - zed * along) * zinv_ref[pl.ds(r, 16), 0:1]
        for g in range(0, 16, 8):
            for t in range(8):
                gsp2_ref[pl.ds((r + g) * 8 + t, 8, stride=8), :] = result[
                    g : g + 8, t * 128 : t * 128 + 128
                ]
        return carry

    lax.fori_loop(0, INNER // 16, back_rows, 0, unroll=UNROLL)
    depthwise(gsp2_ref, edge, taps_ref, forward[::-1], gg2_ref, ROWS)
    gg2_copy.start()

    def mixed_rows(i, carry):
        r = pl.multiple_of(i * 16, 16)
        at = pl.ds(r, 16)
        frame = first_frame + r + lax.broadcasted_iota(jnp.int32, (16, 1), 0)
        grad = get_rows(gg2_ref, r, 16) * jnp.where(frame < length, 1.0, 0.0)
        gate = sg_ref[at, :]
        pack_ref[at, GM : GM + WIDTH] = (grad * gate).astype(BF16)
        pack_ref[at, GM + WIDTH : GO] = (grad * mv_ref[at, :] * gate * (1.0 - gate)).astype(BF16)
        return carry

    lax.fori_loop(0, ROWS // 16, mixed_rows, 0, unroll=UNROLL)

    gm_copy.start()
    for copy in results:
        copy.wait()


def patch_kernel(
    scal_ref, site_ref, ctx_in, patched_ref, up_ref, down_ref,
    wao_ref, win_ref, depth_ref, wout_ref,
    pack_ref, swc_ref, gs_ref, gg2_ref, g2c_ref, residc_ref,
    attr_ref,
    ctx_ref, x_ref, resid_ref, low_ref, g2_ref, s2_ref, sw_ref, gl_ref, t0_ref, t1_ref, t2_ref, taps_ref,
):
    first_frame, length = scal_ref[0], scal_ref[1]
    half = RIM // 2
    place_context(ctx_in, 16, ctx_ref, half)
    x_ref[0:half, :] = up_ref[RIM : RIM + half, :]
    x_ref[half : half + ROWS, :] = patched_ref[...]
    x_ref[half + ROWS : PATCH, :] = down_ref[RIM : RIM + half, :]
    place_taps(depth_ref, taps_ref)
    to_lowered(x_ref, ctx_ref, wao_ref, resid_ref, low_ref)
    frame = first_frame - half + lax.broadcasted_iota(jnp.int32, (PATCH, 1), 0)
    to_gated(low_ref, win_ref, g2_ref, frame, length, None)
    depthwise(g2_ref, half - KERNEL // 2, taps_ref, list(range(KERNEL)), s2_ref, ROWS)
    sw_ref[0:ROWS, :] = swc_ref[half : half + ROWS, :]

    def patch_rows(i, carry):
        r = pl.multiple_of(i * 16, 16)
        at = pl.ds(r, 16)
        inner = pl.ds(pl.multiple_of(half + r, 16), 16)
        centred, inverse = moments(get_rows(s2_ref, r, 16))
        zed = centred * inverse
        swished = (zed * sigmoid(zed)).astype(BF16)
        sw_ref[pl.ds(pl.multiple_of(ROWS + r, 16), 16), :] = swished
        gap = swished.astype(F32) - sw_ref[at, :].astype(F32)
        t2_ref[at, :] = lane_sum(gap * gs_ref[inner, :])
        frame = first_frame + r + lax.broadcasted_iota(jnp.int32, (16, 1), 0)
        grad = get_rows(gg2_ref, r, 16) * jnp.where(frame < length, 1.0, 0.0)
        gap = get_rows(g2_ref, half + r, 16) - get_rows(g2c_ref, RIM + r, 16)
        t1_ref[at, :] = lane_sum(gap * grad)
        return carry

    lax.fori_loop(0, ROWS // 16, patch_rows, 0, unroll=UNROLL)

    t3 = jnp.zeros((ROWS, 128), F32)
    for j in range(4):
        at = slice(j * 256, j * 256 + 256)
        out = dot(sw_ref[...], wout_ref[:, at])
        out_clean = residc_ref[RIM : RIM + ROWS, at].astype(F32) + out[:ROWS]
        out_patch = resid_ref[half : half + ROWS, at].astype(F32) + out[ROWS:]
        gap = out_patch.astype(BF16).astype(F32) - out_clean.astype(BF16).astype(F32)
        t3 = t3 + lane_sum(gap * pack_ref[:, GO + j * 256 : GO + j * 256 + 256].astype(F32))
    for j in range(4):
        at = slice(j * 256, j * 256 + 256)
        gl_ref[:, at] = dot_nt(pack_ref[:, GM:GO], win_ref[at, :])

    def resid_rows(i, carry):
        r = pl.multiple_of(i * 16, 16)
        at = pl.ds(r, 16)
        clean = residc_ref[pl.ds(pl.multiple_of(RIM + r, 16), 16), :].astype(F32)
        patch = resid_ref[pl.ds(pl.multiple_of(half + r, 16), 16), :].astype(F32)
        centred, inverse = moments(clean)
        normed = centred * inverse
        grad = gl_ref[at, :]
        mean = jnp.mean(grad, axis=-1, keepdims=True)
        along = jnp.mean(grad * normed, axis=-1, keepdims=True)
        grad_resid = pack_ref[at, GO:].astype(F32) + (grad - mean - normed * along) * inverse
        t0_ref[at, :] = lane_sum((patch - clean) * grad_resid)
        return carry

    lax.fori_loop(0, ROWS // 16, resid_rows, 0, unroll=UNROLL)

    columns = [
        jnp.sum(part, axis=1, keepdims=True) for part in (t0_ref[...], t1_ref[...], t2_ref[...], t3)
    ]
    lane = lane_of(ROWS)
    chosen = jnp.zeros((ROWS, 128), F32)
    for i in range(attr_ref.shape[0]):
        site = site_ref[i]
        column = columns[0]
        for k in range(1, 4):
            column = jnp.where(site == k, columns[k], column)
        chosen = jnp.where(lane == i, column, chosen)
    attr_ref[...] = chosen.T[: attr_ref.shape[0]]


def weight_kernel(
    own_hbm, pack_hbm, other_hbm, out_hbm,
    left_ref, gm_ref, go_ref, out_ref, in_sems, out_sems,
):
    pairs = (
        (own_hbm, left_ref, 0),
        (other_hbm.at[:, pl.ds(0, WIDTH)], left_ref, ROWS),
        (pack_hbm.at[:, pl.ds(GO, WIDTH)], go_ref, 0),
        (other_hbm.at[:, pl.ds(GO, WIDTH)], go_ref, ROWS),
        (pack_hbm.at[:, pl.ds(GM, 2 * WIDTH)], gm_ref, 0),
        (other_hbm.at[:, pl.ds(GM, 2 * WIDTH)], gm_ref, ROWS),
    )
    copies = [
        pltpu.make_async_copy(source, target.at[pl.ds(row, ROWS)], in_sems.at[i])
        for i, (source, target, row) in enumerate(pairs)
    ]
    for copy in copies:
        copy.start()

    def send(i):
        at = pl.ds(i * WIDTH, WIDTH)
        return pltpu.make_async_copy(out_ref.at[:, :, at], out_hbm.at[:, :, at], out_sems.at[i])

    def put(at, product):
        half = product.shape[0] // 2
        lower = product[:half].reshape(half // 8, 8, 256)
        upper = product[half:].reshape(half // 8, 8, 256)
        out_ref[:, :, at : at + 256] = jnp.concatenate([lower, upper], axis=1).astype(BF16)

    for copy in copies[:4]:
        copy.wait()
    swished = left_ref[:, 512:1024].T
    for j in range(0, WIDTH, 256):
        put(2 * WIDTH + j, dot(swished, go_ref[:, j : j + 256]))
    send(2).start()
    for copy in copies[4:]:
        copy.wait()
    low = left_ref[:, 0:512].T
    for j in range(0, 2 * WIDTH, 256):
        put(j, dot(low, gm_ref[:, j : j + 256]))
        if j + 256 == WIDTH:
            send(0).start()
    send(1).start()
    for i in range(3):
        send(i).wait()


def fold_kernel(scal_ref, pieces_ref, mine_ref, theirs_ref):
    upper = scal_ref[4]

    def fold(at):
        total = pieces_ref[0, :, at].astype(F32)
        for k in range(1, pieces_ref.shape[0]):
            total = total + pieces_ref[k, :, at].astype(F32)
        first, second = total[:8], total[8:]
        mine_ref[:, at] = jnp.where(upper == 0, first, second)
        return jnp.where(upper == 0, second, first)

    middle = theirs_ref.shape[1]
    for j in range(0, middle, 256):
        low = fold(slice(j, j + 256))
        high = fold(slice(middle + j, middle + j + 256))
        theirs_ref[:, j : j + 256] = jnp.concatenate([low, high], axis=0).astype(BF16)


def join_kernel(mine_ref, theirs_ref, in_ref, out_ref):
    theirs = theirs_ref[...].astype(F32)
    whole = mine_ref[...] + jnp.concatenate([theirs[:8], theirs[8:]], axis=1)
    in_ref[...] = whole[:, : 2 * WIDTH]
    out_ref[...] = whole[:, 2 * WIDTH :]


VMEM = pl.BlockSpec(memory_space=pltpu.VMEM)
SMEM = pl.BlockSpec(memory_space=pltpu.SMEM)
HBM = pl.BlockSpec(memory_space=pltpu.HBM)


def kernel_call(body, out_shape, in_specs, scratch, limit, flops, moved, out_spec=VMEM):
    return pl.pallas_call(
        body,
        out_shape=out_shape,
        in_specs=in_specs,
        out_specs=[out_spec] * len(out_shape),
        scratch_shapes=scratch,
        compiler_params=pltpu.CompilerParams(vmem_limit_bytes=limit << 20),
        cost_estimate=pl.CostEstimate(flops=flops, bytes_accessed=moved, transcendentals=0),
    )


def shape(dims, dtype):
    return jax.ShapeDtypeStruct(dims, dtype)


def per_device(
    clean_input, corrupt_input, patch_mask, lengths, site_ids, w_query, w_key, w_value,
    w_attn_out, w_pointwise_in, depth_kernel, w_pointwise_out, cotangent,
):
    frames = lax.axis_size("frames")
    position = lax.axis_index("frames")
    core = lax.rem(lax.axis_index("dp"), 2)
    scalars = jnp.stack(
        [position * ROWS, lengths[0], core, lax.rem(position, 2), lax.axis_index("dp") // 2]
    ).astype(jnp.int32)
    clean, corrupt, cot = clean_input[0], corrupt_input[0], cotangent[0]

    msg, patched, up, down = kernel_call(
        project_kernel,
        [shape((frames, ROWS, 128), BF16), shape((ROWS, WIDTH), BF16),
         shape((2 * RIM, WIDTH), BF16), shape((2 * RIM, WIDTH), BF16)],
        [HBM] * 3 + [VMEM] + [HBM] * 3,
        [pltpu.VMEM((2 * ROWS, WIDTH), BF16), pltpu.VMEM((ROWS, ROWS), F32),
         pltpu.VMEM((ROWS, WIDTH), BF16), pltpu.VMEM((ROWS, WIDTH), BF16),
         pltpu.VMEM((WIDTH, 512), BF16), pltpu.VMEM((WIDTH, 512), BF16),
         pltpu.VMEM((WIDTH, 512), BF16), pltpu.SemaphoreType.DMA((7,))],
        62, 8 * 10**8, 6 * 10**6,
    )(clean, corrupt, cot, patch_mask, w_query, w_key, w_value)
    forward = [(i, i + 1) for i in range(frames - 1)]
    backward = [(i + 1, i) for i in range(frames - 1)]
    from_left = lax.ppermute(up, "frames", forward)
    from_right = lax.ppermute(down, "frames", backward)
    recv = lax.all_to_all(msg, "frames", 0, 0, tiled=True)
    recv, from_left, from_right = lax.optimization_barrier((recv, from_left, from_right))
    keys = frames * ROWS // 2
    (context,) = kernel_call(
        attend_kernel,
        [shape((frames, 112, 128), BF16)],
        [SMEM, VMEM],
        [pltpu.VMEM((keys, 128), BF16), pltpu.VMEM((80, keys), BF16),
         pltpu.VMEM((128, 2 * keys), BF16),
         pltpu.VMEM((keys, 512), F32), pltpu.VMEM((keys, 512), F32),
         pltpu.VMEM((frames * 64, 128), F32), pltpu.VMEM((frames * 8, 128), F32)],
        20, 8 * 10**9, 10**6,
    )(scalars, recv)
    contexts = lax.all_to_all(context, "frames", 0, 0, tiled=True)
    own, pack, swished, grad_swished, grad_gated, gated, resid = kernel_call(
        clean_kernel,
        [shape((ROWS, WIDTH), BF16), shape((ROWS, 4 * WIDTH), BF16),
         shape((INNER, WIDTH), BF16), shape((INNER, WIDTH), F32),
         shape((ROWS * 8, 128), F32), shape((CLEAN * 8, 128), F32), shape((CLEAN, WIDTH), BF16)],
        [SMEM] + [HBM] * 9,
        [pltpu.VMEM((16, 112, 128), BF16), pltpu.VMEM((512, WIDTH), BF16),
         pltpu.VMEM((WIDTH, 2 * WIDTH), BF16), pltpu.VMEM((KERNEL, WIDTH), BF16),
         pltpu.VMEM((WIDTH, WIDTH), BF16),
         pltpu.VMEM((ROWS, WIDTH), BF16), pltpu.VMEM((ROWS, 4 * WIDTH), BF16),
         pltpu.VMEM((INNER, WIDTH), BF16), pltpu.VMEM((INNER, WIDTH), F32),
         pltpu.VMEM((ROWS * 8, 128), F32), pltpu.VMEM((CLEAN * 8, 128), F32),
         pltpu.VMEM((CLEAN, WIDTH), BF16),
         pltpu.VMEM((CLEAN, 512), BF16), pltpu.VMEM((CLEAN, WIDTH), BF16),
         pltpu.VMEM((CLEAN, WIDTH), BF16),
         pltpu.VMEM((ROWS, WIDTH), F32), pltpu.VMEM((ROWS, WIDTH), F32),
         pltpu.VMEM((INNER * 8, 128), F32), pltpu.VMEM((INNER, WIDTH), F32),
         pltpu.VMEM((INNER, 128), F32), pltpu.VMEM((INNER, WIDTH), BF16),
         pltpu.VMEM((INNER * 8, 128), F32), pltpu.VMEM((32 * 8, 128), F32),
         pltpu.SemaphoreType.DMA((18,)), pltpu.SemaphoreType.DMA((9,))],
        59, 3 * 10**9, 10**7, HBM,
    )(scalars, contexts, clean, cot, from_left, from_right,
      w_attn_out, w_pointwise_in, depth_kernel, w_pointwise_out)

    cores = [(i, i ^ 1) for i in range(lax.axis_size("dp"))]
    other = lax.ppermute(pack, "dp", cores)
    (partial,) = kernel_call(
        weight_kernel,
        [shape((frames, 16, 3 * WIDTH), BF16)],
        [HBM] * 3,
        [pltpu.VMEM((2 * ROWS, WIDTH), BF16), pltpu.VMEM((2 * ROWS, 2 * WIDTH), BF16),
         pltpu.VMEM((2 * ROWS, WIDTH), BF16), pltpu.VMEM((frames, 16, 3 * WIDTH), BF16),
         pltpu.SemaphoreType.DMA((6,)), pltpu.SemaphoreType.DMA((3,))],
        59, 8 * 10**8, 10**7, HBM,
    )(own, pack, other)
    pieces = lax.all_to_all(partial, "frames", 0, 0, tiled=True)
    (attribution,) = kernel_call(
        patch_kernel,
        [shape((site_ids.shape[0], ROWS), F32)],
        [SMEM, SMEM] + [VMEM] * 14,
        [pltpu.VMEM((PATCH, 512), BF16), pltpu.VMEM((PATCH, WIDTH), BF16),
         pltpu.VMEM((PATCH, WIDTH), BF16), pltpu.VMEM((PATCH, WIDTH), BF16),
         pltpu.VMEM((PATCH * 8, 128), F32), pltpu.VMEM((ROWS * 8, 128), F32),
         pltpu.VMEM((2 * ROWS, WIDTH), BF16), pltpu.VMEM((ROWS, WIDTH), F32),
         pltpu.VMEM((ROWS, 128), F32), pltpu.VMEM((ROWS, 128), F32), pltpu.VMEM((ROWS, 128), F32),
         pltpu.VMEM((32 * 8, 128), F32)],
        28, 3 * 10**9, 10**7,
    )(scalars, site_ids, contexts, patched, from_left, from_right,
      w_attn_out, w_pointwise_in, depth_kernel, w_pointwise_out,
      pack, swished, grad_swished, grad_gated, gated, resid)
    pieces, attribution = lax.optimization_barrier((pieces, attribution))
    mine, theirs = kernel_call(
        fold_kernel,
        [shape((8, 3 * WIDTH), F32), shape((16, 3 * WIDTH // 2), BF16)],
        [SMEM, VMEM],
        [],
        16, 10**8, 3 * 10**6,
    )(scalars, pieces)
    half_dp = lax.axis_size("dp") // 2
    theirs = lax.ppermute(theirs, "dp", [(i, i ^ half_dp) for i in range(2 * half_dp)])
    grad_in, grad_out = kernel_call(
        join_kernel,
        [shape((8, 2 * WIDTH), F32), shape((8, WIDTH), F32)],
        [VMEM] * 2,
        [],
        16, 10**6, 10**6,
    )(mine, theirs)
    return attribution[None], grad_in, grad_out


def solution(mesh):
    placed = (
        P("dp", "frames", None), P("dp", "frames", None), P("dp", "frames"), P("dp"), P(), P(), P(),
        P(), P(), P(), P(), P(), P("dp", "frames", None),
    )
    return jax.shard_map(
        per_device,
        mesh=mesh,
        in_specs=placed,
        out_specs=(P("dp", None, "frames"), P(("dp", "frames"), None), P(("dp", "frames"), None)),
        check_vma=False,
    )
```

```python
import jax
import jax.numpy as jnp
from jax import lax
from jax.experimental import pallas as pl
from jax.experimental.pallas import tpu as pltpu
from jax.sharding import PartitionSpec as P

HEADS = 8
DH = 64
KERNEL = 31
RIM = 32
EPSILON = 1e-05
FLOOR = -1e30
LOG2E = 1.4426950408889634
F32 = jnp.float32
BF16 = jnp.bfloat16
ROWS = 128
WIDTH = 1024
CLEAN = ROWS + 2 * RIM
PATCH = ROWS + RIM
BOTH = CLEAN + PATCH
INNER = ROWS + RIM
GM = WIDTH
GO = 3 * WIDTH
UNROLL = True
TAP_UNROLL = 4
LOAD_UNROLL = 4
PACK_UNROLL = 4
CHUNK = 256


def lane_of(rows):
    return lax.broadcasted_iota(jnp.int32, (rows, 128), 1)


def swap(tile):
    return pltpu.roll(tile, 64, 1)


def moments(values):
    mean = jnp.mean(values, axis=-1, keepdims=True)
    centred = values - mean
    variance = jnp.mean(centred * centred, axis=-1, keepdims=True)
    return centred, lax.rsqrt(variance + EPSILON)


def dot(left, right):
    return jnp.dot(left, right, preferred_element_type=F32)


def dot_nt(left, right):
    return lax.dot_general(left, right, (((1,), (1,)), ((), ())), preferred_element_type=F32)


def dot_tn(left, right):
    return lax.dot_general(left, right, (((0,), (0,)), ((), ())), preferred_element_type=F32)


def sigmoid(values):
    return 0.5 * jnp.tanh(0.5 * values) + 0.5


def lane_sum(values):
    total = values[:, :128]
    for start in range(128, values.shape[1], 128):
        total = total + values[:, start : start + 128]
    return total


def project_kernel(
    clean_hbm, corrupt_hbm, cot_hbm, mask_ref, wq_hbm, wk_hbm, wv_hbm,
    msg_out, patched_out, up_out, down_out,
    msg_ref, patched_ref, up_ref, down_ref,
    hidden_ref, mask_col, clean_ref, corrupt_ref, wq_ref, wk_ref, wv_ref, sems, out_sems,
):
    half = RIM // 2
    copies = [
        pltpu.make_async_copy(source, target, sems.at[i])
        for i, (source, target) in enumerate((
            (clean_hbm, clean_ref),
            (corrupt_hbm, corrupt_ref),
            (wk_hbm, wk_ref),
            (wv_hbm, wv_ref),
            (wq_hbm, wq_ref),
            (cot_hbm.at[pl.ds(ROWS - half, half)], up_ref.at[pl.ds(RIM + half, half)]),
            (cot_hbm.at[pl.ds(0, half)], down_ref.at[pl.ds(RIM + half, half)]),
        ))
    ]
    for copy in copies:
        copy.start()
    spread_mask = jnp.broadcast_to(mask_ref[...].astype(F32), (ROWS, ROWS))
    mask_col[...] = spread_mask.T
    copies[0].wait()
    copies[1].wait()

    def rows(i, carry):
        at = pl.ds(pl.multiple_of(i * 16, 16), 16)
        below = pl.ds(pl.multiple_of(ROWS + i * 16, 16), 16)
        clean = clean_ref[at, :].astype(F32)
        corrupt = corrupt_ref[at, :].astype(F32)
        patched = jnp.where(mask_col[at, 0:1] == 1.0, corrupt, clean)
        patched_ref[at, :] = patched.astype(BF16)
        for dest, source in ((at, clean), (below, patched)):
            centred, inverse = moments(source)
            hidden_ref[dest, :] = (centred * inverse).astype(BF16)
        return carry

    lax.fori_loop(0, ROWS // 16, rows, 0, unroll=UNROLL)
    up_ref[0:RIM, :] = clean_ref[ROWS - RIM : ROWS, :]
    up_ref[RIM : RIM + half, :] = patched_ref[ROWS - half : ROWS, :]
    down_ref[0:RIM, :] = clean_ref[0:RIM, :]
    down_ref[RIM : RIM + half, :] = patched_ref[0:half, :]
    for copy in copies[2:]:
        copy.wait()
    results = [
        pltpu.make_async_copy(source, target, out_sems.at[i])
        for i, (source, target) in enumerate((
            (up_ref, up_out), (down_ref, down_out), (patched_ref, patched_out),
            *(
                (msg_ref.at[pl.ds(at, 8)], msg_out.at[pl.ds(at, 8)])
                for at in (0, 16, 8, 24)
            ),
        ))
    ]
    for copy in results[:3]:
        copy.start()

    low = lane_of(ROWS) < 64
    low_q = lane_of(64) < 64
    for pair in range(2):
        cols = slice(pair * 256, pair * 256 + 256)
        hidden = hidden_ref[...]
        query = dot(hidden, wq_ref[:, cols])
        keys = dot(hidden, wk_ref[:, cols])
        values = dot(hidden, wv_ref[:, cols])
        for sub in range(2):
            tile = slice(sub * 128, sub * 128 + 128)
            for run in range(2):
                part = slice(run * ROWS, run * ROWS + ROWS)
                k, v, q = keys[part, tile], values[part, tile], query[part, tile]
                base = run * 16 + (pair * 2 + sub) * 4
                kv = (jnp.where(low, k, swap(v)).astype(BF16), jnp.where(low, swap(k), v).astype(BF16))
                early, late = q[:64], q[64:]
                asked = (
                    jnp.where(low_q, early, swap(late)).astype(BF16),
                    jnp.where(low_q, swap(early), late).astype(BF16),
                )
                for odd in range(2):
                    for side in range(2):
                        dest = base + odd * 2 + side
                        msg_ref[dest, 0:64, :] = kv[odd][side * 64 : side * 64 + 64]
                        msg_ref[dest, 64:128, :] = asked[odd]
        results[3 + 2 * pair].start()
        results[4 + 2 * pair].start()
    for copy in results:
        copy.wait()


def attend_kernel(
    scal_ref, recv_ref, out_ref, k_ref, vt_ref, qt_ref, s0_ref, s1_ref, c_ref, r_ref
):
    length, side = scal_ref[1], scal_ref[3]
    sources = recv_ref.shape[0]
    lane = lane_of(128)
    row = lax.broadcasted_iota(jnp.int32, (128, 128), 0)
    scale = DH ** (-0.5) * LOG2E

    def load(s, carry):
        at = pl.multiple_of(s * 128, 128)
        kv = recv_ref[pl.ds(2 * s, 2), 0:64, :].astype(F32).reshape(128, 128)
        frame = (2 * s + row // 64) * ROWS + side * 64 + row % 64
        bias = jnp.where(frame < length, 0.0, FLOOR)
        keyed = jnp.where(lane < 64, kv, jnp.where(lane == 64, bias, 0.0))
        k_ref[pl.ds(at, 128), :] = keyed.astype(BF16)
        vt_ref[0:64, pl.ds(at, 128)] = kv.T[64:128].astype(BF16)
        vt_ref[64:80, pl.ds(at, 128)] = jnp.ones((16, 128), BF16)
        raw = recv_ref[pl.ds(2 * s, 2), 64:128, :].astype(F32).reshape(128, 128).T
        fill = jnp.where(row == 64, 1.0, 0.0)
        other = jnp.concatenate([raw[64:], raw[:64]], axis=0)
        at = pl.multiple_of(s * 256, 256)
        qt_ref[:, pl.ds(at, 128)] = jnp.where(row < 64, raw, fill).astype(BF16)
        qt_ref[:, pl.ds(at + 128, 128)] = jnp.where(row < 64, other, fill).astype(BF16)
        return carry

    lax.fori_loop(0, sources // 2, load, 0, unroll=LOAD_UNROLL)

    many = s0_ref.shape[1]
    chunk = CHUNK
    pieces = k_ref.shape[0] // chunk
    blocks = sources * ROWS // many

    def score_piece(query, s_ref, k, top):
        at = slice(k * chunk, k * chunk + chunk)
        scores = dot(k_ref[at, :], query)
        s_ref[at, :] = scores
        best = jnp.max(scores.reshape(chunk // 8, 8, many), axis=0)
        return best if top is None else jnp.maximum(top, best)

    def weigh_piece(s_ref, best, k, accum):
        at = slice(k * chunk, k * chunk + chunk)
        weights = jnp.exp2((s_ref[at, :] - best) * scale).astype(BF16)
        addend = dot(vt_ref[:, at], weights)
        return addend if accum is None else accum + addend

    def finish(top):
        return jnp.max(top, axis=0, keepdims=True)

    def queries(b):
        return qt_ref[:, pl.ds(pl.multiple_of(b * many, many), many)]

    low8 = lane_of(8) < 64

    def store(b, accum, best):
        total = accum[64:65, :]
        result = accum[0:64, :] / total
        level = jnp.broadcast_to(best * scale + jnp.log2(total), (8, many))
        for g in range(many // 256):
            first = slice(g * 256, g * 256 + 128)
            second = slice(g * 256 + 128, g * 256 + 256)
            both = jnp.concatenate([result[:, first], result[:, second]], axis=0)
            at = b * (many // 256) + g
            c_ref[pl.ds(pl.multiple_of(at * 128, 128), 128), :] = both.T
            early, late = level[:, first], level[:, second]
            r_ref[pl.ds(pl.multiple_of(at * 16, 16), 8), :] = jnp.where(low8, early, swap(late))
            r_ref[pl.ds(pl.multiple_of(at * 16 + 8, 8), 8), :] = jnp.where(low8, swap(early), late)

    def step(b, s_ref, best, next_b, next_s):
        query = None if next_s is None else queries(next_b)
        top, accum = None, None
        for k in range(pieces):
            if query is not None:
                top = score_piece(query, next_s, k, top)
            accum = weigh_piece(s_ref, best, k, accum)
        store(b, accum, best)
        return None if query is None else finish(top)

    query, top = queries(0), None
    for k in range(pieces):
        top = score_piece(query, s0_ref, k, top)

    def pair(i, best):
        best = step(2 * i, s0_ref, best, 2 * i + 1, s1_ref)
        return step(2 * i + 1, s1_ref, best, 2 * i + 2, s0_ref)

    best = lax.fori_loop(0, blocks // 2 - 1, pair, finish(top))
    best = step(blocks - 2, s0_ref, best, blocks - 1, s1_ref)
    step(blocks - 1, s1_ref, best, None, None)

    low32 = lane_of(32) < 64
    row8 = lax.broadcasted_iota(jnp.int32, (8, 128), 0)

    def pack(d, carry):
        after = lax.rem(d + 1, sources)
        before = lax.rem(d + sources - 1, sources)
        out_ref[d, 0:64, :] = c_ref[pl.ds(pl.multiple_of(d * 64, 64), 64), :].astype(BF16)
        right = c_ref[pl.ds(pl.multiple_of(after * 64, 64), 32), :]
        left = c_ref[pl.ds(pl.multiple_of(before * 64 + 32, 32), 32), :]
        out_ref[d, 64:96, :] = jnp.where(low32, right, left).astype(BF16)
        own = r_ref[pl.ds(pl.multiple_of(d * 8, 8), 8), :]
        rim = jnp.where(
            low8,
            r_ref[pl.ds(pl.multiple_of(after * 8, 8), 8), :],
            r_ref[pl.ds(pl.multiple_of(before * 8, 8), 8), :],
        )
        rows = jnp.where(row8 < 3, own, rim)
        high = rows.astype(BF16).astype(F32)
        rest = rows - high
        middle = rest.astype(BF16).astype(F32)
        last = rest - middle
        level = row8 % 3
        rows = jnp.where(level == 0, high, jnp.where(level == 1, middle, last))
        out_ref[d, 96:112, :] = jnp.concatenate([rows, rows], axis=0).astype(BF16)
        return carry

    lax.fori_loop(0, sources, pack, 0, unroll=PACK_UNROLL)


def depthwise(source, source_row, taps_ref, order, target, count):
    def rows(i, carry):
        first = source_row + i * 8
        taps = [taps_ref[t * 8 : t * 8 + 8, :] for t in order]
        sums = [None] * 8
        for s in range(KERNEL + 7):
            piece = source[pl.ds(pl.multiple_of((first + s) * 8, 8), 8), :]
            for o in range(8):
                if 0 <= s - o < KERNEL:
                    term = taps[s - o] * piece
                    sums[o] = term if sums[o] is None else sums[o] + term
        for o in range(8):
            target[pl.ds(pl.multiple_of((i * 8 + o) * 8, 8), 8), :] = sums[o]
        return carry

    lax.fori_loop(0, count // 8, rows, 0, unroll=TAP_UNROLL)


def put_rows(ref, row, tile, values):
    for r in range(0, values.shape[0], 8):
        ref[pl.ds((row + r) * 8 + tile, 8, stride=8), :] = values[r : r + 8]


def get_rows(ref, row, count):
    groups = []
    for r in range(0, count, 8):
        tiles = [ref[pl.ds((row + r) * 8 + t, 8, stride=8), :] for t in range(8)]
        groups.append(jnp.concatenate(tiles, axis=1))
    return jnp.concatenate(groups, axis=0) if len(groups) > 1 else groups[0]


def place_context(ctx_in, base, ctx_ref, rim):
    row8 = lax.broadcasted_iota(jnp.int32, (8, 128), 0)
    zero = jnp.zeros((8, 128), F32)
    levels = [[zero, zero], [zero, zero]]
    for h in range(HEADS):
        for side in range(2):
            block = ctx_in[base + h * 2 + side, 96:112, :].astype(F32)
            for kind in range(2):
                at = kind * 3
                level = block[at : at + 1] + block[at + 1 : at + 2] + block[at + 2 : at + 3]
                levels[kind][side] = jnp.where(row8 == h, level, levels[kind][side])
    shares = []
    for first, second in levels:
        shares.append(1.0 / (1.0 + jnp.exp2(second - first)))
        shares.append(1.0 / (1.0 + jnp.exp2(first - second)))
    share = jnp.concatenate(shares + [jnp.zeros((96, 128), F32)], axis=0).T
    low = lane_of(96) < 64
    low_rows = lane_of(ROWS) < 64
    for t in range(HEADS // 2):
        at = slice(t * 128, t * 128 + 128)
        own = left = right = None
        for side in range(2):
            even = ctx_in[base + t * 4 + side, 0:96, :].astype(F32)
            odd = ctx_in[base + t * 4 + 2 + side, 0:96, :].astype(F32)
            first = jnp.where(low, even, swap(odd))
            second = jnp.where(low, swap(even), odd)
            scale = []
            for kind in range(2):
                column = kind * 16 + side * 8 + 2 * t
                scale.append(jnp.where(
                    low_rows, share[:, column : column + 1], share[:, column + 1 : column + 2]
                ))
            part = jnp.concatenate([first[:64], second[:64]], axis=0) * scale[0]
            after = first[64:96] * scale[1][0:32]
            before = second[64:96] * scale[1][96:128]
            own = part if own is None else own + part
            left = before if left is None else left + before
            right = after if right is None else right + after
        ctx_ref[0:rim, at] = left[RIM - rim :].astype(BF16)
        ctx_ref[rim : rim + ROWS, at] = own.astype(BF16)
        ctx_ref[rim + ROWS :, at] = right[:rim].astype(BF16)


def place_taps(depth_ref, taps_ref):
    for r in range(0, KERNEL + 1, 8):
        got = min(8, KERNEL - r)
        block = depth_ref[r : r + got, :].astype(F32)
        if got < 8:
            block = jnp.concatenate([block, jnp.zeros((8 - got, WIDTH), F32)], axis=0)
        for t in range(8):
            put_rows(taps_ref, r, t, block[:, t * 128 : t * 128 + 128])


def to_lowered(x_ref, ctx_ref, wao_ref, resid_ref, low_ref):
    for j in range(4):
        at = slice(j * 256, j * 256 + 256)
        joined = x_ref[:, at].astype(F32) + dot(ctx_ref[...], wao_ref[:, at])
        resid_ref[:, at] = joined.astype(BF16)

    def lower(i, carry):
        at = pl.ds(pl.multiple_of(i * 16, 16), 16)
        centred, inverse = moments(resid_ref[at, :].astype(F32))
        low_ref[at, :] = (centred * inverse).astype(BF16)
        return carry

    lax.fori_loop(0, x_ref.shape[0] // 16, lower, 0, unroll=UNROLL)


def to_gated(low_ref, win_ref, g2_ref, frame, length, keep, arrivals=None):
    live = jnp.where((frame >= 0) & (frame < length), 1.0, 0.0)
    for j in range(4):
        at = slice(j * 256, j * 256 + 256)
        gate_at = slice(WIDTH + j * 256, WIDTH + j * 256 + 256)
        if arrivals is not None:
            arrivals[2 * j].wait()
            arrivals[2 * j + 1].wait()
        value = dot(low_ref[...], win_ref[:, at])
        gate = sigmoid(dot(low_ref[...], win_ref[:, gate_at]))
        if keep is not None:
            mv_ref, sg_ref = keep
            mv_ref[:, at] = value[RIM : RIM + ROWS]
            sg_ref[:, at] = gate[RIM : RIM + ROWS]
        gated = (value * gate * live).astype(BF16).astype(F32)
        for t in range(2):
            put_rows(g2_ref, 0, j * 2 + t, gated[:, t * 128 : t * 128 + 128])


def clean_kernel(
    scal_ref, ctx_hbm, clean_hbm, cot_hbm, up_hbm, down_hbm,
    wao_hbm, win_hbm, depth_hbm, wout_hbm,
    own_out, pack_out, sw_out, gs_out, gg2_out, g2_out, resid_out,
    ctx_in, wao_ref, win_ref, depth_ref, wout_ref,
    own_ref, pack_ref, sw_ref, gs_ref, gg2_ref, g2_ref, resid_ref,
    ctx_ref, x_ref, low_ref, mv_ref, sg_ref, s2_ref, zed_ref, zinv_ref, gox_ref, gsp2_ref, taps_ref,
    in_sems, out_sems,
):
    first_frame, length, core = scal_ref[0], scal_ref[1], scal_ref[2]
    half = RIM // 2
    copies = [
        pltpu.make_async_copy(source, target, in_sems.at[i])
        for i, (source, target) in enumerate((
            (ctx_hbm.at[pl.ds(0, 16)], ctx_in),
            (up_hbm.at[pl.ds(0, RIM)], x_ref.at[pl.ds(0, RIM)]),
            (clean_hbm, x_ref.at[pl.ds(RIM, ROWS)]),
            (down_hbm.at[pl.ds(0, RIM)], x_ref.at[pl.ds(RIM + ROWS, RIM)]),
            (wao_hbm, wao_ref),
            (depth_hbm, depth_ref),
            (up_hbm.at[pl.ds(RIM + half, half)], gox_ref.at[pl.ds(0, half)]),
            (cot_hbm, gox_ref.at[pl.ds(half, ROWS)]),
            (down_hbm.at[pl.ds(RIM + half, half)], gox_ref.at[pl.ds(half + ROWS, half)]),
            *(
                (win_hbm.at[:, pl.ds(at, 256)], win_ref.at[:, pl.ds(at, 256)])
                for j in range(0, WIDTH, 256)
                for at in (j, WIDTH + j)
            ),
            (wout_hbm, wout_ref),
        ))
    ]
    for copy in copies:
        copy.start()
    results = [
        pltpu.make_async_copy(source, target, out_sems.at[i])
        for i, (source, target) in enumerate((
            (own_ref, own_out),
            *(
                (pack_ref.at[:, pl.ds(at, size)], pack_out.at[:, pl.ds(at, size)])
                for at, size in ((0, WIDTH), (GM, 2 * WIDTH), (GO, WIDTH))
            ),
            (sw_ref, sw_out), (gs_ref, gs_out), (gg2_ref, gg2_out), (g2_ref, g2_out),
            (resid_ref, resid_out),
        ))
    ]
    own_copy, send_copy, gm_copy, go_copy, sw_copy, gs_copy, gg2_copy, g2_copy, resid_copy = results
    copies[0].wait()
    place_context(ctx_in, 0, ctx_ref, RIM)
    for copy in copies[1:9]:
        copy.wait()
    place_taps(depth_ref, taps_ref)
    for row in range(0, INNER, 16):
        at = slice(row, row + 16)
        frame = first_frame - half + row + lax.broadcasted_iota(jnp.int32, (16, 1), 0)
        gox_ref[at, :] = (gox_ref[at, :].astype(F32) * jnp.where(frame < length, 1.0, 0.0)).astype(BF16)
    pack_ref[:, GO:] = gox_ref[half : half + ROWS, :]
    go_copy.start()

    to_lowered(x_ref, ctx_ref, wao_ref, resid_ref, low_ref)
    resid_copy.start()
    frame = first_frame - RIM + lax.broadcasted_iota(jnp.int32, (CLEAN, 1), 0)
    to_gated(low_ref, win_ref, g2_ref, frame, length, (mv_ref, sg_ref), copies[9:17])
    g2_copy.start()
    forward = list(range(KERNEL))
    edge = half - KERNEL // 2
    depthwise(g2_ref, edge, taps_ref, forward, s2_ref, INNER)

    def clean_rows(i, carry):
        r = pl.multiple_of(i * 16, 16)
        centred, inverse = moments(get_rows(s2_ref, r, 16))
        zed = centred * inverse
        zed_ref[pl.ds(r, 16), :] = zed
        zinv_ref[pl.ds(r, 16), :] = jnp.broadcast_to(inverse, (16, 128))
        sw_ref[pl.ds(r, 16), :] = (zed * sigmoid(zed)).astype(BF16)
        return carry

    lax.fori_loop(0, INNER // 16, clean_rows, 0, unroll=UNROLL)
    sw_copy.start()

    for part in range(4):
        dest = part * 256
        source, row = (low_ref, RIM) if part < 2 else (sw_ref, half)
        lo = (part % 2) * 512
        first = source[row : row + ROWS, lo : lo + 256].astype(F32)
        second = source[row : row + ROWS, lo + 256 : lo + 512].astype(F32)
        own_ref[:, dest : dest + 256] = jnp.where(core == 0, first, second).astype(BF16)
        pack_ref[:, dest : dest + 256] = jnp.where(core == 0, second, first).astype(BF16)
    own_copy.start()
    send_copy.start()

    copies[17].wait()
    for j in range(4):
        at = slice(j * 256, j * 256 + 256)
        gs_ref[:, at] = dot_nt(gox_ref[...], wout_ref[at, :])
    gs_copy.start()

    def back_rows(i, carry):
        r = pl.multiple_of(i * 16, 16)
        zed = zed_ref[pl.ds(r, 16), :]
        grad = gs_ref[pl.ds(r, 16), :]
        gate = sigmoid(zed)
        grad_zed = grad * (gate * (1.0 + zed * (1.0 - gate)))
        mean = jnp.mean(grad_zed, axis=-1, keepdims=True)
        along = jnp.mean(grad_zed * zed, axis=-1, keepdims=True)
        result = (grad_zed - mean - zed * along) * zinv_ref[pl.ds(r, 16), 0:1]
        for g in range(0, 16, 8):
            for t in range(8):
                gsp2_ref[pl.ds((r + g) * 8 + t, 8, stride=8), :] = result[
                    g : g + 8, t * 128 : t * 128 + 128
                ]
        return carry

    lax.fori_loop(0, INNER // 16, back_rows, 0, unroll=UNROLL)
    depthwise(gsp2_ref, edge, taps_ref, forward[::-1], gg2_ref, ROWS)
    gg2_copy.start()

    def mixed_rows(i, carry):
        r = pl.multiple_of(i * 16, 16)
        at = pl.ds(r, 16)
        frame = first_frame + r + lax.broadcasted_iota(jnp.int32, (16, 1), 0)
        grad = get_rows(gg2_ref, r, 16) * jnp.where(frame < length, 1.0, 0.0)
        gate = sg_ref[at, :]
        pack_ref[at, GM : GM + WIDTH] = (grad * gate).astype(BF16)
        pack_ref[at, GM + WIDTH : GO] = (grad * mv_ref[at, :] * gate * (1.0 - gate)).astype(BF16)
        return carry

    lax.fori_loop(0, ROWS // 16, mixed_rows, 0, unroll=UNROLL)

    gm_copy.start()
    for copy in results:
        copy.wait()


def patch_kernel(
    scal_ref, site_ref, ctx_in, patched_ref, up_ref, down_ref,
    wao_ref, win_ref, depth_ref, wout_ref,
    pack_ref, swc_ref, gs_ref, gg2_ref, g2c_ref, residc_ref,
    attr_ref,
    ctx_ref, x_ref, resid_ref, low_ref, g2_ref, s2_ref, sw_ref, gl_ref, t0_ref, t1_ref, t2_ref, taps_ref,
):
    first_frame, length = scal_ref[0], scal_ref[1]
    half = RIM // 2
    place_context(ctx_in, 16, ctx_ref, half)
    x_ref[0:half, :] = up_ref[RIM : RIM + half, :]
    x_ref[half : half + ROWS, :] = patched_ref[...]
    x_ref[half + ROWS : PATCH, :] = down_ref[RIM : RIM + half, :]
    place_taps(depth_ref, taps_ref)
    to_lowered(x_ref, ctx_ref, wao_ref, resid_ref, low_ref)
    frame = first_frame - half + lax.broadcasted_iota(jnp.int32, (PATCH, 1), 0)
    to_gated(low_ref, win_ref, g2_ref, frame, length, None)
    depthwise(g2_ref, half - KERNEL // 2, taps_ref, list(range(KERNEL)), s2_ref, ROWS)
    sw_ref[0:ROWS, :] = swc_ref[half : half + ROWS, :]

    def patch_rows(i, carry):
        r = pl.multiple_of(i * 16, 16)
        at = pl.ds(r, 16)
        inner = pl.ds(pl.multiple_of(half + r, 16), 16)
        centred, inverse = moments(get_rows(s2_ref, r, 16))
        zed = centred * inverse
        swished = (zed * sigmoid(zed)).astype(BF16)
        sw_ref[pl.ds(pl.multiple_of(ROWS + r, 16), 16), :] = swished
        gap = swished.astype(F32) - sw_ref[at, :].astype(F32)
        t2_ref[at, :] = lane_sum(gap * gs_ref[inner, :])
        frame = first_frame + r + lax.broadcasted_iota(jnp.int32, (16, 1), 0)
        grad = get_rows(gg2_ref, r, 16) * jnp.where(frame < length, 1.0, 0.0)
        gap = get_rows(g2_ref, half + r, 16) - get_rows(g2c_ref, RIM + r, 16)
        t1_ref[at, :] = lane_sum(gap * grad)
        return carry

    lax.fori_loop(0, ROWS // 16, patch_rows, 0, unroll=UNROLL)

    t3 = jnp.zeros((ROWS, 128), F32)
    for j in range(4):
        at = slice(j * 256, j * 256 + 256)
        out = dot(sw_ref[...], wout_ref[:, at])
        out_clean = residc_ref[RIM : RIM + ROWS, at].astype(F32) + out[:ROWS]
        out_patch = resid_ref[half : half + ROWS, at].astype(F32) + out[ROWS:]
        gap = out_patch.astype(BF16).astype(F32) - out_clean.astype(BF16).astype(F32)
        t3 = t3 + lane_sum(gap * pack_ref[:, GO + j * 256 : GO + j * 256 + 256].astype(F32))
    for j in range(4):
        at = slice(j * 256, j * 256 + 256)
        gl_ref[:, at] = dot_nt(pack_ref[:, GM:GO], win_ref[at, :])

    def resid_rows(i, carry):
        r = pl.multiple_of(i * 16, 16)
        at = pl.ds(r, 16)
        clean = residc_ref[pl.ds(pl.multiple_of(RIM + r, 16), 16), :].astype(F32)
        patch = resid_ref[pl.ds(pl.multiple_of(half + r, 16), 16), :].astype(F32)
        centred, inverse = moments(clean)
        normed = centred * inverse
        grad = gl_ref[at, :]
        mean = jnp.mean(grad, axis=-1, keepdims=True)
        along = jnp.mean(grad * normed, axis=-1, keepdims=True)
        grad_resid = pack_ref[at, GO:].astype(F32) + (grad - mean - normed * along) * inverse
        t0_ref[at, :] = lane_sum((patch - clean) * grad_resid)
        return carry

    lax.fori_loop(0, ROWS // 16, resid_rows, 0, unroll=UNROLL)

    columns = [
        jnp.sum(part, axis=1, keepdims=True) for part in (t0_ref[...], t1_ref[...], t2_ref[...], t3)
    ]
    lane = lane_of(ROWS)
    chosen = jnp.zeros((ROWS, 128), F32)
    for i in range(attr_ref.shape[0]):
        site = site_ref[i]
        column = columns[0]
        for k in range(1, 4):
            column = jnp.where(site == k, columns[k], column)
        chosen = jnp.where(lane == i, column, chosen)
    attr_ref[...] = chosen.T[: attr_ref.shape[0]]


def weight_kernel(
    own_hbm, pack_hbm, other_hbm, out_hbm,
    left_ref, gm_ref, go_ref, out_ref, in_sems, out_sems,
):
    pairs = (
        (own_hbm, left_ref, 0),
        (other_hbm.at[:, pl.ds(0, WIDTH)], left_ref, ROWS),
        (pack_hbm.at[:, pl.ds(GO, WIDTH)], go_ref, 0),
        (other_hbm.at[:, pl.ds(GO, WIDTH)], go_ref, ROWS),
        (pack_hbm.at[:, pl.ds(GM, 2 * WIDTH)], gm_ref, 0),
        (other_hbm.at[:, pl.ds(GM, 2 * WIDTH)], gm_ref, ROWS),
    )
    copies = [
        pltpu.make_async_copy(source, target.at[pl.ds(row, ROWS)], in_sems.at[i])
        for i, (source, target, row) in enumerate(pairs)
    ]
    for copy in copies:
        copy.start()

    def send(i):
        at = pl.ds(i * 512, 512)
        return pltpu.make_async_copy(out_ref.at[:, :, at], out_hbm.at[:, :, at], out_sems.at[i])

    def put(at, product):
        half = product.shape[0] // 2
        lower = product[:half].reshape(half // 8, 8, 256)
        upper = product[half:].reshape(half // 8, 8, 256)
        out_ref[:, :, at : at + 256] = jnp.concatenate([lower, upper], axis=1).astype(BF16)

    for copy in copies[:4]:
        copy.wait()
    swished = left_ref[:, WIDTH // 2 :].T
    for j in range(0, WIDTH, 256):
        put(2 * WIDTH + j, dot(swished, go_ref[:, j : j + 256]))
        if j % 512:
            send(4 + j // 512).start()
    for copy in copies[4:]:
        copy.wait()
    low = left_ref[:, : WIDTH // 2].T
    for j in range(0, 2 * WIDTH, 256):
        put(j, dot(low, gm_ref[:, j : j + 256]))
        if j % 512:
            send(j // 512).start()
    for i in range(6):
        send(i).wait()


def fold_kernel(scal_ref, pieces_ref, mine_ref, theirs_ref):
    upper = scal_ref[4]

    def fold(at):
        total = pieces_ref[0, :, at].astype(F32)
        for k in range(1, pieces_ref.shape[0]):
            total = total + pieces_ref[k, :, at].astype(F32)
        first, second = total[:8], total[8:]
        mine_ref[:, at] = jnp.where(upper == 0, first, second)
        return jnp.where(upper == 0, second, first)

    middle = theirs_ref.shape[1]
    for j in range(0, middle, 256):
        low = fold(slice(j, j + 256))
        high = fold(slice(middle + j, middle + j + 256))
        theirs_ref[:, j : j + 256] = jnp.concatenate([low, high], axis=0).astype(BF16)


def join_kernel(mine_ref, theirs_ref, in_ref, out_ref):
    theirs = theirs_ref[...].astype(F32)
    whole = mine_ref[...] + jnp.concatenate([theirs[:8], theirs[8:]], axis=1)
    in_ref[...] = whole[:, : 2 * WIDTH]
    out_ref[...] = whole[:, 2 * WIDTH :]


VMEM = pl.BlockSpec(memory_space=pltpu.VMEM)
SMEM = pl.BlockSpec(memory_space=pltpu.SMEM)
HBM = pl.BlockSpec(memory_space=pltpu.HBM)


def kernel_call(body, out_shape, in_specs, scratch, limit, flops, moved, out_spec=VMEM):
    return pl.pallas_call(
        body,
        out_shape=out_shape,
        in_specs=in_specs,
        out_specs=[out_spec] * len(out_shape),
        scratch_shapes=scratch,
        compiler_params=pltpu.CompilerParams(vmem_limit_bytes=limit << 20),
        cost_estimate=pl.CostEstimate(flops=flops, bytes_accessed=moved, transcendentals=0),
    )


def shape(dims, dtype):
    return jax.ShapeDtypeStruct(dims, dtype)


def per_device(
    clean_input, corrupt_input, patch_mask, lengths, site_ids, w_query, w_key, w_value,
    w_attn_out, w_pointwise_in, depth_kernel, w_pointwise_out, cotangent,
):
    frames = lax.axis_size("frames")
    position = lax.axis_index("frames")
    core = lax.rem(lax.axis_index("dp"), 2)
    scalars = jnp.stack(
        [position * ROWS, lengths[0], core, lax.rem(position, 2), lax.axis_index("dp") // 2]
    ).astype(jnp.int32)
    clean, corrupt, cot = clean_input[0], corrupt_input[0], cotangent[0]

    msg, patched, up, down = kernel_call(
        project_kernel,
        [shape((frames, ROWS, 128), BF16), shape((ROWS, WIDTH), BF16),
         shape((2 * RIM, WIDTH), BF16), shape((2 * RIM, WIDTH), BF16)],
        [HBM] * 3 + [VMEM] + [HBM] * 3,
        [pltpu.VMEM((frames, ROWS, 128), BF16), pltpu.VMEM((ROWS, WIDTH), BF16),
         pltpu.VMEM((2 * RIM, WIDTH), BF16), pltpu.VMEM((2 * RIM, WIDTH), BF16),
         pltpu.VMEM((2 * ROWS, WIDTH), BF16), pltpu.VMEM((ROWS, ROWS), F32),
         pltpu.VMEM((ROWS, WIDTH), BF16), pltpu.VMEM((ROWS, WIDTH), BF16),
         pltpu.VMEM((WIDTH, 512), BF16), pltpu.VMEM((WIDTH, 512), BF16),
         pltpu.VMEM((WIDTH, 512), BF16), pltpu.SemaphoreType.DMA((7,)), pltpu.SemaphoreType.DMA((7,))],
        62, 8 * 10**8, 6 * 10**6, HBM,
    )(clean, corrupt, cot, patch_mask, w_query, w_key, w_value)
    forward = [(i, i + 1) for i in range(frames - 1)]
    backward = [(i + 1, i) for i in range(frames - 1)]
    from_left = lax.ppermute(up, "frames", forward)
    from_right = lax.ppermute(down, "frames", backward)
    recv = lax.all_to_all(msg, "frames", 0, 0, tiled=True)
    recv, from_left, from_right = lax.optimization_barrier((recv, from_left, from_right))
    keys = frames * ROWS // 2
    (context,) = kernel_call(
        attend_kernel,
        [shape((frames, 112, 128), BF16)],
        [SMEM, VMEM],
        [pltpu.VMEM((keys, 128), BF16), pltpu.VMEM((80, keys), BF16),
         pltpu.VMEM((128, 2 * keys), BF16),
         pltpu.VMEM((keys, 512), F32), pltpu.VMEM((keys, 512), F32),
         pltpu.VMEM((frames * 64, 128), F32), pltpu.VMEM((frames * 8, 128), F32)],
        20, 8 * 10**9, 10**6,
    )(scalars, recv)
    contexts = lax.all_to_all(context, "frames", 0, 0, tiled=True)
    own, pack, swished, grad_swished, grad_gated, gated, resid = kernel_call(
        clean_kernel,
        [shape((ROWS, WIDTH), BF16), shape((ROWS, 4 * WIDTH), BF16),
         shape((INNER, WIDTH), BF16), shape((INNER, WIDTH), F32),
         shape((ROWS * 8, 128), F32), shape((CLEAN * 8, 128), F32), shape((CLEAN, WIDTH), BF16)],
        [SMEM] + [HBM] * 9,
        [pltpu.VMEM((16, 112, 128), BF16), pltpu.VMEM((512, WIDTH), BF16),
         pltpu.VMEM((WIDTH, 2 * WIDTH), BF16), pltpu.VMEM((KERNEL, WIDTH), BF16),
         pltpu.VMEM((WIDTH, WIDTH), BF16),
         pltpu.VMEM((ROWS, WIDTH), BF16), pltpu.VMEM((ROWS, 4 * WIDTH), BF16),
         pltpu.VMEM((INNER, WIDTH), BF16), pltpu.VMEM((INNER, WIDTH), F32),
         pltpu.VMEM((ROWS * 8, 128), F32), pltpu.VMEM((CLEAN * 8, 128), F32),
         pltpu.VMEM((CLEAN, WIDTH), BF16),
         pltpu.VMEM((CLEAN, 512), BF16), pltpu.VMEM((CLEAN, WIDTH), BF16),
         pltpu.VMEM((CLEAN, WIDTH), BF16),
         pltpu.VMEM((ROWS, WIDTH), F32), pltpu.VMEM((ROWS, WIDTH), F32),
         pltpu.VMEM((INNER * 8, 128), F32), pltpu.VMEM((INNER, WIDTH), F32),
         pltpu.VMEM((INNER, 128), F32), pltpu.VMEM((INNER, WIDTH), BF16),
         pltpu.VMEM((INNER * 8, 128), F32), pltpu.VMEM((32 * 8, 128), F32),
         pltpu.SemaphoreType.DMA((18,)), pltpu.SemaphoreType.DMA((9,))],
        59, 3 * 10**9, 10**7, HBM,
    )(scalars, contexts, clean, cot, from_left, from_right,
      w_attn_out, w_pointwise_in, depth_kernel, w_pointwise_out)

    cores = [(i, i ^ 1) for i in range(lax.axis_size("dp"))]
    other = lax.ppermute(pack, "dp", cores)
    (partial,) = kernel_call(
        weight_kernel,
        [shape((frames, 16, 3 * WIDTH), BF16)],
        [HBM] * 3,
        [pltpu.VMEM((2 * ROWS, WIDTH), BF16), pltpu.VMEM((2 * ROWS, 2 * WIDTH), BF16),
         pltpu.VMEM((2 * ROWS, WIDTH), BF16), pltpu.VMEM((frames, 16, 3 * WIDTH), BF16),
         pltpu.SemaphoreType.DMA((6,)), pltpu.SemaphoreType.DMA((6,))],
        59, 8 * 10**8, 10**7, HBM,
    )(own, pack, other)
    pieces = lax.all_to_all(partial, "frames", 0, 0, tiled=True)
    (attribution,) = kernel_call(
        patch_kernel,
        [shape((site_ids.shape[0], ROWS), F32)],
        [SMEM, SMEM] + [VMEM] * 14,
        [pltpu.VMEM((PATCH, 512), BF16), pltpu.VMEM((PATCH, WIDTH), BF16),
         pltpu.VMEM((PATCH, WIDTH), BF16), pltpu.VMEM((PATCH, WIDTH), BF16),
         pltpu.VMEM((PATCH * 8, 128), F32), pltpu.VMEM((ROWS * 8, 128), F32),
         pltpu.VMEM((2 * ROWS, WIDTH), BF16), pltpu.VMEM((ROWS, WIDTH), F32),
         pltpu.VMEM((ROWS, 128), F32), pltpu.VMEM((ROWS, 128), F32), pltpu.VMEM((ROWS, 128), F32),
         pltpu.VMEM((32 * 8, 128), F32)],
        28, 3 * 10**9, 10**7,
    )(scalars, site_ids, contexts, patched, from_left, from_right,
      w_attn_out, w_pointwise_in, depth_kernel, w_pointwise_out,
      pack, swished, grad_swished, grad_gated, gated, resid)
    pieces, attribution = lax.optimization_barrier((pieces, attribution))
    mine, theirs = kernel_call(
        fold_kernel,
        [shape((8, 3 * WIDTH), F32), shape((16, 3 * WIDTH // 2), BF16)],
        [SMEM, VMEM],
        [],
        16, 10**8, 3 * 10**6,
    )(scalars, pieces)
    half_dp = lax.axis_size("dp") // 2
    theirs = lax.ppermute(theirs, "dp", [(i, i ^ half_dp) for i in range(2 * half_dp)])
    grad_in, grad_out = kernel_call(
        join_kernel,
        [shape((8, 2 * WIDTH), F32), shape((8, WIDTH), F32)],
        [VMEM] * 2,
        [],
        16, 10**6, 10**6,
    )(mine, theirs)
    return attribution[None], grad_in, grad_out


def solution(mesh):
    placed = (
        P("dp", "frames", None), P("dp", "frames", None), P("dp", "frames"), P("dp"), P(), P(), P(),
        P(), P(), P(), P(), P(), P("dp", "frames", None),
    )
    return jax.shard_map(
        per_device,
        mesh=mesh,
        in_specs=placed,
        out_specs=(P("dp", None, "frames"), P(("dp", "frames"), None), P(("dp", "frames"), None)),
        check_vma=False,
    )
```

```python
import jax
import jax.numpy as jnp
from jax import lax
from jax.experimental import pallas as pl
from jax.experimental.pallas import tpu as pltpu
from jax.sharding import PartitionSpec as P

HEADS = 8
DH = 64
KERNEL = 31
RIM = 32
EPSILON = 1e-05
FLOOR = -1e30
LOG2E = 1.4426950408889634
F32 = jnp.float32
BF16 = jnp.bfloat16
ROWS = 128
WIDTH = 1024
CLEAN = ROWS + 2 * RIM
PATCH = ROWS + RIM
BOTH = CLEAN + PATCH
INNER = ROWS + RIM
GM = WIDTH
GO = 3 * WIDTH
UNROLL = True
TAP_UNROLL = 4
LOAD_UNROLL = 16
PACK_UNROLL = 8
CHUNK = 256


def lane_of(rows):
    return lax.broadcasted_iota(jnp.int32, (rows, 128), 1)


def swap(tile):
    return pltpu.roll(tile, 64, 1)


def moments(values):
    mean = jnp.mean(values, axis=-1, keepdims=True)
    centred = values - mean
    variance = jnp.mean(centred * centred, axis=-1, keepdims=True)
    return centred, lax.rsqrt(variance + EPSILON)


def dot(left, right):
    return jnp.dot(left, right, preferred_element_type=F32)


def dot_nt(left, right):
    return lax.dot_general(left, right, (((1,), (1,)), ((), ())), preferred_element_type=F32)


def dot_tn(left, right):
    return lax.dot_general(left, right, (((0,), (0,)), ((), ())), preferred_element_type=F32)


def sigmoid(values):
    return 0.5 * jnp.tanh(0.5 * values) + 0.5


def lane_sum(values):
    total = values[:, :128]
    for start in range(128, values.shape[1], 128):
        total = total + values[:, start : start + 128]
    return total


def project_kernel(
    clean_hbm, corrupt_hbm, cot_hbm, mask_ref, wq_hbm, wk_hbm, wv_hbm,
    msg_out, patched_out, up_out, down_out,
    msg_ref, patched_ref, up_ref, down_ref,
    hidden_ref, mask_col, clean_ref, corrupt_ref, wq_ref, wk_ref, wv_ref, sems, out_sems,
):
    half = RIM // 2
    copies = [
        pltpu.make_async_copy(source, target, sems.at[i])
        for i, (source, target) in enumerate((
            (clean_hbm, clean_ref),
            (corrupt_hbm, corrupt_ref),
            (wk_hbm, wk_ref),
            (wv_hbm, wv_ref),
            (wq_hbm, wq_ref),
            (cot_hbm.at[pl.ds(ROWS - half, half)], up_ref.at[pl.ds(RIM + half, half)]),
            (cot_hbm.at[pl.ds(0, half)], down_ref.at[pl.ds(RIM + half, half)]),
        ))
    ]
    for copy in copies:
        copy.start()
    spread_mask = jnp.broadcast_to(mask_ref[...].astype(F32), (ROWS, ROWS))
    mask_col[...] = spread_mask.T
    copies[0].wait()
    copies[1].wait()

    def rows(i, carry):
        at = pl.ds(pl.multiple_of(i * 16, 16), 16)
        below = pl.ds(pl.multiple_of(ROWS + i * 16, 16), 16)
        clean = clean_ref[at, :].astype(F32)
        corrupt = corrupt_ref[at, :].astype(F32)
        patched = jnp.where(mask_col[at, 0:1] == 1.0, corrupt, clean)
        patched_ref[at, :] = patched.astype(BF16)
        for dest, source in ((at, clean), (below, patched)):
            centred, inverse = moments(source)
            hidden_ref[dest, :] = (centred * inverse).astype(BF16)
        return carry

    lax.fori_loop(0, ROWS // 16, rows, 0, unroll=UNROLL)
    up_ref[0:RIM, :] = clean_ref[ROWS - RIM : ROWS, :]
    up_ref[RIM : RIM + half, :] = patched_ref[ROWS - half : ROWS, :]
    down_ref[0:RIM, :] = clean_ref[0:RIM, :]
    down_ref[RIM : RIM + half, :] = patched_ref[0:half, :]
    for copy in copies[2:]:
        copy.wait()
    results = [
        pltpu.make_async_copy(source, target, out_sems.at[i])
        for i, (source, target) in enumerate((
            (up_ref, up_out), (down_ref, down_out), (patched_ref, patched_out),
            *(
                (msg_ref.at[pl.ds(at, 8)], msg_out.at[pl.ds(at, 8)])
                for at in (0, 16, 8, 24)
            ),
        ))
    ]
    for copy in results[:3]:
        copy.start()

    low = lane_of(ROWS) < 64
    low_q = lane_of(64) < 64
    for pair in range(2):
        cols = slice(pair * 256, pair * 256 + 256)
        hidden = hidden_ref[...]
        query = dot(hidden, wq_ref[:, cols])
        keys = dot(hidden, wk_ref[:, cols])
        values = dot(hidden, wv_ref[:, cols])
        for sub in range(2):
            tile = slice(sub * 128, sub * 128 + 128)
            for run in range(2):
                part = slice(run * ROWS, run * ROWS + ROWS)
                k, v, q = keys[part, tile], values[part, tile], query[part, tile]
                base = run * 16 + (pair * 2 + sub) * 4
                kv = (jnp.where(low, k, swap(v)).astype(BF16), jnp.where(low, swap(k), v).astype(BF16))
                early, late = q[:64], q[64:]
                asked = (
                    jnp.where(low_q, early, swap(late)).astype(BF16),
                    jnp.where(low_q, swap(early), late).astype(BF16),
                )
                for odd in range(2):
                    for side in range(2):
                        dest = base + odd * 2 + side
                        msg_ref[dest, 0:64, :] = kv[odd][side * 64 : side * 64 + 64]
                        msg_ref[dest, 64:128, :] = asked[odd]
        results[3 + 2 * pair].start()
        results[4 + 2 * pair].start()
    for copy in results:
        copy.wait()


def attend_kernel(
    scal_ref, recv_ref, out_ref, k_ref, vt_ref, qt_ref, s0_ref, s1_ref, c_ref, r_ref
):
    length, side = scal_ref[1], scal_ref[3]
    sources = recv_ref.shape[0]
    lane = lane_of(128)
    row = lax.broadcasted_iota(jnp.int32, (128, 128), 0)
    scale = DH ** (-0.5) * LOG2E

    def load(s, carry):
        at = pl.multiple_of(s * 128, 128)
        kv = recv_ref[pl.ds(2 * s, 2), 0:64, :].astype(F32).reshape(128, 128)
        frame = (2 * s + row // 64) * ROWS + side * 64 + row % 64
        bias = jnp.where(frame < length, 0.0, FLOOR)
        keyed = jnp.where(lane < 64, kv, jnp.where(lane == 64, bias, 0.0))
        k_ref[pl.ds(at, 128), :] = keyed.astype(BF16)
        vt_ref[0:64, pl.ds(at, 128)] = kv.T[64:128].astype(BF16)
        vt_ref[64:80, pl.ds(at, 128)] = jnp.ones((16, 128), BF16)
        raw = recv_ref[pl.ds(2 * s, 2), 64:128, :].astype(F32).reshape(128, 128).T
        fill = jnp.where(row == 64, 1.0, 0.0)
        other = jnp.concatenate([raw[64:], raw[:64]], axis=0)
        at = pl.multiple_of(s * 256, 256)
        qt_ref[:, pl.ds(at, 128)] = jnp.where(row < 64, raw, fill).astype(BF16)
        qt_ref[:, pl.ds(at + 128, 128)] = jnp.where(row < 64, other, fill).astype(BF16)
        return carry

    lax.fori_loop(0, sources // 2, load, 0, unroll=LOAD_UNROLL)

    many = s0_ref.shape[1]
    chunk = CHUNK
    pieces = k_ref.shape[0] // chunk
    blocks = sources * ROWS // many

    def score_piece(query, s_ref, k, top):
        at = slice(k * chunk, k * chunk + chunk)
        scores = dot(k_ref[at, :], query)
        s_ref[at, :] = scores
        best = jnp.max(scores.reshape(chunk // 8, 8, many), axis=0)
        return best if top is None else jnp.maximum(top, best)

    def weigh_piece(s_ref, best, k, accum):
        at = slice(k * chunk, k * chunk + chunk)
        weights = jnp.exp2((s_ref[at, :] - best) * scale).astype(BF16)
        addend = dot(vt_ref[:, at], weights)
        return addend if accum is None else accum + addend

    def finish(top):
        return jnp.max(top, axis=0, keepdims=True)

    def queries(b):
        return qt_ref[:, pl.ds(pl.multiple_of(b * many, many), many)]

    low8 = lane_of(8) < 64

    def store(b, accum, best):
        total = accum[64:65, :]
        result = accum[0:64, :] / total
        level = jnp.broadcast_to(best * scale + jnp.log2(total), (8, many))
        for g in range(many // 256):
            first = slice(g * 256, g * 256 + 128)
            second = slice(g * 256 + 128, g * 256 + 256)
            both = jnp.concatenate([result[:, first], result[:, second]], axis=0)
            at = b * (many // 256) + g
            c_ref[pl.ds(pl.multiple_of(at * 128, 128), 128), :] = both.T
            early, late = level[:, first], level[:, second]
            r_ref[pl.ds(pl.multiple_of(at * 16, 16), 8), :] = jnp.where(low8, early, swap(late))
            r_ref[pl.ds(pl.multiple_of(at * 16 + 8, 8), 8), :] = jnp.where(low8, swap(early), late)

    def step(b, s_ref, best, next_b, next_s):
        query = None if next_s is None else queries(next_b)
        top, accum = None, None
        for k in range(pieces):
            if query is not None:
                top = score_piece(query, next_s, k, top)
            accum = weigh_piece(s_ref, best, k, accum)
        store(b, accum, best)
        return None if query is None else finish(top)

    query, top = queries(0), None
    for k in range(pieces):
        top = score_piece(query, s0_ref, k, top)

    def pair(i, best):
        best = step(2 * i, s0_ref, best, 2 * i + 1, s1_ref)
        return step(2 * i + 1, s1_ref, best, 2 * i + 2, s0_ref)

    best = lax.fori_loop(0, blocks // 2 - 1, pair, finish(top))
    best = step(blocks - 2, s0_ref, best, blocks - 1, s1_ref)
    step(blocks - 1, s1_ref, best, None, None)

    low32 = lane_of(32) < 64
    row8 = lax.broadcasted_iota(jnp.int32, (8, 128), 0)

    def pack(d, carry):
        after = lax.rem(d + 1, sources)
        before = lax.rem(d + sources - 1, sources)
        out_ref[d, 0:64, :] = c_ref[pl.ds(pl.multiple_of(d * 64, 64), 64), :].astype(BF16)
        right = c_ref[pl.ds(pl.multiple_of(after * 64, 64), 32), :]
        left = c_ref[pl.ds(pl.multiple_of(before * 64 + 32, 32), 32), :]
        out_ref[d, 64:96, :] = jnp.where(low32, right, left).astype(BF16)
        own = r_ref[pl.ds(pl.multiple_of(d * 8, 8), 8), :]
        rim = jnp.where(
            low8,
            r_ref[pl.ds(pl.multiple_of(after * 8, 8), 8), :],
            r_ref[pl.ds(pl.multiple_of(before * 8, 8), 8), :],
        )
        rows = jnp.where(row8 < 3, own, rim)
        high = rows.astype(BF16).astype(F32)
        rest = rows - high
        middle = rest.astype(BF16).astype(F32)
        last = rest - middle
        level = row8 % 3
        rows = jnp.where(level == 0, high, jnp.where(level == 1, middle, last))
        out_ref[d, 96:112, :] = jnp.concatenate([rows, rows], axis=0).astype(BF16)
        return carry

    lax.fori_loop(0, sources, pack, 0, unroll=PACK_UNROLL)


def depthwise(source, source_row, taps_ref, order, target, count):
    def rows(i, carry):
        first = source_row + i * 8
        taps = [taps_ref[t * 8 : t * 8 + 8, :] for t in order]
        sums = [None] * 8
        for s in range(KERNEL + 7):
            piece = source[pl.ds(pl.multiple_of((first + s) * 8, 8), 8), :]
            for o in range(8):
                if 0 <= s - o < KERNEL:
                    term = taps[s - o] * piece
                    sums[o] = term if sums[o] is None else sums[o] + term
        for o in range(8):
            target[pl.ds(pl.multiple_of((i * 8 + o) * 8, 8), 8), :] = sums[o]
        return carry

    lax.fori_loop(0, count // 8, rows, 0, unroll=TAP_UNROLL)


def put_rows(ref, row, tile, values):
    for r in range(0, values.shape[0], 8):
        ref[pl.ds((row + r) * 8 + tile, 8, stride=8), :] = values[r : r + 8]


def get_rows(ref, row, count):
    groups = []
    for r in range(0, count, 8):
        tiles = [ref[pl.ds((row + r) * 8 + t, 8, stride=8), :] for t in range(8)]
        groups.append(jnp.concatenate(tiles, axis=1))
    return jnp.concatenate(groups, axis=0) if len(groups) > 1 else groups[0]


def place_context(ctx_in, base, ctx_ref, rim):
    row8 = lax.broadcasted_iota(jnp.int32, (8, 128), 0)
    zero = jnp.zeros((8, 128), F32)
    levels = [[zero, zero], [zero, zero]]
    for h in range(HEADS):
        for side in range(2):
            block = ctx_in[base + h * 2 + side, 96:112, :].astype(F32)
            for kind in range(2):
                at = kind * 3
                level = block[at : at + 1] + block[at + 1 : at + 2] + block[at + 2 : at + 3]
                levels[kind][side] = jnp.where(row8 == h, level, levels[kind][side])
    shares = []
    for first, second in levels:
        shares.append(1.0 / (1.0 + jnp.exp2(second - first)))
        shares.append(1.0 / (1.0 + jnp.exp2(first - second)))
    share = jnp.concatenate(shares + [jnp.zeros((96, 128), F32)], axis=0).T
    low = lane_of(96) < 64
    low_rows = lane_of(ROWS) < 64
    for t in range(HEADS // 2):
        at = slice(t * 128, t * 128 + 128)
        own = left = right = None
        for side in range(2):
            even = ctx_in[base + t * 4 + side, 0:96, :].astype(F32)
            odd = ctx_in[base + t * 4 + 2 + side, 0:96, :].astype(F32)
            first = jnp.where(low, even, swap(odd))
            second = jnp.where(low, swap(even), odd)
            scale = []
            for kind in range(2):
                column = kind * 16 + side * 8 + 2 * t
                scale.append(jnp.where(
                    low_rows, share[:, column : column + 1], share[:, column + 1 : column + 2]
                ))
            part = jnp.concatenate([first[:64], second[:64]], axis=0) * scale[0]
            after = first[64:96] * scale[1][0:32]
            before = second[64:96] * scale[1][96:128]
            own = part if own is None else own + part
            left = before if left is None else left + before
            right = after if right is None else right + after
        ctx_ref[0:rim, at] = left[RIM - rim :].astype(BF16)
        ctx_ref[rim : rim + ROWS, at] = own.astype(BF16)
        ctx_ref[rim + ROWS :, at] = right[:rim].astype(BF16)


def place_taps(depth_ref, taps_ref):
    for r in range(0, KERNEL + 1, 8):
        got = min(8, KERNEL - r)
        block = depth_ref[r : r + got, :].astype(F32)
        if got < 8:
            block = jnp.concatenate([block, jnp.zeros((8 - got, WIDTH), F32)], axis=0)
        for t in range(8):
            put_rows(taps_ref, r, t, block[:, t * 128 : t * 128 + 128])


def to_lowered(x_ref, ctx_ref, wao_ref, resid_ref, low_ref):
    for j in range(4):
        at = slice(j * 256, j * 256 + 256)
        joined = x_ref[:, at].astype(F32) + dot(ctx_ref[...], wao_ref[:, at])
        resid_ref[:, at] = joined.astype(BF16)

    def lower(i, carry):
        at = pl.ds(pl.multiple_of(i * 16, 16), 16)
        centred, inverse = moments(resid_ref[at, :].astype(F32))
        low_ref[at, :] = (centred * inverse).astype(BF16)
        return carry

    lax.fori_loop(0, x_ref.shape[0] // 16, lower, 0, unroll=UNROLL)


def to_gated(low_ref, win_ref, g2_ref, frame, length, keep, arrivals=None):
    live = jnp.where((frame >= 0) & (frame < length), 1.0, 0.0)
    for j in range(4):
        at = slice(j * 256, j * 256 + 256)
        gate_at = slice(WIDTH + j * 256, WIDTH + j * 256 + 256)
        if arrivals is not None:
            arrivals[2 * j].wait()
            arrivals[2 * j + 1].wait()
        value = dot(low_ref[...], win_ref[:, at])
        gate = sigmoid(dot(low_ref[...], win_ref[:, gate_at]))
        if keep is not None:
            mv_ref, sg_ref = keep
            mv_ref[:, at] = value[RIM : RIM + ROWS]
            sg_ref[:, at] = gate[RIM : RIM + ROWS]
        gated = (value * gate * live).astype(BF16).astype(F32)
        for t in range(2):
            put_rows(g2_ref, 0, j * 2 + t, gated[:, t * 128 : t * 128 + 128])


def clean_kernel(
    scal_ref, ctx_hbm, clean_hbm, cot_hbm, up_hbm, down_hbm,
    wao_hbm, win_hbm, depth_hbm, wout_hbm,
    own_out, pack_out, sw_out, gs_out, gg2_out, g2_out, resid_out,
    ctx_in, wao_ref, win_ref, depth_ref, wout_ref,
    own_ref, pack_ref, sw_ref, gs_ref, gg2_ref, g2_ref, resid_ref,
    ctx_ref, x_ref, low_ref, mv_ref, sg_ref, s2_ref, zed_ref, zinv_ref, gox_ref, gsp2_ref, taps_ref,
    in_sems, out_sems,
):
    first_frame, length, core = scal_ref[0], scal_ref[1], scal_ref[2]
    half = RIM // 2
    copies = [
        pltpu.make_async_copy(source, target, in_sems.at[i])
        for i, (source, target) in enumerate((
            (ctx_hbm.at[pl.ds(0, 16)], ctx_in),
            (up_hbm.at[pl.ds(0, RIM)], x_ref.at[pl.ds(0, RIM)]),
            (clean_hbm, x_ref.at[pl.ds(RIM, ROWS)]),
            (down_hbm.at[pl.ds(0, RIM)], x_ref.at[pl.ds(RIM + ROWS, RIM)]),
            (wao_hbm, wao_ref),
            (depth_hbm, depth_ref),
            (up_hbm.at[pl.ds(RIM + half, half)], gox_ref.at[pl.ds(0, half)]),
            (cot_hbm, gox_ref.at[pl.ds(half, ROWS)]),
            (down_hbm.at[pl.ds(RIM + half, half)], gox_ref.at[pl.ds(half + ROWS, half)]),
            *(
                (win_hbm.at[:, pl.ds(at, 256)], win_ref.at[:, pl.ds(at, 256)])
                for j in range(0, WIDTH, 256)
                for at in (j, WIDTH + j)
            ),
            (wout_hbm, wout_ref),
        ))
    ]
    for copy in copies:
        copy.start()
    results = [
        pltpu.make_async_copy(source, target, out_sems.at[i])
        for i, (source, target) in enumerate((
            (own_ref, own_out),
            *(
                (pack_ref.at[:, pl.ds(at, size)], pack_out.at[:, pl.ds(at, size)])
                for at, size in ((0, WIDTH), (GM, 2 * WIDTH), (GO, WIDTH))
            ),
            (sw_ref, sw_out), (gs_ref, gs_out), (gg2_ref, gg2_out), (g2_ref, g2_out),
            (resid_ref, resid_out),
        ))
    ]
    own_copy, send_copy, gm_copy, go_copy, sw_copy, gs_copy, gg2_copy, g2_copy, resid_copy = results
    copies[0].wait()
    place_context(ctx_in, 0, ctx_ref, RIM)
    for copy in copies[1:9]:
        copy.wait()
    place_taps(depth_ref, taps_ref)
    for row in range(0, INNER, 16):
        at = slice(row, row + 16)
        frame = first_frame - half + row + lax.broadcasted_iota(jnp.int32, (16, 1), 0)
        gox_ref[at, :] = (gox_ref[at, :].astype(F32) * jnp.where(frame < length, 1.0, 0.0)).astype(BF16)
    pack_ref[:, GO:] = gox_ref[half : half + ROWS, :]
    go_copy.start()

    to_lowered(x_ref, ctx_ref, wao_ref, resid_ref, low_ref)
    resid_copy.start()
    frame = first_frame - RIM + lax.broadcasted_iota(jnp.int32, (CLEAN, 1), 0)
    to_gated(low_ref, win_ref, g2_ref, frame, length, (mv_ref, sg_ref), copies[9:17])
    g2_copy.start()
    forward = list(range(KERNEL))
    edge = half - KERNEL // 2
    depthwise(g2_ref, edge, taps_ref, forward, s2_ref, INNER)

    def clean_rows(i, carry):
        r = pl.multiple_of(i * 16, 16)
        centred, inverse = moments(get_rows(s2_ref, r, 16))
        zed = centred * inverse
        zed_ref[pl.ds(r, 16), :] = zed
        zinv_ref[pl.ds(r, 16), :] = jnp.broadcast_to(inverse, (16, 128))
        sw_ref[pl.ds(r, 16), :] = (zed * sigmoid(zed)).astype(BF16)
        return carry

    lax.fori_loop(0, INNER // 16, clean_rows, 0, unroll=UNROLL)
    sw_copy.start()

    for part in range(4):
        dest = part * 256
        source, row = (low_ref, RIM) if part < 2 else (sw_ref, half)
        lo = (part % 2) * 512
        first = source[row : row + ROWS, lo : lo + 256].astype(F32)
        second = source[row : row + ROWS, lo + 256 : lo + 512].astype(F32)
        own_ref[:, dest : dest + 256] = jnp.where(core == 0, first, second).astype(BF16)
        pack_ref[:, dest : dest + 256] = jnp.where(core == 0, second, first).astype(BF16)
    own_copy.start()
    send_copy.start()

    copies[17].wait()
    for j in range(4):
        at = slice(j * 256, j * 256 + 256)
        gs_ref[:, at] = dot_nt(gox_ref[...], wout_ref[at, :])
    gs_copy.start()

    def back_rows(i, carry):
        r = pl.multiple_of(i * 16, 16)
        zed = zed_ref[pl.ds(r, 16), :]
        grad = gs_ref[pl.ds(r, 16), :]
        gate = sigmoid(zed)
        grad_zed = grad * (gate * (1.0 + zed * (1.0 - gate)))
        mean = jnp.mean(grad_zed, axis=-1, keepdims=True)
        along = jnp.mean(grad_zed * zed, axis=-1, keepdims=True)
        result = (grad_zed - mean - zed * along) * zinv_ref[pl.ds(r, 16), 0:1]
        for g in range(0, 16, 8):
            for t in range(8):
                gsp2_ref[pl.ds((r + g) * 8 + t, 8, stride=8), :] = result[
                    g : g + 8, t * 128 : t * 128 + 128
                ]
        return carry

    lax.fori_loop(0, INNER // 16, back_rows, 0, unroll=UNROLL)
    depthwise(gsp2_ref, edge, taps_ref, forward[::-1], gg2_ref, ROWS)
    gg2_copy.start()

    def mixed_rows(i, carry):
        r = pl.multiple_of(i * 16, 16)
        at = pl.ds(r, 16)
        frame = first_frame + r + lax.broadcasted_iota(jnp.int32, (16, 1), 0)
        grad = get_rows(gg2_ref, r, 16) * jnp.where(frame < length, 1.0, 0.0)
        gate = sg_ref[at, :]
        pack_ref[at, GM : GM + WIDTH] = (grad * gate).astype(BF16)
        pack_ref[at, GM + WIDTH : GO] = (grad * mv_ref[at, :] * gate * (1.0 - gate)).astype(BF16)
        return carry

    lax.fori_loop(0, ROWS // 16, mixed_rows, 0, unroll=UNROLL)

    gm_copy.start()
    for copy in results:
        copy.wait()


def patch_kernel(
    scal_ref, site_ref, ctx_in, patched_ref, up_ref, down_ref,
    wao_ref, win_ref, depth_ref, wout_ref,
    pack_ref, swc_ref, gs_ref, gg2_ref, g2c_ref, residc_ref,
    attr_ref,
    ctx_ref, x_ref, resid_ref, low_ref, g2_ref, s2_ref, sw_ref, gl_ref, t0_ref, t1_ref, t2_ref, taps_ref,
):
    first_frame, length = scal_ref[0], scal_ref[1]
    half = RIM // 2
    place_context(ctx_in, 16, ctx_ref, half)
    x_ref[0:half, :] = up_ref[RIM : RIM + half, :]
    x_ref[half : half + ROWS, :] = patched_ref[...]
    x_ref[half + ROWS : PATCH, :] = down_ref[RIM : RIM + half, :]
    place_taps(depth_ref, taps_ref)
    to_lowered(x_ref, ctx_ref, wao_ref, resid_ref, low_ref)
    frame = first_frame - half + lax.broadcasted_iota(jnp.int32, (PATCH, 1), 0)
    to_gated(low_ref, win_ref, g2_ref, frame, length, None)
    depthwise(g2_ref, half - KERNEL // 2, taps_ref, list(range(KERNEL)), s2_ref, ROWS)
    sw_ref[0:ROWS, :] = swc_ref[half : half + ROWS, :]

    def patch_rows(i, carry):
        r = pl.multiple_of(i * 16, 16)
        at = pl.ds(r, 16)
        inner = pl.ds(pl.multiple_of(half + r, 16), 16)
        centred, inverse = moments(get_rows(s2_ref, r, 16))
        zed = centred * inverse
        swished = (zed * sigmoid(zed)).astype(BF16)
        sw_ref[pl.ds(pl.multiple_of(ROWS + r, 16), 16), :] = swished
        gap = swished.astype(F32) - sw_ref[at, :].astype(F32)
        t2_ref[at, :] = lane_sum(gap * gs_ref[inner, :])
        frame = first_frame + r + lax.broadcasted_iota(jnp.int32, (16, 1), 0)
        grad = get_rows(gg2_ref, r, 16) * jnp.where(frame < length, 1.0, 0.0)
        gap = get_rows(g2_ref, half + r, 16) - get_rows(g2c_ref, RIM + r, 16)
        t1_ref[at, :] = lane_sum(gap * grad)
        return carry

    lax.fori_loop(0, ROWS // 16, patch_rows, 0, unroll=UNROLL)

    t3 = jnp.zeros((ROWS, 128), F32)
    for j in range(4):
        at = slice(j * 256, j * 256 + 256)
        out = dot(sw_ref[...], wout_ref[:, at])
        out_clean = residc_ref[RIM : RIM + ROWS, at].astype(F32) + out[:ROWS]
        out_patch = resid_ref[half : half + ROWS, at].astype(F32) + out[ROWS:]
        gap = out_patch.astype(BF16).astype(F32) - out_clean.astype(BF16).astype(F32)
        t3 = t3 + lane_sum(gap * pack_ref[:, GO + j * 256 : GO + j * 256 + 256].astype(F32))
    for j in range(4):
        at = slice(j * 256, j * 256 + 256)
        gl_ref[:, at] = dot_nt(pack_ref[:, GM:GO], win_ref[at, :])

    def resid_rows(i, carry):
        r = pl.multiple_of(i * 16, 16)
        at = pl.ds(r, 16)
        clean = residc_ref[pl.ds(pl.multiple_of(RIM + r, 16), 16), :].astype(F32)
        patch = resid_ref[pl.ds(pl.multiple_of(half + r, 16), 16), :].astype(F32)
        centred, inverse = moments(clean)
        normed = centred * inverse
        grad = gl_ref[at, :]
        mean = jnp.mean(grad, axis=-1, keepdims=True)
        along = jnp.mean(grad * normed, axis=-1, keepdims=True)
        grad_resid = pack_ref[at, GO:].astype(F32) + (grad - mean - normed * along) * inverse
        t0_ref[at, :] = lane_sum((patch - clean) * grad_resid)
        return carry

    lax.fori_loop(0, ROWS // 16, resid_rows, 0, unroll=UNROLL)

    columns = [
        jnp.sum(part, axis=1, keepdims=True) for part in (t0_ref[...], t1_ref[...], t2_ref[...], t3)
    ]
    lane = lane_of(ROWS)
    chosen = jnp.zeros((ROWS, 128), F32)
    for i in range(attr_ref.shape[0]):
        site = site_ref[i]
        column = columns[0]
        for k in range(1, 4):
            column = jnp.where(site == k, columns[k], column)
        chosen = jnp.where(lane == i, column, chosen)
    attr_ref[...] = chosen.T[: attr_ref.shape[0]]


def weight_kernel(
    own_hbm, pack_hbm, other_hbm, out_hbm,
    left_ref, gm_ref, go_ref, out_ref, in_sems, out_sems,
):
    pairs = (
        (own_hbm, left_ref, 0),
        (other_hbm.at[:, pl.ds(0, WIDTH)], left_ref, ROWS),
        (pack_hbm.at[:, pl.ds(GO, WIDTH)], go_ref, 0),
        (other_hbm.at[:, pl.ds(GO, WIDTH)], go_ref, ROWS),
        (pack_hbm.at[:, pl.ds(GM, 2 * WIDTH)], gm_ref, 0),
        (other_hbm.at[:, pl.ds(GM, 2 * WIDTH)], gm_ref, ROWS),
    )
    copies = [
        pltpu.make_async_copy(source, target.at[pl.ds(row, ROWS)], in_sems.at[i])
        for i, (source, target, row) in enumerate(pairs)
    ]
    for copy in copies:
        copy.start()

    def send(i):
        at = pl.ds(i * 512, 512)
        return pltpu.make_async_copy(out_ref.at[:, :, at], out_hbm.at[:, :, at], out_sems.at[i])

    def put(at, product):
        half = product.shape[0] // 2
        lower = product[:half].reshape(half // 8, 8, 256)
        upper = product[half:].reshape(half // 8, 8, 256)
        out_ref[:, :, at : at + 256] = jnp.concatenate([lower, upper], axis=1).astype(BF16)

    for copy in copies[:4]:
        copy.wait()
    swished = left_ref[:, WIDTH // 2 :].T
    for j in range(0, WIDTH, 256):
        put(2 * WIDTH + j, dot(swished, go_ref[:, j : j + 256]))
        if j % 512:
            send(4 + j // 512).start()
    for copy in copies[4:]:
        copy.wait()
    low = left_ref[:, : WIDTH // 2].T
    for j in range(0, 2 * WIDTH, 256):
        put(j, dot(low, gm_ref[:, j : j + 256]))
        if j % 512:
            send(j // 512).start()
    for i in range(6):
        send(i).wait()


def fold_kernel(scal_ref, pieces_ref, mine_ref, theirs_ref):
    upper = scal_ref[4]

    def fold(at):
        total = pieces_ref[0, :, at].astype(F32)
        for k in range(1, pieces_ref.shape[0]):
            total = total + pieces_ref[k, :, at].astype(F32)
        first, second = total[:8], total[8:]
        mine_ref[:, at] = jnp.where(upper == 0, first, second)
        return jnp.where(upper == 0, second, first)

    middle = theirs_ref.shape[1]
    for j in range(0, middle, 256):
        low = fold(slice(j, j + 256))
        high = fold(slice(middle + j, middle + j + 256))
        theirs_ref[:, j : j + 256] = jnp.concatenate([low, high], axis=0).astype(BF16)


def join_kernel(mine_ref, theirs_ref, in_ref, out_ref):
    theirs = theirs_ref[...].astype(F32)
    whole = mine_ref[...] + jnp.concatenate([theirs[:8], theirs[8:]], axis=1)
    in_ref[...] = whole[:, : 2 * WIDTH]
    out_ref[...] = whole[:, 2 * WIDTH :]


VMEM = pl.BlockSpec(memory_space=pltpu.VMEM)
SMEM = pl.BlockSpec(memory_space=pltpu.SMEM)
HBM = pl.BlockSpec(memory_space=pltpu.HBM)


def kernel_call(body, out_shape, in_specs, scratch, limit, flops, moved, out_spec=VMEM):
    return pl.pallas_call(
        body,
        out_shape=out_shape,
        in_specs=in_specs,
        out_specs=[out_spec] * len(out_shape),
        scratch_shapes=scratch,
        compiler_params=pltpu.CompilerParams(vmem_limit_bytes=limit << 20),
        cost_estimate=pl.CostEstimate(flops=flops, bytes_accessed=moved, transcendentals=0),
    )


def shape(dims, dtype):
    return jax.ShapeDtypeStruct(dims, dtype)


def per_device(
    clean_input, corrupt_input, patch_mask, lengths, site_ids, w_query, w_key, w_value,
    w_attn_out, w_pointwise_in, depth_kernel, w_pointwise_out, cotangent,
):
    frames = lax.axis_size("frames")
    position = lax.axis_index("frames")
    core = lax.rem(lax.axis_index("dp"), 2)
    scalars = jnp.stack(
        [position * ROWS, lengths[0], core, lax.rem(position, 2), lax.axis_index("dp") // 2]
    ).astype(jnp.int32)
    clean, corrupt, cot = clean_input[0], corrupt_input[0], cotangent[0]

    msg, patched, up, down = kernel_call(
        project_kernel,
        [shape((frames, ROWS, 128), BF16), shape((ROWS, WIDTH), BF16),
         shape((2 * RIM, WIDTH), BF16), shape((2 * RIM, WIDTH), BF16)],
        [HBM] * 3 + [VMEM] + [HBM] * 3,
        [pltpu.VMEM((frames, ROWS, 128), BF16), pltpu.VMEM((ROWS, WIDTH), BF16),
         pltpu.VMEM((2 * RIM, WIDTH), BF16), pltpu.VMEM((2 * RIM, WIDTH), BF16),
         pltpu.VMEM((2 * ROWS, WIDTH), BF16), pltpu.VMEM((ROWS, ROWS), F32),
         pltpu.VMEM((ROWS, WIDTH), BF16), pltpu.VMEM((ROWS, WIDTH), BF16),
         pltpu.VMEM((WIDTH, 512), BF16), pltpu.VMEM((WIDTH, 512), BF16),
         pltpu.VMEM((WIDTH, 512), BF16), pltpu.SemaphoreType.DMA((7,)), pltpu.SemaphoreType.DMA((7,))],
        62, 8 * 10**8, 6 * 10**6, HBM,
    )(clean, corrupt, cot, patch_mask, w_query, w_key, w_value)
    forward = [(i, i + 1) for i in range(frames - 1)]
    backward = [(i + 1, i) for i in range(frames - 1)]
    from_left = lax.ppermute(up, "frames", forward)
    from_right = lax.ppermute(down, "frames", backward)
    recv = lax.all_to_all(msg, "frames", 0, 0, tiled=True)
    recv, from_left, from_right = lax.optimization_barrier((recv, from_left, from_right))
    keys = frames * ROWS // 2
    (context,) = kernel_call(
        attend_kernel,
        [shape((frames, 112, 128), BF16)],
        [SMEM, VMEM],
        [pltpu.VMEM((keys, 128), BF16), pltpu.VMEM((80, keys), BF16),
         pltpu.VMEM((128, 2 * keys), BF16),
         pltpu.VMEM((keys, 512), F32), pltpu.VMEM((keys, 512), F32),
         pltpu.VMEM((frames * 64, 128), F32), pltpu.VMEM((frames * 8, 128), F32)],
        20, 8 * 10**9, 10**6,
    )(scalars, recv)
    contexts = lax.all_to_all(context, "frames", 0, 0, tiled=True)
    own, pack, swished, grad_swished, grad_gated, gated, resid = kernel_call(
        clean_kernel,
        [shape((ROWS, WIDTH), BF16), shape((ROWS, 4 * WIDTH), BF16),
         shape((INNER, WIDTH), BF16), shape((INNER, WIDTH), F32),
         shape((ROWS * 8, 128), F32), shape((CLEAN * 8, 128), F32), shape((CLEAN, WIDTH), BF16)],
        [SMEM] + [HBM] * 9,
        [pltpu.VMEM((16, 112, 128), BF16), pltpu.VMEM((512, WIDTH), BF16),
         pltpu.VMEM((WIDTH, 2 * WIDTH), BF16), pltpu.VMEM((KERNEL, WIDTH), BF16),
         pltpu.VMEM((WIDTH, WIDTH), BF16),
         pltpu.VMEM((ROWS, WIDTH), BF16), pltpu.VMEM((ROWS, 4 * WIDTH), BF16),
         pltpu.VMEM((INNER, WIDTH), BF16), pltpu.VMEM((INNER, WIDTH), F32),
         pltpu.VMEM((ROWS * 8, 128), F32), pltpu.VMEM((CLEAN * 8, 128), F32),
         pltpu.VMEM((CLEAN, WIDTH), BF16),
         pltpu.VMEM((CLEAN, 512), BF16), pltpu.VMEM((CLEAN, WIDTH), BF16),
         pltpu.VMEM((CLEAN, WIDTH), BF16),
         pltpu.VMEM((ROWS, WIDTH), F32), pltpu.VMEM((ROWS, WIDTH), F32),
         pltpu.VMEM((INNER * 8, 128), F32), pltpu.VMEM((INNER, WIDTH), F32),
         pltpu.VMEM((INNER, 128), F32), pltpu.VMEM((INNER, WIDTH), BF16),
         pltpu.VMEM((INNER * 8, 128), F32), pltpu.VMEM((32 * 8, 128), F32),
         pltpu.SemaphoreType.DMA((18,)), pltpu.SemaphoreType.DMA((9,))],
        59, 3 * 10**9, 10**7, HBM,
    )(scalars, contexts, clean, cot, from_left, from_right,
      w_attn_out, w_pointwise_in, depth_kernel, w_pointwise_out)

    cores = [(i, i ^ 1) for i in range(lax.axis_size("dp"))]
    other = lax.ppermute(pack, "dp", cores)
    (partial,) = kernel_call(
        weight_kernel,
        [shape((frames, 16, 3 * WIDTH), BF16)],
        [HBM] * 3,
        [pltpu.VMEM((2 * ROWS, WIDTH), BF16), pltpu.VMEM((2 * ROWS, 2 * WIDTH), BF16),
         pltpu.VMEM((2 * ROWS, WIDTH), BF16), pltpu.VMEM((frames, 16, 3 * WIDTH), BF16),
         pltpu.SemaphoreType.DMA((6,)), pltpu.SemaphoreType.DMA((6,))],
        59, 8 * 10**8, 10**7, HBM,
    )(own, pack, other)
    pieces = lax.all_to_all(partial, "frames", 0, 0, tiled=True)
    (attribution,) = kernel_call(
        patch_kernel,
        [shape((site_ids.shape[0], ROWS), F32)],
        [SMEM, SMEM] + [VMEM] * 14,
        [pltpu.VMEM((PATCH, 512), BF16), pltpu.VMEM((PATCH, WIDTH), BF16),
         pltpu.VMEM((PATCH, WIDTH), BF16), pltpu.VMEM((PATCH, WIDTH), BF16),
         pltpu.VMEM((PATCH * 8, 128), F32), pltpu.VMEM((ROWS * 8, 128), F32),
         pltpu.VMEM((2 * ROWS, WIDTH), BF16), pltpu.VMEM((ROWS, WIDTH), F32),
         pltpu.VMEM((ROWS, 128), F32), pltpu.VMEM((ROWS, 128), F32), pltpu.VMEM((ROWS, 128), F32),
         pltpu.VMEM((32 * 8, 128), F32)],
        28, 3 * 10**9, 10**7,
    )(scalars, site_ids, contexts, patched, from_left, from_right,
      w_attn_out, w_pointwise_in, depth_kernel, w_pointwise_out,
      pack, swished, grad_swished, grad_gated, gated, resid)
    pieces, attribution = lax.optimization_barrier((pieces, attribution))
    mine, theirs = kernel_call(
        fold_kernel,
        [shape((8, 3 * WIDTH), F32), shape((16, 3 * WIDTH // 2), BF16)],
        [SMEM, VMEM],
        [],
        16, 10**8, 3 * 10**6,
    )(scalars, pieces)
    half_dp = lax.axis_size("dp") // 2
    theirs = lax.ppermute(theirs, "dp", [(i, i ^ half_dp) for i in range(2 * half_dp)])
    grad_in, grad_out = kernel_call(
        join_kernel,
        [shape((8, 2 * WIDTH), F32), shape((8, WIDTH), F32)],
        [VMEM] * 2,
        [],
        16, 10**6, 10**6,
    )(mine, theirs)
    return attribution[None], grad_in, grad_out


def solution(mesh):
    placed = (
        P("dp", "frames", None), P("dp", "frames", None), P("dp", "frames"), P("dp"), P(), P(), P(),
        P(), P(), P(), P(), P(), P("dp", "frames", None),
    )
    return jax.shard_map(
        per_device,
        mesh=mesh,
        in_specs=placed,
        out_specs=(P("dp", None, "frames"), P(("dp", "frames"), None), P(("dp", "frames"), None)),
        check_vma=False,
    )
```

```python
import jax
import jax.numpy as jnp
from jax import lax
from jax.experimental import pallas as pl
from jax.experimental.pallas import tpu as pltpu
from jax.sharding import PartitionSpec as P

HEADS = 8
DH = 64
KERNEL = 31
RIM = 32
EPSILON = 1e-05
FLOOR = -1e30
LOG2E = 1.4426950408889634
F32 = jnp.float32
BF16 = jnp.bfloat16
ROWS = 128
WIDTH = 1024
CLEAN = ROWS + 2 * RIM
PATCH = ROWS + RIM
BOTH = CLEAN + PATCH
INNER = ROWS + RIM
GM = WIDTH
GO = 3 * WIDTH
UNROLL = True
TAP_UNROLL = 8
LOAD_UNROLL = 16
PACK_UNROLL = 16
CHUNK = 256


def lane_of(rows):
    return lax.broadcasted_iota(jnp.int32, (rows, 128), 1)


def swap(tile):
    return pltpu.roll(tile, 64, 1)


def moments(values):
    mean = jnp.mean(values, axis=-1, keepdims=True)
    centred = values - mean
    variance = jnp.mean(centred * centred, axis=-1, keepdims=True)
    return centred, lax.rsqrt(variance + EPSILON)


def dot(left, right):
    return jnp.dot(left, right, preferred_element_type=F32)


def dot_nt(left, right):
    return lax.dot_general(left, right, (((1,), (1,)), ((), ())), preferred_element_type=F32)


def dot_tn(left, right):
    return lax.dot_general(left, right, (((0,), (0,)), ((), ())), preferred_element_type=F32)


def sigmoid(values):
    return 0.5 * jnp.tanh(0.5 * values) + 0.5


def lane_sum(values):
    total = values[:, :128]
    for start in range(128, values.shape[1], 128):
        total = total + values[:, start : start + 128]
    return total


def project_kernel(
    clean_hbm, corrupt_hbm, cot_hbm, mask_ref, wq_hbm, wk_hbm, wv_hbm,
    msg_out, patched_out, up_out, down_out,
    msg_ref, patched_ref, up_ref, down_ref,
    hidden_ref, mask_col, clean_ref, corrupt_ref, wq_ref, wk_ref, wv_ref, sems, out_sems,
):
    half = RIM // 2
    copies = [
        pltpu.make_async_copy(source, target, sems.at[i])
        for i, (source, target) in enumerate((
            (clean_hbm, clean_ref),
            (corrupt_hbm, corrupt_ref),
            (wk_hbm, wk_ref),
            (wv_hbm, wv_ref),
            (wq_hbm, wq_ref),
            (cot_hbm.at[pl.ds(ROWS - half, half)], up_ref.at[pl.ds(RIM + half, half)]),
            (cot_hbm.at[pl.ds(0, half)], down_ref.at[pl.ds(RIM + half, half)]),
        ))
    ]
    for copy in copies:
        copy.start()
    spread_mask = jnp.broadcast_to(mask_ref[...].astype(F32), (ROWS, ROWS))
    mask_col[...] = spread_mask.T
    copies[0].wait()
    copies[1].wait()

    def rows(i, carry):
        at = pl.ds(pl.multiple_of(i * 16, 16), 16)
        below = pl.ds(pl.multiple_of(ROWS + i * 16, 16), 16)
        clean = clean_ref[at, :].astype(F32)
        corrupt = corrupt_ref[at, :].astype(F32)
        patched = jnp.where(mask_col[at, 0:1] == 1.0, corrupt, clean)
        patched_ref[at, :] = patched.astype(BF16)
        for dest, source in ((at, clean), (below, patched)):
            centred, inverse = moments(source)
            hidden_ref[dest, :] = (centred * inverse).astype(BF16)
        return carry

    lax.fori_loop(0, ROWS // 16, rows, 0, unroll=UNROLL)
    up_ref[0:RIM, :] = clean_ref[ROWS - RIM : ROWS, :]
    up_ref[RIM : RIM + half, :] = patched_ref[ROWS - half : ROWS, :]
    down_ref[0:RIM, :] = clean_ref[0:RIM, :]
    down_ref[RIM : RIM + half, :] = patched_ref[0:half, :]
    for copy in copies[2:]:
        copy.wait()
    results = [
        pltpu.make_async_copy(source, target, out_sems.at[i])
        for i, (source, target) in enumerate((
            (up_ref, up_out), (down_ref, down_out), (patched_ref, patched_out),
            *(
                (msg_ref.at[pl.ds(at, 8)], msg_out.at[pl.ds(at, 8)])
                for at in (0, 16, 8, 24)
            ),
        ))
    ]
    for copy in results[:3]:
        copy.start()

    low = lane_of(ROWS) < 64
    low_q = lane_of(64) < 64
    for pair in range(2):
        cols = slice(pair * 256, pair * 256 + 256)
        hidden = hidden_ref[...]
        query = dot(hidden, wq_ref[:, cols])
        keys = dot(hidden, wk_ref[:, cols])
        values = dot(hidden, wv_ref[:, cols])
        for sub in range(2):
            tile = slice(sub * 128, sub * 128 + 128)
            for run in range(2):
                part = slice(run * ROWS, run * ROWS + ROWS)
                k, v, q = keys[part, tile], values[part, tile], query[part, tile]
                base = run * 16 + (pair * 2 + sub) * 4
                kv = (jnp.where(low, k, swap(v)).astype(BF16), jnp.where(low, swap(k), v).astype(BF16))
                early, late = q[:64], q[64:]
                asked = (
                    jnp.where(low_q, early, swap(late)).astype(BF16),
                    jnp.where(low_q, swap(early), late).astype(BF16),
                )
                for odd in range(2):
                    for side in range(2):
                        dest = base + odd * 2 + side
                        msg_ref[dest, 0:64, :] = kv[odd][side * 64 : side * 64 + 64]
                        msg_ref[dest, 64:128, :] = asked[odd]
        results[3 + 2 * pair].start()
        results[4 + 2 * pair].start()
    for copy in results:
        copy.wait()


def attend_kernel(
    scal_ref, recv_ref, out_ref, k_ref, vt_ref, qt_ref, s0_ref, s1_ref, c_ref, r_ref
):
    length, side = scal_ref[1], scal_ref[3]
    sources = recv_ref.shape[0]
    lane = lane_of(128)
    row = lax.broadcasted_iota(jnp.int32, (128, 128), 0)
    scale = DH ** (-0.5) * LOG2E

    def load(s, carry):
        at = pl.multiple_of(s * 128, 128)
        kv = recv_ref[pl.ds(2 * s, 2), 0:64, :].astype(F32).reshape(128, 128)
        frame = (2 * s + row // 64) * ROWS + side * 64 + row % 64
        bias = jnp.where(frame < length, 0.0, FLOOR)
        keyed = jnp.where(lane < 64, kv, jnp.where(lane == 64, bias, 0.0))
        k_ref[pl.ds(at, 128), :] = keyed.astype(BF16)
        vt_ref[0:64, pl.ds(at, 128)] = kv.T[64:128].astype(BF16)
        vt_ref[64:80, pl.ds(at, 128)] = jnp.ones((16, 128), BF16)
        raw = recv_ref[pl.ds(2 * s, 2), 64:128, :].astype(F32).reshape(128, 128).T
        fill = jnp.where(row == 64, 1.0, 0.0)
        other = jnp.concatenate([raw[64:], raw[:64]], axis=0)
        at = pl.multiple_of(s * 256, 256)
        qt_ref[:, pl.ds(at, 128)] = jnp.where(row < 64, raw, fill).astype(BF16)
        qt_ref[:, pl.ds(at + 128, 128)] = jnp.where(row < 64, other, fill).astype(BF16)
        return carry

    lax.fori_loop(0, sources // 2, load, 0, unroll=LOAD_UNROLL)

    many = s0_ref.shape[1]
    chunk = CHUNK
    pieces = k_ref.shape[0] // chunk
    blocks = sources * ROWS // many

    def score_piece(query, s_ref, k, top):
        at = slice(k * chunk, k * chunk + chunk)
        scores = dot(k_ref[at, :], query)
        s_ref[at, :] = scores
        best = jnp.max(scores.reshape(chunk // 8, 8, many), axis=0)
        return best if top is None else jnp.maximum(top, best)

    def weigh_piece(s_ref, best, k, accum):
        at = slice(k * chunk, k * chunk + chunk)
        weights = jnp.exp2((s_ref[at, :] - best) * scale).astype(BF16)
        addend = dot(vt_ref[:, at], weights)
        return addend if accum is None else accum + addend

    def finish(top):
        return jnp.max(top, axis=0, keepdims=True)

    def queries(b):
        return qt_ref[:, pl.ds(pl.multiple_of(b * many, many), many)]

    low8 = lane_of(8) < 64

    def store(b, accum, best):
        total = accum[64:65, :]
        result = accum[0:64, :] / total
        level = jnp.broadcast_to(best * scale + jnp.log2(total), (8, many))
        for g in range(many // 256):
            first = slice(g * 256, g * 256 + 128)
            second = slice(g * 256 + 128, g * 256 + 256)
            both = jnp.concatenate([result[:, first], result[:, second]], axis=0)
            at = b * (many // 256) + g
            c_ref[pl.ds(pl.multiple_of(at * 128, 128), 128), :] = both.T
            early, late = level[:, first], level[:, second]
            r_ref[pl.ds(pl.multiple_of(at * 16, 16), 8), :] = jnp.where(low8, early, swap(late))
            r_ref[pl.ds(pl.multiple_of(at * 16 + 8, 8), 8), :] = jnp.where(low8, swap(early), late)

    def step(b, s_ref, best, next_b, next_s):
        query = None if next_s is None else queries(next_b)
        top, accum = None, None
        for k in range(pieces):
            if query is not None:
                top = score_piece(query, next_s, k, top)
            accum = weigh_piece(s_ref, best, k, accum)
        store(b, accum, best)
        return None if query is None else finish(top)

    query, top = queries(0), None
    for k in range(pieces):
        top = score_piece(query, s0_ref, k, top)

    def pair(i, best):
        best = step(2 * i, s0_ref, best, 2 * i + 1, s1_ref)
        return step(2 * i + 1, s1_ref, best, 2 * i + 2, s0_ref)

    best = lax.fori_loop(0, blocks // 2 - 1, pair, finish(top))
    best = step(blocks - 2, s0_ref, best, blocks - 1, s1_ref)
    step(blocks - 1, s1_ref, best, None, None)

    low32 = lane_of(32) < 64
    row8 = lax.broadcasted_iota(jnp.int32, (8, 128), 0)

    def pack(d, carry):
        after = lax.rem(d + 1, sources)
        before = lax.rem(d + sources - 1, sources)
        out_ref[d, 0:64, :] = c_ref[pl.ds(pl.multiple_of(d * 64, 64), 64), :].astype(BF16)
        right = c_ref[pl.ds(pl.multiple_of(after * 64, 64), 32), :]
        left = c_ref[pl.ds(pl.multiple_of(before * 64 + 32, 32), 32), :]
        out_ref[d, 64:96, :] = jnp.where(low32, right, left).astype(BF16)
        own = r_ref[pl.ds(pl.multiple_of(d * 8, 8), 8), :]
        rim = jnp.where(
            low8,
            r_ref[pl.ds(pl.multiple_of(after * 8, 8), 8), :],
            r_ref[pl.ds(pl.multiple_of(before * 8, 8), 8), :],
        )
        rows = jnp.where(row8 < 3, own, rim)
        high = rows.astype(BF16).astype(F32)
        rest = rows - high
        middle = rest.astype(BF16).astype(F32)
        last = rest - middle
        level = row8 % 3
        rows = jnp.where(level == 0, high, jnp.where(level == 1, middle, last))
        out_ref[d, 96:112, :] = jnp.concatenate([rows, rows], axis=0).astype(BF16)
        return carry

    lax.fori_loop(0, sources, pack, 0, unroll=PACK_UNROLL)


def depthwise(source, source_row, taps_ref, order, target, count):
    def rows(i, carry):
        first = source_row + i * 8
        taps = [taps_ref[t * 8 : t * 8 + 8, :] for t in order]
        sums = [None] * 8
        for s in range(KERNEL + 7):
            piece = source[pl.ds(pl.multiple_of((first + s) * 8, 8), 8), :]
            for o in range(8):
                if 0 <= s - o < KERNEL:
                    term = taps[s - o] * piece
                    sums[o] = term if sums[o] is None else sums[o] + term
        for o in range(8):
            target[pl.ds(pl.multiple_of((i * 8 + o) * 8, 8), 8), :] = sums[o]
        return carry

    lax.fori_loop(0, count // 8, rows, 0, unroll=TAP_UNROLL)


def put_rows(ref, row, tile, values):
    for r in range(0, values.shape[0], 8):
        ref[pl.ds((row + r) * 8 + tile, 8, stride=8), :] = values[r : r + 8]


def get_rows(ref, row, count):
    groups = []
    for r in range(0, count, 8):
        tiles = [ref[pl.ds((row + r) * 8 + t, 8, stride=8), :] for t in range(8)]
        groups.append(jnp.concatenate(tiles, axis=1))
    return jnp.concatenate(groups, axis=0) if len(groups) > 1 else groups[0]


def place_context(ctx_in, base, ctx_ref, rim):
    row8 = lax.broadcasted_iota(jnp.int32, (8, 128), 0)
    zero = jnp.zeros((8, 128), F32)
    levels = [[zero, zero], [zero, zero]]
    for h in range(HEADS):
        for side in range(2):
            block = ctx_in[base + h * 2 + side, 96:112, :].astype(F32)
            for kind in range(2):
                at = kind * 3
                level = block[at : at + 1] + block[at + 1 : at + 2] + block[at + 2 : at + 3]
                levels[kind][side] = jnp.where(row8 == h, level, levels[kind][side])
    shares = []
    for first, second in levels:
        shares.append(1.0 / (1.0 + jnp.exp2(second - first)))
        shares.append(1.0 / (1.0 + jnp.exp2(first - second)))
    share = jnp.concatenate(shares + [jnp.zeros((96, 128), F32)], axis=0).T
    low = lane_of(96) < 64
    low_rows = lane_of(ROWS) < 64
    for t in range(HEADS // 2):
        at = slice(t * 128, t * 128 + 128)
        own = left = right = None
        for side in range(2):
            even = ctx_in[base + t * 4 + side, 0:96, :].astype(F32)
            odd = ctx_in[base + t * 4 + 2 + side, 0:96, :].astype(F32)
            first = jnp.where(low, even, swap(odd))
            second = jnp.where(low, swap(even), odd)
            scale = []
            for kind in range(2):
                column = kind * 16 + side * 8 + 2 * t
                scale.append(jnp.where(
                    low_rows, share[:, column : column + 1], share[:, column + 1 : column + 2]
                ))
            part = jnp.concatenate([first[:64], second[:64]], axis=0) * scale[0]
            after = first[64:96] * scale[1][0:32]
            before = second[64:96] * scale[1][96:128]
            own = part if own is None else own + part
            left = before if left is None else left + before
            right = after if right is None else right + after
        ctx_ref[0:rim, at] = left[RIM - rim :].astype(BF16)
        ctx_ref[rim : rim + ROWS, at] = own.astype(BF16)
        ctx_ref[rim + ROWS :, at] = right[:rim].astype(BF16)


def place_taps(depth_ref, taps_ref):
    for r in range(0, KERNEL + 1, 8):
        got = min(8, KERNEL - r)
        block = depth_ref[r : r + got, :].astype(F32)
        if got < 8:
            block = jnp.concatenate([block, jnp.zeros((8 - got, WIDTH), F32)], axis=0)
        for t in range(8):
            put_rows(taps_ref, r, t, block[:, t * 128 : t * 128 + 128])


def to_lowered(x_ref, ctx_ref, wao_ref, resid_ref, low_ref):
    for j in range(4):
        at = slice(j * 256, j * 256 + 256)
        joined = x_ref[:, at].astype(F32) + dot(ctx_ref[...], wao_ref[:, at])
        resid_ref[:, at] = joined.astype(BF16)

    def lower(i, carry):
        at = pl.ds(pl.multiple_of(i * 16, 16), 16)
        centred, inverse = moments(resid_ref[at, :].astype(F32))
        low_ref[at, :] = (centred * inverse).astype(BF16)
        return carry

    lax.fori_loop(0, x_ref.shape[0] // 16, lower, 0, unroll=UNROLL)


def to_gated(low_ref, win_ref, g2_ref, frame, length, keep, arrivals=None):
    live = jnp.where((frame >= 0) & (frame < length), 1.0, 0.0)
    for j in range(4):
        at = slice(j * 256, j * 256 + 256)
        gate_at = slice(WIDTH + j * 256, WIDTH + j * 256 + 256)
        if arrivals is not None:
            arrivals[2 * j].wait()
            arrivals[2 * j + 1].wait()
        value = dot(low_ref[...], win_ref[:, at])
        gate = sigmoid(dot(low_ref[...], win_ref[:, gate_at]))
        if keep is not None:
            mv_ref, sg_ref = keep
            mv_ref[:, at] = value[RIM : RIM + ROWS]
            sg_ref[:, at] = gate[RIM : RIM + ROWS]
        gated = (value * gate * live).astype(BF16).astype(F32)
        for t in range(2):
            put_rows(g2_ref, 0, j * 2 + t, gated[:, t * 128 : t * 128 + 128])


def clean_kernel(
    scal_ref, ctx_hbm, clean_hbm, cot_hbm, up_hbm, down_hbm,
    wao_hbm, win_hbm, depth_hbm, wout_hbm,
    own_out, pack_out, sw_out, gs_out, gg2_out, g2_out, resid_out,
    ctx_in, wao_ref, win_ref, depth_ref, wout_ref,
    own_ref, pack_ref, sw_ref, gs_ref, gg2_ref, g2_ref, resid_ref,
    ctx_ref, x_ref, low_ref, mv_ref, sg_ref, s2_ref, zed_ref, zinv_ref, gox_ref, gsp2_ref, taps_ref,
    in_sems, out_sems,
):
    first_frame, length, core = scal_ref[0], scal_ref[1], scal_ref[2]
    half = RIM // 2
    copies = [
        pltpu.make_async_copy(source, target, in_sems.at[i])
        for i, (source, target) in enumerate((
            (ctx_hbm.at[pl.ds(0, 16)], ctx_in),
            (up_hbm.at[pl.ds(0, RIM)], x_ref.at[pl.ds(0, RIM)]),
            (clean_hbm, x_ref.at[pl.ds(RIM, ROWS)]),
            (down_hbm.at[pl.ds(0, RIM)], x_ref.at[pl.ds(RIM + ROWS, RIM)]),
            (wao_hbm, wao_ref),
            (depth_hbm, depth_ref),
            (up_hbm.at[pl.ds(RIM + half, half)], gox_ref.at[pl.ds(0, half)]),
            (cot_hbm, gox_ref.at[pl.ds(half, ROWS)]),
            (down_hbm.at[pl.ds(RIM + half, half)], gox_ref.at[pl.ds(half + ROWS, half)]),
            *(
                (win_hbm.at[:, pl.ds(at, 256)], win_ref.at[:, pl.ds(at, 256)])
                for j in range(0, WIDTH, 256)
                for at in (j, WIDTH + j)
            ),
            (wout_hbm, wout_ref),
        ))
    ]
    for copy in copies:
        copy.start()
    results = [
        pltpu.make_async_copy(source, target, out_sems.at[i])
        for i, (source, target) in enumerate((
            (own_ref, own_out),
            *(
                (pack_ref.at[:, pl.ds(at, size)], pack_out.at[:, pl.ds(at, size)])
                for at, size in ((0, WIDTH), (GM, 2 * WIDTH), (GO, WIDTH))
            ),
            (sw_ref, sw_out), (gs_ref, gs_out), (gg2_ref, gg2_out), (g2_ref, g2_out),
            (resid_ref, resid_out),
        ))
    ]
    own_copy, send_copy, gm_copy, go_copy, sw_copy, gs_copy, gg2_copy, g2_copy, resid_copy = results
    copies[0].wait()
    place_context(ctx_in, 0, ctx_ref, RIM)
    for copy in copies[1:9]:
        copy.wait()
    place_taps(depth_ref, taps_ref)
    for row in range(0, INNER, 16):
        at = slice(row, row + 16)
        frame = first_frame - half + row + lax.broadcasted_iota(jnp.int32, (16, 1), 0)
        gox_ref[at, :] = (gox_ref[at, :].astype(F32) * jnp.where(frame < length, 1.0, 0.0)).astype(BF16)
    pack_ref[:, GO:] = gox_ref[half : half + ROWS, :]
    go_copy.start()

    to_lowered(x_ref, ctx_ref, wao_ref, resid_ref, low_ref)
    resid_copy.start()
    frame = first_frame - RIM + lax.broadcasted_iota(jnp.int32, (CLEAN, 1), 0)
    to_gated(low_ref, win_ref, g2_ref, frame, length, (mv_ref, sg_ref), copies[9:17])
    g2_copy.start()
    forward = list(range(KERNEL))
    edge = half - KERNEL // 2
    depthwise(g2_ref, edge, taps_ref, forward, s2_ref, INNER)

    def clean_rows(i, carry):
        r = pl.multiple_of(i * 16, 16)
        centred, inverse = moments(get_rows(s2_ref, r, 16))
        zed = centred * inverse
        zed_ref[pl.ds(r, 16), :] = zed
        zinv_ref[pl.ds(r, 16), :] = jnp.broadcast_to(inverse, (16, 128))
        sw_ref[pl.ds(r, 16), :] = (zed * sigmoid(zed)).astype(BF16)
        return carry

    lax.fori_loop(0, INNER // 16, clean_rows, 0, unroll=UNROLL)
    sw_copy.start()

    for part in range(4):
        dest = part * 256
        source, row = (low_ref, RIM) if part < 2 else (sw_ref, half)
        lo = (part % 2) * 512
        first = source[row : row + ROWS, lo : lo + 256].astype(F32)
        second = source[row : row + ROWS, lo + 256 : lo + 512].astype(F32)
        own_ref[:, dest : dest + 256] = jnp.where(core == 0, first, second).astype(BF16)
        pack_ref[:, dest : dest + 256] = jnp.where(core == 0, second, first).astype(BF16)
    own_copy.start()
    send_copy.start()

    copies[17].wait()
    for j in range(4):
        at = slice(j * 256, j * 256 + 256)
        gs_ref[:, at] = dot_nt(gox_ref[...], wout_ref[at, :])
    gs_copy.start()

    def back_rows(i, carry):
        r = pl.multiple_of(i * 16, 16)
        zed = zed_ref[pl.ds(r, 16), :]
        grad = gs_ref[pl.ds(r, 16), :]
        gate = sigmoid(zed)
        grad_zed = grad * (gate * (1.0 + zed * (1.0 - gate)))
        mean = jnp.mean(grad_zed, axis=-1, keepdims=True)
        along = jnp.mean(grad_zed * zed, axis=-1, keepdims=True)
        result = (grad_zed - mean - zed * along) * zinv_ref[pl.ds(r, 16), 0:1]
        for g in range(0, 16, 8):
            for t in range(8):
                gsp2_ref[pl.ds((r + g) * 8 + t, 8, stride=8), :] = result[
                    g : g + 8, t * 128 : t * 128 + 128
                ]
        return carry

    lax.fori_loop(0, INNER // 16, back_rows, 0, unroll=UNROLL)
    depthwise(gsp2_ref, edge, taps_ref, forward[::-1], gg2_ref, ROWS)
    gg2_copy.start()

    def mixed_rows(i, carry):
        r = pl.multiple_of(i * 16, 16)
        at = pl.ds(r, 16)
        frame = first_frame + r + lax.broadcasted_iota(jnp.int32, (16, 1), 0)
        grad = get_rows(gg2_ref, r, 16) * jnp.where(frame < length, 1.0, 0.0)
        gate = sg_ref[at, :]
        pack_ref[at, GM : GM + WIDTH] = (grad * gate).astype(BF16)
        pack_ref[at, GM + WIDTH : GO] = (grad * mv_ref[at, :] * gate * (1.0 - gate)).astype(BF16)
        return carry

    lax.fori_loop(0, ROWS // 16, mixed_rows, 0, unroll=UNROLL)

    gm_copy.start()
    for copy in results:
        copy.wait()


def patch_kernel(
    scal_ref, site_ref, ctx_in, patched_ref, up_ref, down_ref,
    wao_ref, win_ref, depth_ref, wout_ref,
    pack_ref, swc_ref, gs_ref, gg2_ref, g2c_ref, residc_ref,
    attr_ref,
    ctx_ref, x_ref, resid_ref, low_ref, g2_ref, s2_ref, sw_ref, gl_ref, t0_ref, t1_ref, t2_ref, taps_ref,
):
    first_frame, length = scal_ref[0], scal_ref[1]
    half = RIM // 2
    place_context(ctx_in, 16, ctx_ref, half)
    x_ref[0:half, :] = up_ref[RIM : RIM + half, :]
    x_ref[half : half + ROWS, :] = patched_ref[...]
    x_ref[half + ROWS : PATCH, :] = down_ref[RIM : RIM + half, :]
    place_taps(depth_ref, taps_ref)
    to_lowered(x_ref, ctx_ref, wao_ref, resid_ref, low_ref)
    frame = first_frame - half + lax.broadcasted_iota(jnp.int32, (PATCH, 1), 0)
    to_gated(low_ref, win_ref, g2_ref, frame, length, None)
    depthwise(g2_ref, half - KERNEL // 2, taps_ref, list(range(KERNEL)), s2_ref, ROWS)
    sw_ref[0:ROWS, :] = swc_ref[half : half + ROWS, :]

    def patch_rows(i, carry):
        r = pl.multiple_of(i * 16, 16)
        at = pl.ds(r, 16)
        inner = pl.ds(pl.multiple_of(half + r, 16), 16)
        centred, inverse = moments(get_rows(s2_ref, r, 16))
        zed = centred * inverse
        swished = (zed * sigmoid(zed)).astype(BF16)
        sw_ref[pl.ds(pl.multiple_of(ROWS + r, 16), 16), :] = swished
        gap = swished.astype(F32) - sw_ref[at, :].astype(F32)
        t2_ref[at, :] = lane_sum(gap * gs_ref[inner, :])
        frame = first_frame + r + lax.broadcasted_iota(jnp.int32, (16, 1), 0)
        grad = get_rows(gg2_ref, r, 16) * jnp.where(frame < length, 1.0, 0.0)
        gap = get_rows(g2_ref, half + r, 16) - get_rows(g2c_ref, RIM + r, 16)
        t1_ref[at, :] = lane_sum(gap * grad)
        return carry

    lax.fori_loop(0, ROWS // 16, patch_rows, 0, unroll=UNROLL)

    t3 = jnp.zeros((ROWS, 128), F32)
    for j in range(4):
        at = slice(j * 256, j * 256 + 256)
        out = dot(sw_ref[...], wout_ref[:, at])
        out_clean = residc_ref[RIM : RIM + ROWS, at].astype(F32) + out[:ROWS]
        out_patch = resid_ref[half : half + ROWS, at].astype(F32) + out[ROWS:]
        gap = out_patch.astype(BF16).astype(F32) - out_clean.astype(BF16).astype(F32)
        t3 = t3 + lane_sum(gap * pack_ref[:, GO + j * 256 : GO + j * 256 + 256].astype(F32))
    for j in range(4):
        at = slice(j * 256, j * 256 + 256)
        gl_ref[:, at] = dot_nt(pack_ref[:, GM:GO], win_ref[at, :])

    def resid_rows(i, carry):
        r = pl.multiple_of(i * 16, 16)
        at = pl.ds(r, 16)
        clean = residc_ref[pl.ds(pl.multiple_of(RIM + r, 16), 16), :].astype(F32)
        patch = resid_ref[pl.ds(pl.multiple_of(half + r, 16), 16), :].astype(F32)
        centred, inverse = moments(clean)
        normed = centred * inverse
        grad = gl_ref[at, :]
        mean = jnp.mean(grad, axis=-1, keepdims=True)
        along = jnp.mean(grad * normed, axis=-1, keepdims=True)
        grad_resid = pack_ref[at, GO:].astype(F32) + (grad - mean - normed * along) * inverse
        t0_ref[at, :] = lane_sum((patch - clean) * grad_resid)
        return carry

    lax.fori_loop(0, ROWS // 16, resid_rows, 0, unroll=UNROLL)

    columns = [
        jnp.sum(part, axis=1, keepdims=True) for part in (t0_ref[...], t1_ref[...], t2_ref[...], t3)
    ]
    lane = lane_of(ROWS)
    chosen = jnp.zeros((ROWS, 128), F32)
    for i in range(attr_ref.shape[0]):
        site = site_ref[i]
        column = columns[0]
        for k in range(1, 4):
            column = jnp.where(site == k, columns[k], column)
        chosen = jnp.where(lane == i, column, chosen)
    attr_ref[...] = chosen.T[: attr_ref.shape[0]]


def weight_kernel(
    own_hbm, pack_hbm, other_hbm, out_hbm,
    left_ref, gm_ref, go_ref, out_ref, in_sems, out_sems,
):
    pairs = (
        (own_hbm, left_ref, 0),
        (other_hbm.at[:, pl.ds(0, WIDTH)], left_ref, ROWS),
        (pack_hbm.at[:, pl.ds(GO, WIDTH)], go_ref, 0),
        (other_hbm.at[:, pl.ds(GO, WIDTH)], go_ref, ROWS),
        (pack_hbm.at[:, pl.ds(GM, 2 * WIDTH)], gm_ref, 0),
        (other_hbm.at[:, pl.ds(GM, 2 * WIDTH)], gm_ref, ROWS),
    )
    copies = [
        pltpu.make_async_copy(source, target.at[pl.ds(row, ROWS)], in_sems.at[i])
        for i, (source, target, row) in enumerate(pairs)
    ]
    for copy in copies:
        copy.start()

    def send(i):
        at = pl.ds(i * 512, 512)
        return pltpu.make_async_copy(out_ref.at[:, :, at], out_hbm.at[:, :, at], out_sems.at[i])

    def put(at, product):
        half = product.shape[0] // 2
        lower = product[:half].reshape(half // 8, 8, 256)
        upper = product[half:].reshape(half // 8, 8, 256)
        out_ref[:, :, at : at + 256] = jnp.concatenate([lower, upper], axis=1).astype(BF16)

    for copy in copies[:4]:
        copy.wait()
    swished = left_ref[:, WIDTH // 2 :].T
    for j in range(0, WIDTH, 256):
        put(2 * WIDTH + j, dot(swished, go_ref[:, j : j + 256]))
        if j % 512:
            send(4 + j // 512).start()
    for copy in copies[4:]:
        copy.wait()
    low = left_ref[:, : WIDTH // 2].T
    for j in range(0, 2 * WIDTH, 256):
        put(j, dot(low, gm_ref[:, j : j + 256]))
        if j % 512:
            send(j // 512).start()
    for i in range(6):
        send(i).wait()


def fold_kernel(scal_ref, pieces_ref, mine_ref, theirs_ref):
    upper = scal_ref[4]

    def fold(at):
        total = pieces_ref[0, :, at].astype(F32)
        for k in range(1, pieces_ref.shape[0]):
            total = total + pieces_ref[k, :, at].astype(F32)
        first, second = total[:8], total[8:]
        mine_ref[:, at] = jnp.where(upper == 0, first, second)
        return jnp.where(upper == 0, second, first)

    middle = theirs_ref.shape[1]
    for j in range(0, middle, 256):
        low = fold(slice(j, j + 256))
        high = fold(slice(middle + j, middle + j + 256))
        theirs_ref[:, j : j + 256] = jnp.concatenate([low, high], axis=0).astype(BF16)


def join_kernel(mine_ref, theirs_ref, in_ref, out_ref):
    theirs = theirs_ref[...].astype(F32)
    whole = mine_ref[...] + jnp.concatenate([theirs[:8], theirs[8:]], axis=1)
    in_ref[...] = whole[:, : 2 * WIDTH]
    out_ref[...] = whole[:, 2 * WIDTH :]


VMEM = pl.BlockSpec(memory_space=pltpu.VMEM)
SMEM = pl.BlockSpec(memory_space=pltpu.SMEM)
HBM = pl.BlockSpec(memory_space=pltpu.HBM)


def kernel_call(body, out_shape, in_specs, scratch, limit, flops, moved, out_spec=VMEM):
    return pl.pallas_call(
        body,
        out_shape=out_shape,
        in_specs=in_specs,
        out_specs=[out_spec] * len(out_shape),
        scratch_shapes=scratch,
        compiler_params=pltpu.CompilerParams(vmem_limit_bytes=limit << 20),
        cost_estimate=pl.CostEstimate(flops=flops, bytes_accessed=moved, transcendentals=0),
    )


def shape(dims, dtype):
    return jax.ShapeDtypeStruct(dims, dtype)


def per_device(
    clean_input, corrupt_input, patch_mask, lengths, site_ids, w_query, w_key, w_value,
    w_attn_out, w_pointwise_in, depth_kernel, w_pointwise_out, cotangent,
):
    frames = lax.axis_size("frames")
    position = lax.axis_index("frames")
    core = lax.rem(lax.axis_index("dp"), 2)
    scalars = jnp.stack(
        [position * ROWS, lengths[0], core, lax.rem(position, 2), lax.axis_index("dp") // 2]
    ).astype(jnp.int32)
    clean, corrupt, cot = clean_input[0], corrupt_input[0], cotangent[0]

    msg, patched, up, down = kernel_call(
        project_kernel,
        [shape((frames, ROWS, 128), BF16), shape((ROWS, WIDTH), BF16),
         shape((2 * RIM, WIDTH), BF16), shape((2 * RIM, WIDTH), BF16)],
        [HBM] * 3 + [VMEM] + [HBM] * 3,
        [pltpu.VMEM((frames, ROWS, 128), BF16), pltpu.VMEM((ROWS, WIDTH), BF16),
         pltpu.VMEM((2 * RIM, WIDTH), BF16), pltpu.VMEM((2 * RIM, WIDTH), BF16),
         pltpu.VMEM((2 * ROWS, WIDTH), BF16), pltpu.VMEM((ROWS, ROWS), F32),
         pltpu.VMEM((ROWS, WIDTH), BF16), pltpu.VMEM((ROWS, WIDTH), BF16),
         pltpu.VMEM((WIDTH, 512), BF16), pltpu.VMEM((WIDTH, 512), BF16),
         pltpu.VMEM((WIDTH, 512), BF16), pltpu.SemaphoreType.DMA((7,)), pltpu.SemaphoreType.DMA((7,))],
        62, 8 * 10**8, 6 * 10**6, HBM,
    )(clean, corrupt, cot, patch_mask, w_query, w_key, w_value)
    forward = [(i, i + 1) for i in range(frames - 1)]
    backward = [(i + 1, i) for i in range(frames - 1)]
    from_left = lax.ppermute(up, "frames", forward)
    from_right = lax.ppermute(down, "frames", backward)
    recv = lax.all_to_all(msg, "frames", 0, 0, tiled=True)
    recv, from_left, from_right = lax.optimization_barrier((recv, from_left, from_right))
    keys = frames * ROWS // 2
    (context,) = kernel_call(
        attend_kernel,
        [shape((frames, 112, 128), BF16)],
        [SMEM, VMEM],
        [pltpu.VMEM((keys, 128), BF16), pltpu.VMEM((80, keys), BF16),
         pltpu.VMEM((128, 2 * keys), BF16),
         pltpu.VMEM((keys, 512), F32), pltpu.VMEM((keys, 512), F32),
         pltpu.VMEM((frames * 64, 128), F32), pltpu.VMEM((frames * 8, 128), F32)],
        20, 8 * 10**9, 10**6,
    )(scalars, recv)
    contexts = lax.all_to_all(context, "frames", 0, 0, tiled=True)
    own, pack, swished, grad_swished, grad_gated, gated, resid = kernel_call(
        clean_kernel,
        [shape((ROWS, WIDTH), BF16), shape((ROWS, 4 * WIDTH), BF16),
         shape((INNER, WIDTH), BF16), shape((INNER, WIDTH), F32),
         shape((ROWS * 8, 128), F32), shape((CLEAN * 8, 128), F32), shape((CLEAN, WIDTH), BF16)],
        [SMEM] + [HBM] * 9,
        [pltpu.VMEM((16, 112, 128), BF16), pltpu.VMEM((512, WIDTH), BF16),
         pltpu.VMEM((WIDTH, 2 * WIDTH), BF16), pltpu.VMEM((KERNEL, WIDTH), BF16),
         pltpu.VMEM((WIDTH, WIDTH), BF16),
         pltpu.VMEM((ROWS, WIDTH), BF16), pltpu.VMEM((ROWS, 4 * WIDTH), BF16),
         pltpu.VMEM((INNER, WIDTH), BF16), pltpu.VMEM((INNER, WIDTH), F32),
         pltpu.VMEM((ROWS * 8, 128), F32), pltpu.VMEM((CLEAN * 8, 128), F32),
         pltpu.VMEM((CLEAN, WIDTH), BF16),
         pltpu.VMEM((CLEAN, 512), BF16), pltpu.VMEM((CLEAN, WIDTH), BF16),
         pltpu.VMEM((CLEAN, WIDTH), BF16),
         pltpu.VMEM((ROWS, WIDTH), F32), pltpu.VMEM((ROWS, WIDTH), F32),
         pltpu.VMEM((INNER * 8, 128), F32), pltpu.VMEM((INNER, WIDTH), F32),
         pltpu.VMEM((INNER, 128), F32), pltpu.VMEM((INNER, WIDTH), BF16),
         pltpu.VMEM((INNER * 8, 128), F32), pltpu.VMEM((32 * 8, 128), F32),
         pltpu.SemaphoreType.DMA((18,)), pltpu.SemaphoreType.DMA((9,))],
        59, 3 * 10**9, 10**7, HBM,
    )(scalars, contexts, clean, cot, from_left, from_right,
      w_attn_out, w_pointwise_in, depth_kernel, w_pointwise_out)

    cores = [(i, i ^ 1) for i in range(lax.axis_size("dp"))]
    other = lax.ppermute(pack, "dp", cores)
    (partial,) = kernel_call(
        weight_kernel,
        [shape((frames, 16, 3 * WIDTH), BF16)],
        [HBM] * 3,
        [pltpu.VMEM((2 * ROWS, WIDTH), BF16), pltpu.VMEM((2 * ROWS, 2 * WIDTH), BF16),
         pltpu.VMEM((2 * ROWS, WIDTH), BF16), pltpu.VMEM((frames, 16, 3 * WIDTH), BF16),
         pltpu.SemaphoreType.DMA((6,)), pltpu.SemaphoreType.DMA((6,))],
        59, 8 * 10**8, 10**7, HBM,
    )(own, pack, other)
    pieces = lax.all_to_all(partial, "frames", 0, 0, tiled=True)
    (attribution,) = kernel_call(
        patch_kernel,
        [shape((site_ids.shape[0], ROWS), F32)],
        [SMEM, SMEM] + [VMEM] * 14,
        [pltpu.VMEM((PATCH, 512), BF16), pltpu.VMEM((PATCH, WIDTH), BF16),
         pltpu.VMEM((PATCH, WIDTH), BF16), pltpu.VMEM((PATCH, WIDTH), BF16),
         pltpu.VMEM((PATCH * 8, 128), F32), pltpu.VMEM((ROWS * 8, 128), F32),
         pltpu.VMEM((2 * ROWS, WIDTH), BF16), pltpu.VMEM((ROWS, WIDTH), F32),
         pltpu.VMEM((ROWS, 128), F32), pltpu.VMEM((ROWS, 128), F32), pltpu.VMEM((ROWS, 128), F32),
         pltpu.VMEM((32 * 8, 128), F32)],
        28, 3 * 10**9, 10**7,
    )(scalars, site_ids, contexts, patched, from_left, from_right,
      w_attn_out, w_pointwise_in, depth_kernel, w_pointwise_out,
      pack, swished, grad_swished, grad_gated, gated, resid)
    pieces, attribution = lax.optimization_barrier((pieces, attribution))
    mine, theirs = kernel_call(
        fold_kernel,
        [shape((8, 3 * WIDTH), F32), shape((16, 3 * WIDTH // 2), BF16)],
        [SMEM, VMEM],
        [],
        16, 10**8, 3 * 10**6,
    )(scalars, pieces)
    half_dp = lax.axis_size("dp") // 2
    theirs = lax.ppermute(theirs, "dp", [(i, i ^ half_dp) for i in range(2 * half_dp)])
    grad_in, grad_out = kernel_call(
        join_kernel,
        [shape((8, 2 * WIDTH), F32), shape((8, WIDTH), F32)],
        [VMEM] * 2,
        [],
        16, 10**6, 10**6,
    )(mine, theirs)
    return attribution[None], grad_in, grad_out


def solution(mesh):
    placed = (
        P("dp", "frames", None), P("dp", "frames", None), P("dp", "frames"), P("dp"), P(), P(), P(),
        P(), P(), P(), P(), P(), P("dp", "frames", None),
    )
    return jax.shard_map(
        per_device,
        mesh=mesh,
        in_specs=placed,
        out_specs=(P("dp", None, "frames"), P(("dp", "frames"), None), P(("dp", "frames"), None)),
        check_vma=False,
    )
```

```python
import jax
import jax.numpy as jnp
from jax import lax
from jax.experimental import pallas as pl
from jax.experimental.pallas import tpu as pltpu
from jax.sharding import PartitionSpec as P

HEADS = 8
DH = 64
KERNEL = 31
RIM = 32
EPSILON = 1e-05
FLOOR = -1e30
LOG2E = 1.4426950408889634
F32 = jnp.float32
BF16 = jnp.bfloat16
ROWS = 128
WIDTH = 1024
CLEAN = ROWS + 2 * RIM
PATCH = ROWS + RIM
BOTH = CLEAN + PATCH
INNER = ROWS + RIM
GM = WIDTH
GO = 3 * WIDTH
UNROLL = True
TAP_UNROLL = 8
LOAD_UNROLL = 16
PACK_UNROLL = 32
CHUNK = 256


def lane_of(rows):
    return lax.broadcasted_iota(jnp.int32, (rows, 128), 1)


def swap(tile):
    return pltpu.roll(tile, 64, 1)


def moments(values):
    mean = jnp.mean(values, axis=-1, keepdims=True)
    centred = values - mean
    variance = jnp.mean(centred * centred, axis=-1, keepdims=True)
    return centred, lax.rsqrt(variance + EPSILON)


def dot(left, right):
    return jnp.dot(left, right, preferred_element_type=F32)


def dot_nt(left, right):
    return lax.dot_general(left, right, (((1,), (1,)), ((), ())), preferred_element_type=F32)


def dot_tn(left, right):
    return lax.dot_general(left, right, (((0,), (0,)), ((), ())), preferred_element_type=F32)


def sigmoid(values):
    return 0.5 * jnp.tanh(0.5 * values) + 0.5


def lane_sum(values):
    total = values[:, :128]
    for start in range(128, values.shape[1], 128):
        total = total + values[:, start : start + 128]
    return total


def project_kernel(
    clean_hbm, corrupt_hbm, cot_hbm, mask_ref, wq_hbm, wk_hbm, wv_hbm,
    msg_out, patched_out, up_out, down_out,
    msg_ref, patched_ref, up_ref, down_ref,
    hidden_ref, mask_col, clean_ref, corrupt_ref, wq_ref, wk_ref, wv_ref, sems, out_sems,
):
    half = RIM // 2
    copies = [
        pltpu.make_async_copy(source, target, sems.at[i])
        for i, (source, target) in enumerate((
            (clean_hbm, clean_ref),
            (corrupt_hbm, corrupt_ref),
            (wk_hbm, wk_ref),
            (wv_hbm, wv_ref),
            (wq_hbm, wq_ref),
            (cot_hbm.at[pl.ds(ROWS - half, half)], up_ref.at[pl.ds(RIM + half, half)]),
            (cot_hbm.at[pl.ds(0, half)], down_ref.at[pl.ds(RIM + half, half)]),
        ))
    ]
    for copy in copies:
        copy.start()
    spread_mask = jnp.broadcast_to(mask_ref[...].astype(F32), (ROWS, ROWS))
    mask_col[...] = spread_mask.T
    copies[0].wait()
    copies[1].wait()

    def rows(i, carry):
        at = pl.ds(pl.multiple_of(i * 16, 16), 16)
        below = pl.ds(pl.multiple_of(ROWS + i * 16, 16), 16)
        clean = clean_ref[at, :].astype(F32)
        corrupt = corrupt_ref[at, :].astype(F32)
        patched = jnp.where(mask_col[at, 0:1] == 1.0, corrupt, clean)
        patched_ref[at, :] = patched.astype(BF16)
        for dest, source in ((at, clean), (below, patched)):
            centred, inverse = moments(source)
            hidden_ref[dest, :] = (centred * inverse).astype(BF16)
        return carry

    lax.fori_loop(0, ROWS // 16, rows, 0, unroll=UNROLL)
    up_ref[0:RIM, :] = clean_ref[ROWS - RIM : ROWS, :]
    up_ref[RIM : RIM + half, :] = patched_ref[ROWS - half : ROWS, :]
    down_ref[0:RIM, :] = clean_ref[0:RIM, :]
    down_ref[RIM : RIM + half, :] = patched_ref[0:half, :]
    for copy in copies[2:]:
        copy.wait()
    results = [
        pltpu.make_async_copy(source, target, out_sems.at[i])
        for i, (source, target) in enumerate((
            (up_ref, up_out), (down_ref, down_out), (patched_ref, patched_out),
            *(
                (msg_ref.at[pl.ds(at, 8)], msg_out.at[pl.ds(at, 8)])
                for at in (0, 16, 8, 24)
            ),
        ))
    ]
    for copy in results[:3]:
        copy.start()

    low = lane_of(ROWS) < 64
    low_q = lane_of(64) < 64
    for pair in range(2):
        cols = slice(pair * 256, pair * 256 + 256)
        hidden = hidden_ref[...]
        query = dot(hidden, wq_ref[:, cols])
        keys = dot(hidden, wk_ref[:, cols])
        values = dot(hidden, wv_ref[:, cols])
        for sub in range(2):
            tile = slice(sub * 128, sub * 128 + 128)
            for run in range(2):
                part = slice(run * ROWS, run * ROWS + ROWS)
                k, v, q = keys[part, tile], values[part, tile], query[part, tile]
                base = run * 16 + (pair * 2 + sub) * 4
                kv = (jnp.where(low, k, swap(v)).astype(BF16), jnp.where(low, swap(k), v).astype(BF16))
                early, late = q[:64], q[64:]
                asked = (
                    jnp.where(low_q, early, swap(late)).astype(BF16),
                    jnp.where(low_q, swap(early), late).astype(BF16),
                )
                for odd in range(2):
                    for side in range(2):
                        dest = base + odd * 2 + side
                        msg_ref[dest, 0:64, :] = kv[odd][side * 64 : side * 64 + 64]
                        msg_ref[dest, 64:128, :] = asked[odd]
        results[3 + 2 * pair].start()
        results[4 + 2 * pair].start()
    for copy in results:
        copy.wait()


def attend_kernel(
    scal_ref, recv_ref, out_ref, k_ref, vt_ref, qt_ref, s0_ref, s1_ref, c_ref, r_ref
):
    length, side = scal_ref[1], scal_ref[3]
    sources = recv_ref.shape[0]
    lane = lane_of(128)
    row = lax.broadcasted_iota(jnp.int32, (128, 128), 0)
    scale = DH ** (-0.5) * LOG2E

    def load(s, carry):
        at = pl.multiple_of(s * 128, 128)
        kv = recv_ref[pl.ds(2 * s, 2), 0:64, :].astype(F32).reshape(128, 128)
        frame = (2 * s + row // 64) * ROWS + side * 64 + row % 64
        bias = jnp.where(frame < length, 0.0, FLOOR)
        keyed = jnp.where(lane < 64, kv, jnp.where(lane == 64, bias, 0.0))
        k_ref[pl.ds(at, 128), :] = keyed.astype(BF16)
        vt_ref[0:64, pl.ds(at, 128)] = kv.T[64:128].astype(BF16)
        vt_ref[64:80, pl.ds(at, 128)] = jnp.ones((16, 128), BF16)
        raw = recv_ref[pl.ds(2 * s, 2), 64:128, :].astype(F32).reshape(128, 128).T
        fill = jnp.where(row == 64, 1.0, 0.0)
        other = jnp.concatenate([raw[64:], raw[:64]], axis=0)
        at = pl.multiple_of(s * 256, 256)
        qt_ref[:, pl.ds(at, 128)] = jnp.where(row < 64, raw, fill).astype(BF16)
        qt_ref[:, pl.ds(at + 128, 128)] = jnp.where(row < 64, other, fill).astype(BF16)
        return carry

    lax.fori_loop(0, sources // 2, load, 0, unroll=LOAD_UNROLL)

    many = s0_ref.shape[1]
    chunk = CHUNK
    pieces = k_ref.shape[0] // chunk
    blocks = sources * ROWS // many

    def score_piece(query, s_ref, k, top):
        at = slice(k * chunk, k * chunk + chunk)
        scores = dot(k_ref[at, :], query)
        s_ref[at, :] = scores
        best = jnp.max(scores.reshape(chunk // 8, 8, many), axis=0)
        return best if top is None else jnp.maximum(top, best)

    def weigh_piece(s_ref, best, k, accum):
        at = slice(k * chunk, k * chunk + chunk)
        weights = jnp.exp2((s_ref[at, :] - best) * scale).astype(BF16)
        addend = dot(vt_ref[:, at], weights)
        return addend if accum is None else accum + addend

    def finish(top):
        return jnp.max(top, axis=0, keepdims=True)

    def queries(b):
        return qt_ref[:, pl.ds(pl.multiple_of(b * many, many), many)]

    low8 = lane_of(8) < 64

    def store(b, accum, best):
        total = accum[64:65, :]
        result = accum[0:64, :] / total
        level = jnp.broadcast_to(best * scale + jnp.log2(total), (8, many))
        for g in range(many // 256):
            first = slice(g * 256, g * 256 + 128)
            second = slice(g * 256 + 128, g * 256 + 256)
            both = jnp.concatenate([result[:, first], result[:, second]], axis=0)
            at = b * (many // 256) + g
            c_ref[pl.ds(pl.multiple_of(at * 128, 128), 128), :] = both.T
            early, late = level[:, first], level[:, second]
            r_ref[pl.ds(pl.multiple_of(at * 16, 16), 8), :] = jnp.where(low8, early, swap(late))
            r_ref[pl.ds(pl.multiple_of(at * 16 + 8, 8), 8), :] = jnp.where(low8, swap(early), late)

    def step(b, s_ref, best, next_b, next_s):
        query = None if next_s is None else queries(next_b)
        top, accum = None, None
        for k in range(pieces):
            if query is not None:
                top = score_piece(query, next_s, k, top)
            accum = weigh_piece(s_ref, best, k, accum)
        store(b, accum, best)
        return None if query is None else finish(top)

    query, top = queries(0), None
    for k in range(pieces):
        top = score_piece(query, s0_ref, k, top)

    def pair(i, best):
        best = step(2 * i, s0_ref, best, 2 * i + 1, s1_ref)
        return step(2 * i + 1, s1_ref, best, 2 * i + 2, s0_ref)

    best = lax.fori_loop(0, blocks // 2 - 1, pair, finish(top))
    best = step(blocks - 2, s0_ref, best, blocks - 1, s1_ref)
    step(blocks - 1, s1_ref, best, None, None)

    low32 = lane_of(32) < 64
    row8 = lax.broadcasted_iota(jnp.int32, (8, 128), 0)

    def pack(d, carry):
        after = lax.rem(d + 1, sources)
        before = lax.rem(d + sources - 1, sources)
        out_ref[d, 0:64, :] = c_ref[pl.ds(pl.multiple_of(d * 64, 64), 64), :].astype(BF16)
        right = c_ref[pl.ds(pl.multiple_of(after * 64, 64), 32), :]
        left = c_ref[pl.ds(pl.multiple_of(before * 64 + 32, 32), 32), :]
        out_ref[d, 64:96, :] = jnp.where(low32, right, left).astype(BF16)
        own = r_ref[pl.ds(pl.multiple_of(d * 8, 8), 8), :]
        rim = jnp.where(
            low8,
            r_ref[pl.ds(pl.multiple_of(after * 8, 8), 8), :],
            r_ref[pl.ds(pl.multiple_of(before * 8, 8), 8), :],
        )
        rows = jnp.where(row8 < 3, own, rim)
        high = rows.astype(BF16).astype(F32)
        rest = rows - high
        middle = rest.astype(BF16).astype(F32)
        last = rest - middle
        level = row8 % 3
        rows = jnp.where(level == 0, high, jnp.where(level == 1, middle, last))
        out_ref[d, 96:112, :] = jnp.concatenate([rows, rows], axis=0).astype(BF16)
        return carry

    lax.fori_loop(0, sources, pack, 0, unroll=PACK_UNROLL)


def depthwise(source, source_row, taps_ref, order, target, count):
    def rows(i, carry):
        first = source_row + i * 8
        taps = [taps_ref[t * 8 : t * 8 + 8, :] for t in order]
        sums = [None] * 8
        for s in range(KERNEL + 7):
            piece = source[pl.ds(pl.multiple_of((first + s) * 8, 8), 8), :]
            for o in range(8):
                if 0 <= s - o < KERNEL:
                    term = taps[s - o] * piece
                    sums[o] = term if sums[o] is None else sums[o] + term
        for o in range(8):
            target[pl.ds(pl.multiple_of((i * 8 + o) * 8, 8), 8), :] = sums[o]
        return carry

    lax.fori_loop(0, count // 8, rows, 0, unroll=TAP_UNROLL)


def put_rows(ref, row, tile, values):
    for r in range(0, values.shape[0], 8):
        ref[pl.ds((row + r) * 8 + tile, 8, stride=8), :] = values[r : r + 8]


def get_rows(ref, row, count):
    groups = []
    for r in range(0, count, 8):
        tiles = [ref[pl.ds((row + r) * 8 + t, 8, stride=8), :] for t in range(8)]
        groups.append(jnp.concatenate(tiles, axis=1))
    return jnp.concatenate(groups, axis=0) if len(groups) > 1 else groups[0]


def place_context(ctx_in, base, ctx_ref, rim):
    row8 = lax.broadcasted_iota(jnp.int32, (8, 128), 0)
    zero = jnp.zeros((8, 128), F32)
    levels = [[zero, zero], [zero, zero]]
    for h in range(HEADS):
        for side in range(2):
            block = ctx_in[base + h * 2 + side, 96:112, :].astype(F32)
            for kind in range(2):
                at = kind * 3
                level = block[at : at + 1] + block[at + 1 : at + 2] + block[at + 2 : at + 3]
                levels[kind][side] = jnp.where(row8 == h, level, levels[kind][side])
    shares = []
    for first, second in levels:
        shares.append(1.0 / (1.0 + jnp.exp2(second - first)))
        shares.append(1.0 / (1.0 + jnp.exp2(first - second)))
    share = jnp.concatenate(shares + [jnp.zeros((96, 128), F32)], axis=0).T
    low = lane_of(96) < 64
    low_rows = lane_of(ROWS) < 64
    for t in range(HEADS // 2):
        at = slice(t * 128, t * 128 + 128)
        own = left = right = None
        for side in range(2):
            even = ctx_in[base + t * 4 + side, 0:96, :].astype(F32)
            odd = ctx_in[base + t * 4 + 2 + side, 0:96, :].astype(F32)
            first = jnp.where(low, even, swap(odd))
            second = jnp.where(low, swap(even), odd)
            scale = []
            for kind in range(2):
                column = kind * 16 + side * 8 + 2 * t
                scale.append(jnp.where(
                    low_rows, share[:, column : column + 1], share[:, column + 1 : column + 2]
                ))
            part = jnp.concatenate([first[:64], second[:64]], axis=0) * scale[0]
            after = first[64:96] * scale[1][0:32]
            before = second[64:96] * scale[1][96:128]
            own = part if own is None else own + part
            left = before if left is None else left + before
            right = after if right is None else right + after
        ctx_ref[0:rim, at] = left[RIM - rim :].astype(BF16)
        ctx_ref[rim : rim + ROWS, at] = own.astype(BF16)
        ctx_ref[rim + ROWS :, at] = right[:rim].astype(BF16)


def place_taps(depth_ref, taps_ref):
    for r in range(0, KERNEL + 1, 8):
        got = min(8, KERNEL - r)
        block = depth_ref[r : r + got, :].astype(F32)
        if got < 8:
            block = jnp.concatenate([block, jnp.zeros((8 - got, WIDTH), F32)], axis=0)
        for t in range(8):
            put_rows(taps_ref, r, t, block[:, t * 128 : t * 128 + 128])


def to_lowered(x_ref, ctx_ref, wao_ref, resid_ref, low_ref):
    for j in range(4):
        at = slice(j * 256, j * 256 + 256)
        joined = x_ref[:, at].astype(F32) + dot(ctx_ref[...], wao_ref[:, at])
        resid_ref[:, at] = joined.astype(BF16)

    def lower(i, carry):
        at = pl.ds(pl.multiple_of(i * 16, 16), 16)
        centred, inverse = moments(resid_ref[at, :].astype(F32))
        low_ref[at, :] = (centred * inverse).astype(BF16)
        return carry

    lax.fori_loop(0, x_ref.shape[0] // 16, lower, 0, unroll=UNROLL)


def to_gated(low_ref, win_ref, g2_ref, frame, length, keep, arrivals=None):
    live = jnp.where((frame >= 0) & (frame < length), 1.0, 0.0)
    for j in range(4):
        at = slice(j * 256, j * 256 + 256)
        gate_at = slice(WIDTH + j * 256, WIDTH + j * 256 + 256)
        if arrivals is not None:
            arrivals[2 * j].wait()
            arrivals[2 * j + 1].wait()
        value = dot(low_ref[...], win_ref[:, at])
        gate = sigmoid(dot(low_ref[...], win_ref[:, gate_at]))
        if keep is not None:
            mv_ref, sg_ref = keep
            mv_ref[:, at] = value[RIM : RIM + ROWS]
            sg_ref[:, at] = gate[RIM : RIM + ROWS]
        gated = (value * gate * live).astype(BF16).astype(F32)
        for t in range(2):
            put_rows(g2_ref, 0, j * 2 + t, gated[:, t * 128 : t * 128 + 128])


def clean_kernel(
    scal_ref, ctx_hbm, clean_hbm, cot_hbm, up_hbm, down_hbm,
    wao_hbm, win_hbm, depth_hbm, wout_hbm,
    own_out, pack_out, sw_out, gs_out, gg2_out, g2_out, resid_out,
    ctx_in, wao_ref, win_ref, depth_ref, wout_ref,
    own_ref, pack_ref, sw_ref, gs_ref, gg2_ref, g2_ref, resid_ref,
    ctx_ref, x_ref, low_ref, mv_ref, sg_ref, s2_ref, zed_ref, zinv_ref, gox_ref, gsp2_ref, taps_ref,
    in_sems, out_sems,
):
    first_frame, length, core = scal_ref[0], scal_ref[1], scal_ref[2]
    half = RIM // 2
    copies = [
        pltpu.make_async_copy(source, target, in_sems.at[i])
        for i, (source, target) in enumerate((
            (ctx_hbm.at[pl.ds(0, 16)], ctx_in),
            (up_hbm.at[pl.ds(0, RIM)], x_ref.at[pl.ds(0, RIM)]),
            (clean_hbm, x_ref.at[pl.ds(RIM, ROWS)]),
            (down_hbm.at[pl.ds(0, RIM)], x_ref.at[pl.ds(RIM + ROWS, RIM)]),
            (wao_hbm, wao_ref),
            (depth_hbm, depth_ref),
            (up_hbm.at[pl.ds(RIM + half, half)], gox_ref.at[pl.ds(0, half)]),
            (cot_hbm, gox_ref.at[pl.ds(half, ROWS)]),
            (down_hbm.at[pl.ds(RIM + half, half)], gox_ref.at[pl.ds(half + ROWS, half)]),
            *(
                (win_hbm.at[:, pl.ds(at, 256)], win_ref.at[:, pl.ds(at, 256)])
                for j in range(0, WIDTH, 256)
                for at in (j, WIDTH + j)
            ),
            (wout_hbm, wout_ref),
        ))
    ]
    for copy in copies:
        copy.start()
    results = [
        pltpu.make_async_copy(source, target, out_sems.at[i])
        for i, (source, target) in enumerate((
            (own_ref, own_out),
            *(
                (pack_ref.at[:, pl.ds(at, size)], pack_out.at[:, pl.ds(at, size)])
                for at, size in ((0, WIDTH), (GM, 2 * WIDTH), (GO, WIDTH))
            ),
            (sw_ref, sw_out), (gs_ref, gs_out), (gg2_ref, gg2_out), (g2_ref, g2_out),
            (resid_ref, resid_out),
        ))
    ]
    own_copy, send_copy, gm_copy, go_copy, sw_copy, gs_copy, gg2_copy, g2_copy, resid_copy = results
    copies[0].wait()
    place_context(ctx_in, 0, ctx_ref, RIM)
    for copy in copies[1:9]:
        copy.wait()
    place_taps(depth_ref, taps_ref)
    for row in range(0, INNER, 16):
        at = slice(row, row + 16)
        frame = first_frame - half + row + lax.broadcasted_iota(jnp.int32, (16, 1), 0)
        gox_ref[at, :] = (gox_ref[at, :].astype(F32) * jnp.where(frame < length, 1.0, 0.0)).astype(BF16)
    pack_ref[:, GO:] = gox_ref[half : half + ROWS, :]
    go_copy.start()

    to_lowered(x_ref, ctx_ref, wao_ref, resid_ref, low_ref)
    resid_copy.start()
    frame = first_frame - RIM + lax.broadcasted_iota(jnp.int32, (CLEAN, 1), 0)
    to_gated(low_ref, win_ref, g2_ref, frame, length, (mv_ref, sg_ref), copies[9:17])
    g2_copy.start()
    forward = list(range(KERNEL))
    edge = half - KERNEL // 2
    depthwise(g2_ref, edge, taps_ref, forward, s2_ref, INNER)

    def clean_rows(i, carry):
        r = pl.multiple_of(i * 16, 16)
        centred, inverse = moments(get_rows(s2_ref, r, 16))
        zed = centred * inverse
        zed_ref[pl.ds(r, 16), :] = zed
        zinv_ref[pl.ds(r, 16), :] = jnp.broadcast_to(inverse, (16, 128))
        sw_ref[pl.ds(r, 16), :] = (zed * sigmoid(zed)).astype(BF16)
        return carry

    lax.fori_loop(0, INNER // 16, clean_rows, 0, unroll=UNROLL)
    sw_copy.start()

    for part in range(4):
        dest = part * 256
        source, row = (low_ref, RIM) if part < 2 else (sw_ref, half)
        lo = (part % 2) * 512
        first = source[row : row + ROWS, lo : lo + 256].astype(F32)
        second = source[row : row + ROWS, lo + 256 : lo + 512].astype(F32)
        own_ref[:, dest : dest + 256] = jnp.where(core == 0, first, second).astype(BF16)
        pack_ref[:, dest : dest + 256] = jnp.where(core == 0, second, first).astype(BF16)
    own_copy.start()
    send_copy.start()

    copies[17].wait()
    for j in range(4):
        at = slice(j * 256, j * 256 + 256)
        gs_ref[:, at] = dot_nt(gox_ref[...], wout_ref[at, :])
    gs_copy.start()

    def back_rows(i, carry):
        r = pl.multiple_of(i * 16, 16)
        zed = zed_ref[pl.ds(r, 16), :]
        grad = gs_ref[pl.ds(r, 16), :]
        gate = sigmoid(zed)
        grad_zed = grad * (gate * (1.0 + zed * (1.0 - gate)))
        mean = jnp.mean(grad_zed, axis=-1, keepdims=True)
        along = jnp.mean(grad_zed * zed, axis=-1, keepdims=True)
        result = (grad_zed - mean - zed * along) * zinv_ref[pl.ds(r, 16), 0:1]
        for g in range(0, 16, 8):
            for t in range(8):
                gsp2_ref[pl.ds((r + g) * 8 + t, 8, stride=8), :] = result[
                    g : g + 8, t * 128 : t * 128 + 128
                ]
        return carry

    lax.fori_loop(0, INNER // 16, back_rows, 0, unroll=UNROLL)
    depthwise(gsp2_ref, edge, taps_ref, forward[::-1], gg2_ref, ROWS)
    gg2_copy.start()

    def mixed_rows(i, carry):
        r = pl.multiple_of(i * 16, 16)
        at = pl.ds(r, 16)
        frame = first_frame + r + lax.broadcasted_iota(jnp.int32, (16, 1), 0)
        grad = get_rows(gg2_ref, r, 16) * jnp.where(frame < length, 1.0, 0.0)
        gate = sg_ref[at, :]
        pack_ref[at, GM : GM + WIDTH] = (grad * gate).astype(BF16)
        pack_ref[at, GM + WIDTH : GO] = (grad * mv_ref[at, :] * gate * (1.0 - gate)).astype(BF16)
        return carry

    lax.fori_loop(0, ROWS // 16, mixed_rows, 0, unroll=UNROLL)

    gm_copy.start()
    for copy in results:
        copy.wait()


def patch_kernel(
    scal_ref, site_ref, ctx_in, patched_ref, up_ref, down_ref,
    wao_ref, win_ref, depth_ref, wout_ref,
    pack_ref, swc_ref, gs_ref, gg2_ref, g2c_ref, residc_ref,
    attr_ref,
    ctx_ref, x_ref, resid_ref, low_ref, g2_ref, s2_ref, sw_ref, gl_ref, t0_ref, t1_ref, t2_ref, taps_ref,
):
    first_frame, length = scal_ref[0], scal_ref[1]
    half = RIM // 2
    place_context(ctx_in, 16, ctx_ref, half)
    x_ref[0:half, :] = up_ref[RIM : RIM + half, :]
    x_ref[half : half + ROWS, :] = patched_ref[...]
    x_ref[half + ROWS : PATCH, :] = down_ref[RIM : RIM + half, :]
    place_taps(depth_ref, taps_ref)
    to_lowered(x_ref, ctx_ref, wao_ref, resid_ref, low_ref)
    frame = first_frame - half + lax.broadcasted_iota(jnp.int32, (PATCH, 1), 0)
    to_gated(low_ref, win_ref, g2_ref, frame, length, None)
    depthwise(g2_ref, half - KERNEL // 2, taps_ref, list(range(KERNEL)), s2_ref, ROWS)
    sw_ref[0:ROWS, :] = swc_ref[half : half + ROWS, :]

    def patch_rows(i, carry):
        r = pl.multiple_of(i * 16, 16)
        at = pl.ds(r, 16)
        inner = pl.ds(pl.multiple_of(half + r, 16), 16)
        centred, inverse = moments(get_rows(s2_ref, r, 16))
        zed = centred * inverse
        swished = (zed * sigmoid(zed)).astype(BF16)
        sw_ref[pl.ds(pl.multiple_of(ROWS + r, 16), 16), :] = swished
        gap = swished.astype(F32) - sw_ref[at, :].astype(F32)
        t2_ref[at, :] = lane_sum(gap * gs_ref[inner, :])
        frame = first_frame + r + lax.broadcasted_iota(jnp.int32, (16, 1), 0)
        grad = get_rows(gg2_ref, r, 16) * jnp.where(frame < length, 1.0, 0.0)
        gap = get_rows(g2_ref, half + r, 16) - get_rows(g2c_ref, RIM + r, 16)
        t1_ref[at, :] = lane_sum(gap * grad)
        return carry

    lax.fori_loop(0, ROWS // 16, patch_rows, 0, unroll=UNROLL)

    t3 = jnp.zeros((ROWS, 128), F32)
    for j in range(4):
        at = slice(j * 256, j * 256 + 256)
        out = dot(sw_ref[...], wout_ref[:, at])
        out_clean = residc_ref[RIM : RIM + ROWS, at].astype(F32) + out[:ROWS]
        out_patch = resid_ref[half : half + ROWS, at].astype(F32) + out[ROWS:]
        gap = out_patch.astype(BF16).astype(F32) - out_clean.astype(BF16).astype(F32)
        t3 = t3 + lane_sum(gap * pack_ref[:, GO + j * 256 : GO + j * 256 + 256].astype(F32))
    for j in range(4):
        at = slice(j * 256, j * 256 + 256)
        gl_ref[:, at] = dot_nt(pack_ref[:, GM:GO], win_ref[at, :])

    def resid_rows(i, carry):
        r = pl.multiple_of(i * 16, 16)
        at = pl.ds(r, 16)
        clean = residc_ref[pl.ds(pl.multiple_of(RIM + r, 16), 16), :].astype(F32)
        patch = resid_ref[pl.ds(pl.multiple_of(half + r, 16), 16), :].astype(F32)
        centred, inverse = moments(clean)
        normed = centred * inverse
        grad = gl_ref[at, :]
        mean = jnp.mean(grad, axis=-1, keepdims=True)
        along = jnp.mean(grad * normed, axis=-1, keepdims=True)
        grad_resid = pack_ref[at, GO:].astype(F32) + (grad - mean - normed * along) * inverse
        t0_ref[at, :] = lane_sum((patch - clean) * grad_resid)
        return carry

    lax.fori_loop(0, ROWS // 16, resid_rows, 0, unroll=UNROLL)

    columns = [
        jnp.sum(part, axis=1, keepdims=True) for part in (t0_ref[...], t1_ref[...], t2_ref[...], t3)
    ]
    lane = lane_of(ROWS)
    chosen = jnp.zeros((ROWS, 128), F32)
    for i in range(attr_ref.shape[0]):
        site = site_ref[i]
        column = columns[0]
        for k in range(1, 4):
            column = jnp.where(site == k, columns[k], column)
        chosen = jnp.where(lane == i, column, chosen)
    attr_ref[...] = chosen.T[: attr_ref.shape[0]]


def weight_kernel(
    own_hbm, pack_hbm, other_hbm, out_hbm,
    left_ref, gm_ref, go_ref, out_ref, in_sems, out_sems,
):
    pairs = (
        (own_hbm, left_ref, 0),
        (other_hbm.at[:, pl.ds(0, WIDTH)], left_ref, ROWS),
        (pack_hbm.at[:, pl.ds(GO, WIDTH)], go_ref, 0),
        (other_hbm.at[:, pl.ds(GO, WIDTH)], go_ref, ROWS),
        (pack_hbm.at[:, pl.ds(GM, 2 * WIDTH)], gm_ref, 0),
        (other_hbm.at[:, pl.ds(GM, 2 * WIDTH)], gm_ref, ROWS),
    )
    copies = [
        pltpu.make_async_copy(source, target.at[pl.ds(row, ROWS)], in_sems.at[i])
        for i, (source, target, row) in enumerate(pairs)
    ]
    for copy in copies:
        copy.start()

    def send(i):
        at = pl.ds(i * 512, 512)
        return pltpu.make_async_copy(out_ref.at[:, :, at], out_hbm.at[:, :, at], out_sems.at[i])

    def put(at, product):
        half = product.shape[0] // 2
        lower = product[:half].reshape(half // 8, 8, 256)
        upper = product[half:].reshape(half // 8, 8, 256)
        out_ref[:, :, at : at + 256] = jnp.concatenate([lower, upper], axis=1).astype(BF16)

    for copy in copies[:4]:
        copy.wait()
    swished = left_ref[:, WIDTH // 2 :].T
    for j in range(0, WIDTH, 256):
        put(2 * WIDTH + j, dot(swished, go_ref[:, j : j + 256]))
        if j % 512:
            send(4 + j // 512).start()
    for copy in copies[4:]:
        copy.wait()
    low = left_ref[:, : WIDTH // 2].T
    for j in range(0, 2 * WIDTH, 256):
        put(j, dot(low, gm_ref[:, j : j + 256]))
        if j % 512:
            send(j // 512).start()
    for i in range(6):
        send(i).wait()


def fold_kernel(scal_ref, pieces_ref, mine_ref, theirs_ref):
    upper = scal_ref[4]

    def fold(at):
        total = pieces_ref[0, :, at].astype(F32)
        for k in range(1, pieces_ref.shape[0]):
            total = total + pieces_ref[k, :, at].astype(F32)
        first, second = total[:8], total[8:]
        mine_ref[:, at] = jnp.where(upper == 0, first, second)
        return jnp.where(upper == 0, second, first)

    middle = theirs_ref.shape[1]
    for j in range(0, middle, 256):
        low = fold(slice(j, j + 256))
        high = fold(slice(middle + j, middle + j + 256))
        theirs_ref[:, j : j + 256] = jnp.concatenate([low, high], axis=0).astype(BF16)


def join_kernel(mine_ref, theirs_ref, in_ref, out_ref):
    theirs = theirs_ref[...].astype(F32)
    whole = mine_ref[...] + jnp.concatenate([theirs[:8], theirs[8:]], axis=1)
    in_ref[...] = whole[:, : 2 * WIDTH]
    out_ref[...] = whole[:, 2 * WIDTH :]


VMEM = pl.BlockSpec(memory_space=pltpu.VMEM)
SMEM = pl.BlockSpec(memory_space=pltpu.SMEM)
HBM = pl.BlockSpec(memory_space=pltpu.HBM)


def kernel_call(body, out_shape, in_specs, scratch, limit, flops, moved, out_spec=VMEM):
    return pl.pallas_call(
        body,
        out_shape=out_shape,
        in_specs=in_specs,
        out_specs=[out_spec] * len(out_shape),
        scratch_shapes=scratch,
        compiler_params=pltpu.CompilerParams(vmem_limit_bytes=limit << 20),
        cost_estimate=pl.CostEstimate(flops=flops, bytes_accessed=moved, transcendentals=0),
    )


def shape(dims, dtype):
    return jax.ShapeDtypeStruct(dims, dtype)


def per_device(
    clean_input, corrupt_input, patch_mask, lengths, site_ids, w_query, w_key, w_value,
    w_attn_out, w_pointwise_in, depth_kernel, w_pointwise_out, cotangent,
):
    frames = lax.axis_size("frames")
    position = lax.axis_index("frames")
    core = lax.rem(lax.axis_index("dp"), 2)
    scalars = jnp.stack(
        [position * ROWS, lengths[0], core, lax.rem(position, 2), lax.axis_index("dp") // 2]
    ).astype(jnp.int32)
    clean, corrupt, cot = clean_input[0], corrupt_input[0], cotangent[0]

    msg, patched, up, down = kernel_call(
        project_kernel,
        [shape((frames, ROWS, 128), BF16), shape((ROWS, WIDTH), BF16),
         shape((2 * RIM, WIDTH), BF16), shape((2 * RIM, WIDTH), BF16)],
        [HBM] * 3 + [VMEM] + [HBM] * 3,
        [pltpu.VMEM((frames, ROWS, 128), BF16), pltpu.VMEM((ROWS, WIDTH), BF16),
         pltpu.VMEM((2 * RIM, WIDTH), BF16), pltpu.VMEM((2 * RIM, WIDTH), BF16),
         pltpu.VMEM((2 * ROWS, WIDTH), BF16), pltpu.VMEM((ROWS, ROWS), F32),
         pltpu.VMEM((ROWS, WIDTH), BF16), pltpu.VMEM((ROWS, WIDTH), BF16),
         pltpu.VMEM((WIDTH, 512), BF16), pltpu.VMEM((WIDTH, 512), BF16),
         pltpu.VMEM((WIDTH, 512), BF16), pltpu.SemaphoreType.DMA((7,)), pltpu.SemaphoreType.DMA((7,))],
        62, 8 * 10**8, 6 * 10**6, HBM,
    )(clean, corrupt, cot, patch_mask, w_query, w_key, w_value)
    forward = [(i, i + 1) for i in range(frames - 1)]
    backward = [(i + 1, i) for i in range(frames - 1)]
    from_left = lax.ppermute(up, "frames", forward)
    from_right = lax.ppermute(down, "frames", backward)
    recv = lax.all_to_all(msg, "frames", 0, 0, tiled=True)
    recv, from_left, from_right = lax.optimization_barrier((recv, from_left, from_right))
    keys = frames * ROWS // 2
    (context,) = kernel_call(
        attend_kernel,
        [shape((frames, 112, 128), BF16)],
        [SMEM, VMEM],
        [pltpu.VMEM((keys, 128), BF16), pltpu.VMEM((80, keys), BF16),
         pltpu.VMEM((128, 2 * keys), BF16),
         pltpu.VMEM((keys, 512), F32), pltpu.VMEM((keys, 512), F32),
         pltpu.VMEM((frames * 64, 128), F32), pltpu.VMEM((frames * 8, 128), F32)],
        20, 8 * 10**9, 10**6,
    )(scalars, recv)
    contexts = lax.all_to_all(context, "frames", 0, 0, tiled=True)
    own, pack, swished, grad_swished, grad_gated, gated, resid = kernel_call(
        clean_kernel,
        [shape((ROWS, WIDTH), BF16), shape((ROWS, 4 * WIDTH), BF16),
         shape((INNER, WIDTH), BF16), shape((INNER, WIDTH), F32),
         shape((ROWS * 8, 128), F32), shape((CLEAN * 8, 128), F32), shape((CLEAN, WIDTH), BF16)],
        [SMEM] + [HBM] * 9,
        [pltpu.VMEM((16, 112, 128), BF16), pltpu.VMEM((512, WIDTH), BF16),
         pltpu.VMEM((WIDTH, 2 * WIDTH), BF16), pltpu.VMEM((KERNEL, WIDTH), BF16),
         pltpu.VMEM((WIDTH, WIDTH), BF16),
         pltpu.VMEM((ROWS, WIDTH), BF16), pltpu.VMEM((ROWS, 4 * WIDTH), BF16),
         pltpu.VMEM((INNER, WIDTH), BF16), pltpu.VMEM((INNER, WIDTH), F32),
         pltpu.VMEM((ROWS * 8, 128), F32), pltpu.VMEM((CLEAN * 8, 128), F32),
         pltpu.VMEM((CLEAN, WIDTH), BF16),
         pltpu.VMEM((CLEAN, 512), BF16), pltpu.VMEM((CLEAN, WIDTH), BF16),
         pltpu.VMEM((CLEAN, WIDTH), BF16),
         pltpu.VMEM((ROWS, WIDTH), F32), pltpu.VMEM((ROWS, WIDTH), F32),
         pltpu.VMEM((INNER * 8, 128), F32), pltpu.VMEM((INNER, WIDTH), F32),
         pltpu.VMEM((INNER, 128), F32), pltpu.VMEM((INNER, WIDTH), BF16),
         pltpu.VMEM((INNER * 8, 128), F32), pltpu.VMEM((32 * 8, 128), F32),
         pltpu.SemaphoreType.DMA((18,)), pltpu.SemaphoreType.DMA((9,))],
        59, 3 * 10**9, 10**7, HBM,
    )(scalars, contexts, clean, cot, from_left, from_right,
      w_attn_out, w_pointwise_in, depth_kernel, w_pointwise_out)

    cores = [(i, i ^ 1) for i in range(lax.axis_size("dp"))]
    other = lax.ppermute(pack, "dp", cores)
    (partial,) = kernel_call(
        weight_kernel,
        [shape((frames, 16, 3 * WIDTH), BF16)],
        [HBM] * 3,
        [pltpu.VMEM((2 * ROWS, WIDTH), BF16), pltpu.VMEM((2 * ROWS, 2 * WIDTH), BF16),
         pltpu.VMEM((2 * ROWS, WIDTH), BF16), pltpu.VMEM((frames, 16, 3 * WIDTH), BF16),
         pltpu.SemaphoreType.DMA((6,)), pltpu.SemaphoreType.DMA((6,))],
        59, 8 * 10**8, 10**7, HBM,
    )(own, pack, other)
    pieces = lax.all_to_all(partial, "frames", 0, 0, tiled=True)
    (attribution,) = kernel_call(
        patch_kernel,
        [shape((site_ids.shape[0], ROWS), F32)],
        [SMEM, SMEM] + [VMEM] * 14,
        [pltpu.VMEM((PATCH, 512), BF16), pltpu.VMEM((PATCH, WIDTH), BF16),
         pltpu.VMEM((PATCH, WIDTH), BF16), pltpu.VMEM((PATCH, WIDTH), BF16),
         pltpu.VMEM((PATCH * 8, 128), F32), pltpu.VMEM((ROWS * 8, 128), F32),
         pltpu.VMEM((2 * ROWS, WIDTH), BF16), pltpu.VMEM((ROWS, WIDTH), F32),
         pltpu.VMEM((ROWS, 128), F32), pltpu.VMEM((ROWS, 128), F32), pltpu.VMEM((ROWS, 128), F32),
         pltpu.VMEM((32 * 8, 128), F32)],
        28, 3 * 10**9, 10**7,
    )(scalars, site_ids, contexts, patched, from_left, from_right,
      w_attn_out, w_pointwise_in, depth_kernel, w_pointwise_out,
      pack, swished, grad_swished, grad_gated, gated, resid)
    pieces, attribution = lax.optimization_barrier((pieces, attribution))
    mine, theirs = kernel_call(
        fold_kernel,
        [shape((8, 3 * WIDTH), F32), shape((16, 3 * WIDTH // 2), BF16)],
        [SMEM, VMEM],
        [],
        16, 10**8, 3 * 10**6,
    )(scalars, pieces)
    half_dp = lax.axis_size("dp") // 2
    theirs = lax.ppermute(theirs, "dp", [(i, i ^ half_dp) for i in range(2 * half_dp)])
    grad_in, grad_out = kernel_call(
        join_kernel,
        [shape((8, 2 * WIDTH), F32), shape((8, WIDTH), F32)],
        [VMEM] * 2,
        [],
        16, 10**6, 10**6,
    )(mine, theirs)
    return attribution[None], grad_in, grad_out


def solution(mesh):
    placed = (
        P("dp", "frames", None), P("dp", "frames", None), P("dp", "frames"), P("dp"), P(), P(), P(),
        P(), P(), P(), P(), P(), P("dp", "frames", None),
    )
    return jax.shard_map(
        per_device,
        mesh=mesh,
        in_specs=placed,
        out_specs=(P("dp", None, "frames"), P(("dp", "frames"), None), P(("dp", "frames"), None)),
        check_vma=False,
    )
```
